32 devices in a mesh: groups: 2 (over y), ctx: 4 (over z), head: 4 (over x, core).
Axes of the slice: x: 2, y: 2, z: 4, core: 2. Of those that a mesh axis runs over, the one named last changes fastest.
Arguments:
- queries: bfloat16 [1024, 32, 128], P(('groups', 'ctx'), 'head'), parts along dimension 0, may hold values from -16 to 16
- positions: int32 [1024], P(('groups', 'ctx')), parts along dimension 0, may hold values from 4096 to 6143
- key_codes: bfloat16 [4, 4096, 128], P('groups', 'ctx'), parts along dimension 0, may hold values from -16 to 16
- value_codes: bfloat16 [4, 4096, 128], P('groups', 'ctx'), parts along dimension 0, may hold values from -8 to 8
- scale_index: int32 [4, 2, 32], P('groups', None, 'ctx'), parts along dimension 0, may hold values from 0 to 15
- scale_table: float32 [2, 16], replicated, may hold values from 0.5 to 2
- block_lists: int32 [64, 4, 8], P(('groups', 'head')), parts along dimension 0, may hold values from 0 to 31, as said below
Outputs:
- attended: bfloat16 [1024, 4096], P(('groups', 'ctx', 'head')), parts along dimension 0
The draws below stay inside these ranges and needn't reach their ends.
There are 2 independent parts, one for each index of `groups`. The reference program is written for one: setup_inputs(seed, part) draws one part's arguments, and reference() takes and returns one part's arrays. A program takes and returns all parts, laid end to end along the dimension named above; an argument that names none is the same for every part. Nothing has to cross between parts.
Inputs may be any that keep to these rules, and one draw needn't show every extreme that they name: For query head h and query block b, block_lists[h, b, :] names 8 different key blocks. Call the rows of b's index of ctx (a run of 128 rows) its shard c; every listed block lies on a key shard (a run of 1024 keys) at most 1 shards from c counted around the closed cycle of key shards in either direction, and at least one listed block lies exactly 1 shards away.
All inputs are finite; a program needn't handle non-finite values.
Results may differ from the reference program's by a relative error of at most 0.0065.
The reference program's roundings to bfloat16 on the way (of `key_scaled`, `value_scaled`, `rotated` and `weights_low`) count: a program that leaves them out, or rounds other values in their place, can miss the bound.
Values may be sent and summed in bfloat16 or wider, within the bound.
No kernel may reach another device: no remote copies, remote signals or barrier semaphores. Data moves between devices by JAX's collectives and lax.ppermute only.
A program may use at most 64 MiB of HBM per device.

```python
import math
import jax
import jax.numpy as jnp
from jax import lax

DH = 128
GROUP = 16
BLOCK = 128
NSEL = 8
NSCALES = 16
ROW_DEV = 128
KEY_DEV = 1024
HEADS = 32
KV_HEADS = 2
ROWS = 512
KEYS = 4096
QBLOCKS = 4
KBLOCKS = 32
REACH = 1


def draw_queries(key, part):
    base_key = jax.random.fold_in(key, 0)
    drawn = jax.random.normal(base_key, (ROWS, HEADS, DH), jnp.float32)
    return jnp.clip(drawn, -16.0, 16.0).astype(jnp.bfloat16)


def draw_key_codes(key, part):
    base_key = jax.random.fold_in(key, 0)
    drawn = jax.random.normal(base_key, (KV_HEADS, KEYS, DH), jnp.float32)
    return jnp.clip(drawn, -16.0, 16.0).astype(jnp.bfloat16)


def draw_block_lists(key, part):
    blocks_dev = KEY_DEV // BLOCK
    cycle_size = KBLOCKS // blocks_dev
    window = (2 * REACH + 1) * blocks_dev
    rows_blocks = ROW_DEV // BLOCK
    first_key, second_key, third_key, fourth_key = jax.random.split(key, 4)
    shard_bias = jax.random.randint(first_key, (HEADS, cycle_size), 0, 4)
    random_part = jax.random.randint(second_key, (HEADS, QBLOCKS, window), 0, 16384)
    home_shard = jnp.arange(QBLOCKS, dtype=jnp.int32) // rows_blocks
    slot_ids = jnp.arange(window, dtype=jnp.int32)
    offsets = slot_ids // blocks_dev - REACH
    target_shard = jnp.mod(home_shard[:, None] + offsets[None, :], cycle_size)
    bias_table = shard_bias[:, target_shard]
    scores = (random_part + bias_table * 16384) * window + slot_ids[None, None, :]
    far_side = jax.random.randint(third_key, (HEADS, QBLOCKS), 0, 2)
    far_slot = jax.random.randint(fourth_key, (HEADS, QBLOCKS), 0, blocks_dev) + far_side * (window - blocks_dev)
    scores = jnp.where(slot_ids[None, None, :] == far_slot[:, :, None], 1 << 29, scores)
    top_values, chosen = lax.top_k(scores, NSEL)
    start_block = (home_shard - REACH) * blocks_dev
    return jnp.mod(start_block[None, :, None] + chosen, KBLOCKS).astype(jnp.int32)


def with_ends(values, own_key, smallest, high):
    dims = values.shape
    place = [jax.random.randint(jax.random.fold_in(own_key, axis), (), 0, dims[axis]) for axis in range(len(dims))]
    values = values.at[tuple(place)].set(smallest)
    longest = dims.index(max(dims))
    place[longest] = (place[longest] + 1) % dims[longest]
    return values.at[tuple(place)].set(high)


def block_levels(own_key, extent, pieces, low, largest):
    def one(position, parts):
        draws = jax.random.uniform(jax.random.fold_in(jax.random.fold_in(own_key, 6), position), (parts,), jnp.float32, low / len(pieces), largest / len(pieces))
        return jnp.repeat(jnp.exp(draws), extent[position] // parts).reshape((-1,) + (1,) * (len(extent) - position - 1))

    gain = one(*pieces[0])
    for cut in pieces[1:]:
        gain = gain * one(*cut)
    return gain


def gaussian(stream_key, dims, deviation, reach, shards=(), held_as=jnp.bfloat16):
    result = deviation * jax.random.normal(stream_key, dims, jnp.float32)
    if shards:
        result = result * block_levels(stream_key, dims, shards, -0.22, 0.18)
    return jnp.clip(result, -reach, reach).astype(held_as)


def setup_inputs(seed: int = 0, part: int = 0) -> dict:
    streams_of = jax.random.split(jax.random.key(seed), 8)
    part_keys = jax.random.split(jax.random.fold_in(streams_of[7], part), 8)
    queries = draw_queries(jax.random.fold_in(jax.random.fold_in(streams_of[7], part), 71), part)
    positions = with_ends(jax.random.randint(part_keys[1], (ROWS,), KEYS, KEYS + 4 * ROWS), jax.random.fold_in(part_keys[1], 1), KEYS, (KEYS + 4 * ROWS) - 1).astype(jnp.int32)
    key_codes = draw_key_codes(jax.random.fold_in(jax.random.fold_in(streams_of[7], part), 71), part)
    value_codes = gaussian(part_keys[3], (KV_HEADS, KEYS, DH), 1.0, 8.0, ((1, 4),))
    scale_index = with_ends(jax.random.randint(part_keys[4], (2, KV_HEADS, KBLOCKS), 0, NSCALES), jax.random.fold_in(part_keys[4], 1), 0, NSCALES - 1).astype(jnp.int32)
    scale_table = jnp.clip(jnp.exp(jax.random.uniform(streams_of[5], (2, NSCALES), jnp.float32, math.log(0.5), math.log(2.0))), 0.5, 2.0)
    block_lists = draw_block_lists(jax.random.fold_in(jax.random.fold_in(streams_of[7], part), 71), part)
    return {"queries": queries, "positions": positions, "key_codes": key_codes, "value_codes": value_codes, "scale_index": scale_index, "scale_table": scale_table, "block_lists": block_lists}


ROPE_BASE = 500000.0
FLOOR_VALUE = -1e+30

def rotate(queries, positions):
    halves = queries.shape[2] // 2
    frequency = ROPE_BASE ** (-2.0 * jnp.arange(halves, dtype=jnp.float32) / queries.shape[2])
    angles = positions.astype(jnp.float32)[:, None] * frequency[None, :]
    cosine = jnp.cos(angles)[:, None, :]
    sine_value = jnp.sin(angles)[:, None, :]
    paired = queries.astype(jnp.float32).reshape(queries.shape[0], queries.shape[1], halves, 2)
    even_part = paired[..., 0]
    odd_part = paired[..., 1]
    turned = jnp.stack([even_part * cosine - odd_part * sine_value, even_part * sine_value + odd_part * cosine], axis=-1)
    return turned.reshape(queries.shape).astype(jnp.bfloat16)

def dequantize(code_array, index_rows, table_row):
    scales = table_row[index_rows]
    blocks = code_array.astype(jnp.float32).reshape(code_array.shape[0], -1, BLOCK, code_array.shape[2]) * scales[:, :, None, None]
    return blocks.reshape(code_array.shape).astype(jnp.bfloat16)

def reference(queries, positions, key_codes, value_codes, scale_index, scale_table, block_lists):
    key_scaled = dequantize(key_codes, scale_index[0], scale_table[0])
    value_scaled = dequantize(value_codes, scale_index[1], scale_table[1])
    rotated = jnp.transpose(rotate(queries, positions), (1, 0, 2))
    cycle_size = KEYS // KEY_DEV
    key_ids = jnp.arange(KBLOCKS, dtype=jnp.int32)

    def attend_head(head_number):
        head_rows = rotated[head_number]
        shared = head_number // GROUP
        head_keys = key_scaled[shared]
        head_values = value_scaled[shared]
        head_lists = block_lists[head_number]
        block_mask = jnp.any(head_lists[:, :, None] == key_ids[None, None, :], axis=1)
        allowed = jnp.repeat(jnp.repeat(block_mask, BLOCK, axis=0), BLOCK, axis=1).reshape(ROWS, cycle_size, KEY_DEV)
        scores = jnp.dot(head_rows, head_keys.T, preferred_element_type=jnp.float32) / math.sqrt(DH)
        scores = scores.reshape(ROWS, cycle_size, KEY_DEV)
        shard_max = lax.optimization_barrier(jnp.max(jnp.where(allowed, scores, FLOOR_VALUE), axis=2))
        weights = jnp.where(allowed, jnp.exp(scores - shard_max[:, :, None]), 0.0)
        shard_sum = lax.optimization_barrier(jnp.sum(weights, axis=2))
        weights_low = weights.astype(jnp.bfloat16)
        shard_out = jnp.einsum('rsk,skd->rsd', weights_low.astype(jnp.float32), head_values.reshape(cycle_size, KEY_DEV, DH).astype(jnp.float32))
        total_max = lax.optimization_barrier(jnp.max(shard_max, axis=1))
        factor = jnp.exp(shard_max - total_max[:, None])
        total_sum = lax.optimization_barrier(jnp.sum(factor * shard_sum, axis=1))
        total_out = lax.optimization_barrier(jnp.sum(factor[:, :, None] * shard_out, axis=1))
        return (total_out / total_sum[:, None]).astype(jnp.bfloat16)
    per_head = lax.map(attend_head, jnp.arange(HEADS, dtype=jnp.int32))
    return jnp.transpose(per_head, (1, 0, 2)).reshape(ROWS, HEADS * DH)
```

```python
import functools
import math

import jax
import jax.numpy as jnp
from jax import lax
from jax.experimental import pallas as pl
from jax.experimental.pallas import tpu as pltpu
from jax.sharding import PartitionSpec as P

GROUP = 16
BLOCK = 128
ROPE_BASE = 500000.0
VMEM_GRANT = 16 * 2**20

in_vmem = pl.BlockSpec(memory_space=pltpu.VMEM)
in_smem = pl.BlockSpec(memory_space=pltpu.SMEM)
in_hbm = pl.BlockSpec(memory_space=pltpu.HBM)
granted = pltpu.CompilerParams(vmem_limit_bytes=VMEM_GRANT)


def shifted(x, axis, by):
    count = lax.axis_size(axis)
    return lax.ppermute(x, axis, [(i, (i + by) % count) for i in range(count)])


def swapped(x, axis, mask):
    count = lax.axis_size(axis)
    return lax.ppermute(x, axis, [(i, i ^ mask) for i in range(count)])


def scale_kernel(
    index_ref, table_ref, codes_ref, full_ref, send_ref, held, arrived, *, row, transposed, share, heads_dev
):
    place = lax.axis_index("head")
    kv_head = place * heads_dev // GROUP
    part = lax.rem(place, share)
    copy = pltpu.make_async_copy(codes_ref.at[kv_head], held, arrived)
    copy.start()
    copy.wait()
    blocks = full_ref.shape[0]
    for block in range(blocks):
        scale = table_ref[row, index_ref[row, kv_head, block]]
        scaled = held[block * BLOCK : (block + 1) * BLOCK, :].astype(jnp.float32) * scale
        if transposed:
            scaled = scaled.T
        full_ref[block] = scaled.astype(jnp.bfloat16)
    per_part = send_ref.shape[0]
    send_ref[...] = full_ref[pl.ds(part * per_part, per_part)]


def scale_blocks(codes, scale_index, scale_table, row, transposed, share, heads_dev):
    _, keys_dev, width = codes.shape
    blocks = keys_dev // BLOCK
    return pl.pallas_call(
        functools.partial(
            scale_kernel, row=row, transposed=transposed, share=share, heads_dev=heads_dev
        ),
        in_specs=[in_smem, in_smem, in_hbm],
        out_specs=[in_vmem, in_vmem],
        out_shape=[
            jax.ShapeDtypeStruct((blocks, BLOCK, width), jnp.bfloat16),
            jax.ShapeDtypeStruct((blocks // share, BLOCK, width), jnp.bfloat16),
        ],
        scratch_shapes=[pltpu.VMEM((keys_dev, width), codes.dtype), pltpu.SemaphoreType.DMA(())],
        compiler_params=granted,
        name="scale_keys" if transposed else "scale_values",
    )(scale_index, scale_table, codes)


def gather_parts(parts, store):
    at = 0
    for part in parts:
        store[at : at + part.shape[0]] = part[...]
        at += part.shape[0]


def score_kernel(slots_ref, queries_ref, cosine_ref, sine_ref, *rest):
    *parts, weights_ref, total_ref, store = rest
    heads, rows, width = queries_ref.shape
    picks = slots_ref.shape[1]
    factor = math.log2(math.e) / math.sqrt(width)
    gather_parts(parts, store)
    cosine = cosine_ref[...]
    sine = sine_ref[...]
    even = lax.rem(lax.broadcasted_iota(jnp.int32, (rows, width), 1), 2) == 0
    for head in range(heads):
        plain = queries_ref[head].astype(jnp.float32)
        other = jnp.where(even, pltpu.roll(plain, width - 1, 1), pltpu.roll(plain, 1, 1))
        turned = (plain * cosine + other * sine).astype(jnp.bfloat16)
        scores = [
            jnp.dot(turned, store[slots_ref[head, i]], preferred_element_type=jnp.float32)
            for i in range(picks)
        ]
        top = scores[0]
        for i in range(1, picks):
            top = jnp.maximum(top, scores[i])
        top = jnp.max(top, axis=1, keepdims=True)
        total = jnp.zeros((rows, BLOCK), jnp.float32)
        for i in range(picks):
            weight = jnp.exp2((scores[i] - top) * factor)
            total = total + weight
            weights_ref[head, :, i * BLOCK : (i + 1) * BLOCK] = weight.astype(jnp.bfloat16)
        total = jnp.sum(total, axis=1, keepdims=True)
        total_ref[head] = jnp.broadcast_to(total, (rows, width))


def block_weights(slots, queries, cosine, sine, parts):
    heads, rows, width = queries.shape
    picks = slots.shape[1]
    blocks = sum(part.shape[0] for part in parts)
    return pl.pallas_call(
        score_kernel,
        in_specs=[in_smem] + [in_vmem] * (3 + len(parts)),
        out_specs=[in_vmem, in_vmem],
        out_shape=[
            jax.ShapeDtypeStruct((heads, rows, picks * BLOCK), jnp.bfloat16),
            jax.ShapeDtypeStruct((heads, rows, width), jnp.float32),
        ],
        scratch_shapes=[pltpu.VMEM((blocks, width, BLOCK), jnp.bfloat16)],
        compiler_params=granted,
        name="block_weights",
    )(slots, queries, cosine, sine, *parts)


def value_kernel(slots_ref, weights_ref, total_ref, *rest, inputs):
    parts = rest[:inputs]
    pieces = rest[inputs:-1]
    store = rest[-1]
    heads = weights_ref.shape[0]
    width = total_ref.shape[2]
    picks = slots_ref.shape[1]
    rows = pieces[0].shape[0]
    gather_parts(parts, store)
    for head in range(heads):
        picked = jnp.concatenate([store[slots_ref[head, i]] for i in range(picks)], axis=0)
        out = jnp.dot(weights_ref[head], picked, preferred_element_type=jnp.float32)
        out = out / total_ref[head]
        for n, piece in enumerate(pieces):
            piece[:, head * width : (head + 1) * width] = out[n * rows : (n + 1) * rows].astype(
                jnp.bfloat16
            )


def block_outputs(slots, weights, total, parts, pieces):
    heads, rows, width = total.shape
    blocks = sum(part.shape[0] for part in parts)
    piece = jax.ShapeDtypeStruct((rows // pieces, heads * width), jnp.bfloat16)
    return pl.pallas_call(
        functools.partial(value_kernel, inputs=len(parts)),
        in_specs=[in_smem] + [in_vmem] * (2 + len(parts)),
        out_specs=[in_vmem] * pieces,
        out_shape=[piece] * pieces,
        scratch_shapes=[pltpu.VMEM((blocks, BLOCK, width), jnp.bfloat16)],
        compiler_params=granted,
        name="block_outputs",
    )(slots, weights, total, *parts)


def join_kernel(*refs):
    *pieces, out_ref = refs
    place = lax.axis_index("head")
    width = pieces[0].shape[1]
    for mask, piece in enumerate(pieces):
        column = pl.multiple_of(jnp.bitwise_xor(place, mask) * width, width)
        out_ref[:, pl.ds(column, width)] = piece[...]


def join_pieces(pieces):
    rows, width = pieces[0].shape
    return pl.pallas_call(
        join_kernel,
        in_specs=[in_vmem] * len(pieces),
        out_specs=in_vmem,
        out_shape=jax.ShapeDtypeStruct((rows, width * len(pieces)), jnp.bfloat16),
        compiler_params=granted,
        name="join_pieces",
    )(*pieces)


def on_device(queries, positions, key_codes, value_codes, scale_index, scale_table, block_lists):
    cycle_size = lax.axis_size("ctx")
    cycle_place = lax.axis_index("ctx")
    head_count = lax.axis_size("head")
    head_place = lax.axis_index("head")
    reach_hops = min(3, (cycle_size - 1) // 2)
    rows_dev, heads_dev, head_width = queries.shape
    key_blocks = key_codes.shape[1] // BLOCK
    share = GROUP // heads_dev

    def spread(codes, row):
        full, own = scale_blocks(
            codes, scale_index, scale_table, row, row == 0, share, heads_dev
        )
        parts = [full]
        ahead = behind = own
        for _ in range(reach_hops):
            ahead = shifted(ahead, "ctx", 1)
            behind = shifted(behind, "ctx", -1)
            for arrived in (ahead, behind):
                parts.append(arrived)
                for mask in range(1, share):
                    parts.append(swapped(arrived, "head", mask))
        return parts

    key_parts = spread(key_codes, 0)
    value_parts = spread(value_codes, 1)

    lists = lax.dynamic_index_in_dim(block_lists, cycle_place, 1, keepdims=False)
    offset = jnp.mod(lists // key_blocks - cycle_place, cycle_size)
    behind = cycle_size - offset
    inner = lists % key_blocks
    per_part = key_blocks // share
    mixed = jnp.bitwise_xor(inner // per_part, head_place % share) * per_part + inner % per_part
    slots = jnp.where(
        offset == 0,
        inner,
        mixed
        + key_blocks * jnp.where(offset <= reach_hops, 2 * offset, 2 * behind - 1),
    )

    frequency = ROPE_BASE ** (
        -2.0 * (jnp.arange(head_width) // 2).astype(jnp.float32) / head_width
    )
    angles = positions.astype(jnp.float32)[:, None] * frequency[None, :]
    signs = jnp.where(jnp.arange(head_width) % 2 == 0, -1.0, 1.0)
    cosine = jnp.cos(angles)
    sine = jnp.sin(angles) * signs[None, :]

    rows_piece = rows_dev // head_count

    def reordered(x):
        shape = x.shape
        cut = x.reshape((head_count, rows_piece) + shape[1:])
        taken = [
            lax.dynamic_index_in_dim(cut, jnp.bitwise_xor(head_place, mask), 0, keepdims=False)
            for mask in range(head_count)
        ]
        return jnp.concatenate(taken, axis=0)

    turned_rows = jnp.transpose(reordered(queries), (1, 0, 2))
    weights, total = block_weights(
        slots, turned_rows, reordered(cosine), reordered(sine), key_parts
    )
    pieces = block_outputs(slots, weights, total, value_parts, head_count)
    moved = [pieces[0]] + [swapped(pieces[mask], "head", mask) for mask in range(1, head_count)]
    return join_pieces(moved)


def solution(mesh):
    placed = (
        P(("groups", "ctx"), "head", None),
        P(("groups", "ctx")),
        P("groups", "ctx", None),
        P("groups", "ctx", None),
        P("groups", None, "ctx"),
        P(),
        P(("groups", "head"), None, None),
    )
    return jax.shard_map(
        on_device,
        mesh=mesh,
        in_specs=placed,
        out_specs=P(("groups", "ctx", "head"), None),
        check_vma=False,
    )
```

```python
import functools
import math

import jax
import jax.numpy as jnp
from jax import lax
from jax.experimental import pallas as pl
from jax.experimental.pallas import tpu as pltpu
from jax.sharding import PartitionSpec as P

GROUP = 16
BLOCK = 128
ROPE_BASE = 500000.0
VMEM_GRANT = 16 * 2**20

in_vmem = pl.BlockSpec(memory_space=pltpu.VMEM)
granted = pltpu.CompilerParams(vmem_limit_bytes=VMEM_GRANT)


def sent(x, hop, share):
    cycle = lax.axis_size("ctx")
    heads = lax.axis_size("head")
    pairs = []
    for place in range(cycle):
        for head in range(heads):
            by = hop if head % share == 0 else -hop
            pairs.append((place * heads + head, (place + by) % cycle * heads + head))
    return lax.ppermute(x, ("ctx", "head"), pairs)


def swapped(x, mask):
    return lax.ppermute(x, "head", [(i, i ^ mask) for i in range(lax.axis_size("head"))])


def scale_kernel(scales_ref, codes_ref, _, out_ref, *, row):
    scales = scales_ref[...]
    for block in range(out_ref.shape[0]):
        codes = codes_ref[block * BLOCK : (block + 1) * BLOCK, :].astype(jnp.float32)
        out_ref[block] = (codes * scales[row, block]).astype(jnp.bfloat16)


def scale_blocks(scales, codes, before, row):
    keys_dev, width = codes.shape
    return pl.pallas_call(
        functools.partial(scale_kernel, row=row),
        in_specs=[in_vmem, in_vmem, pl.BlockSpec(memory_space=pl.ANY)],
        out_specs=in_vmem,
        out_shape=jax.ShapeDtypeStruct((keys_dev // BLOCK, BLOCK, width), jnp.bfloat16),
        compiler_params=granted,
        name="scale_values",
    )(scales, codes, before)


def scaled_keys(codes_ref, scales, blocks, store, at):
    for block in range(blocks):
        codes = codes_ref[block * BLOCK : (block + 1) * BLOCK, :].astype(jnp.float32)
        store[at + block] = (codes * scales[0, block]).T.astype(jnp.bfloat16)


def turn_kernel(queries_ref, cosine_ref, sine_ref, codes_ref, scales_ref, *outs):
    own_ref, sibling_ref, keys_ref = outs
    heads_dev, rows, width = own_ref.shape
    cosine = cosine_ref[...]
    sine = sine_ref[...]
    even = lax.rem(lax.broadcasted_iota(jnp.int32, cosine.shape, 1), 2) == 0
    for head in range(heads_dev):
        plain = queries_ref[head].astype(jnp.float32)
        other = jnp.where(even, pltpu.roll(plain, width - 1, 1), pltpu.roll(plain, 1, 1))
        turned = (plain * cosine + other * sine).astype(jnp.bfloat16)
        own_ref[head] = turned[:rows]
        sibling_ref[head] = turned[rows:]
    scaled_keys(codes_ref, scales_ref[...], keys_ref.shape[0], keys_ref, 0)


def turn_queries(queries, cosine, sine, codes, scales):
    heads_dev, rows, width = queries.shape
    half = jax.ShapeDtypeStruct((heads_dev, rows // 2, width), jnp.bfloat16)
    return pl.pallas_call(
        turn_kernel,
        in_specs=[in_vmem] * 5,
        out_specs=[in_vmem] * 3,
        out_shape=[
            half,
            half,
            jax.ShapeDtypeStruct((codes.shape[0] // BLOCK, width, BLOCK), jnp.bfloat16),
        ],
        compiler_params=granted,
        name="turn_queries",
    )(queries, cosine, sine, codes, scales)


def score_kernel(slots_ref, own_ref, sibling_ref, near_ref, table_ref, *rest):
    *parts, weights_ref, total_ref, store = rest
    heads_dev, rows, width = own_ref.shape
    heads = slots_ref.shape[0]
    picks = slots_ref.shape[1]
    slots = slots_ref[...]
    factor = math.log2(math.e) / math.sqrt(width)
    blocks = near_ref.shape[0]
    store[:blocks] = near_ref[...]
    table = table_ref[...]
    entries = lax.broadcasted_iota(jnp.int32, (table.shape[0], width), 0).astype(jnp.float32)
    for n, part in enumerate(parts):
        index = part[blocks * BLOCK :, :].astype(jnp.float32)
        scales = jnp.sum(jnp.where(index == entries, table, 0.0), axis=0, keepdims=True)
        scaled_keys(part, scales, blocks, store, (n + 1) * blocks)
    for head in range(heads):
        turned = (own_ref if head < heads_dev else sibling_ref)[head % heads_dev]
        scores = [
            jnp.dot(turned, store[slots[head, i]], preferred_element_type=jnp.float32)
            for i in range(picks)
        ]
        top = scores[0]
        for i in range(1, picks):
            top = jnp.maximum(top, scores[i])
        top = jnp.max(top, axis=1, keepdims=True)
        total = jnp.zeros((rows, BLOCK), jnp.float32)
        for i in range(picks):
            weight = jnp.exp2((scores[i] - top) * factor)
            total = total + weight
            weights_ref[head, :, i * BLOCK : (i + 1) * BLOCK] = weight.astype(jnp.bfloat16)
        total = jnp.sum(total, axis=1, keepdims=True)
        total_ref[head] = jnp.broadcast_to(total, (rows, width))


def block_weights(slots, own, sibling, near, table, parts):
    _, rows, width = own.shape
    heads, picks = slots.shape
    blocks = near.shape[0] * (1 + len(parts))
    return pl.pallas_call(
        score_kernel,
        in_specs=[in_vmem] * (5 + len(parts)),
        out_specs=[in_vmem, in_vmem],
        out_shape=[
            jax.ShapeDtypeStruct((heads, rows, picks * BLOCK), jnp.bfloat16),
            jax.ShapeDtypeStruct((heads, rows, width), jnp.float32),
        ],
        scratch_shapes=[pltpu.VMEM((blocks, width, BLOCK), jnp.bfloat16)],
        compiler_params=granted,
        name="block_weights",
    )(slots, own, sibling, near, table, *parts)


def value_kernel(slots_ref, weights_ref, total_ref, *rest, inputs):
    parts = rest[:inputs]
    pieces = rest[inputs:-1]
    store = rest[-1]
    heads, _, width = total_ref.shape
    picks = slots_ref.shape[1]
    rows = pieces[0].shape[0]
    slots = slots_ref[...]
    at = 0
    for part in parts:
        store[at : at + part.shape[0]] = part[...]
        at += part.shape[0]
    for head in range(heads):
        picked = jnp.concatenate([store[slots[head, i]] for i in range(picks)], axis=0)
        out = jnp.dot(weights_ref[head], picked, preferred_element_type=jnp.float32)
        out = out / total_ref[head]
        for n, piece in enumerate(pieces):
            piece[:, head * width : (head + 1) * width] = out[n * rows : (n + 1) * rows].astype(
                jnp.bfloat16
            )


def block_outputs(slots, weights, total, parts, pieces):
    heads, rows, width = total.shape
    blocks = sum(part.shape[0] for part in parts)
    piece = jax.ShapeDtypeStruct((rows // pieces, heads * width), jnp.bfloat16)
    return pl.pallas_call(
        functools.partial(value_kernel, inputs=len(parts)),
        in_specs=[in_vmem] * (3 + len(parts)),
        out_specs=[in_vmem] * pieces,
        out_shape=[piece] * pieces,
        scratch_shapes=[pltpu.VMEM((blocks, BLOCK, width), jnp.bfloat16)],
        compiler_params=granted,
        name="block_outputs",
    )(slots, weights, total, *parts)


def join_kernel(*refs, share):
    *pieces, out_ref = refs
    place = lax.axis_index("head")
    width = pieces[0].shape[1] // share
    for n, piece in enumerate(pieces):
        for part in range(share):
            column = pl.multiple_of(jnp.bitwise_xor(place, n * share + part) * width, width)
            out_ref[:, pl.ds(column, width)] = piece[:, part * width : (part + 1) * width]


def join_pieces(pieces, share):
    rows, width = pieces[0].shape
    return pl.pallas_call(
        functools.partial(join_kernel, share=share),
        in_specs=[in_vmem] * len(pieces),
        out_specs=in_vmem,
        out_shape=jax.ShapeDtypeStruct((rows, width * len(pieces)), jnp.bfloat16),
        compiler_params=granted,
        name="join_pieces",
    )(*pieces)


def on_device(queries, positions, key_codes, value_codes, scale_index, scale_table, block_lists):
    cycle_size = lax.axis_size("ctx")
    cycle_place = lax.axis_index("ctx")
    head_count = lax.axis_size("head")
    head_place = lax.axis_index("head")
    reach_hops = min(3, (cycle_size - 1) // 2)
    rows_dev, heads_dev, head_width = queries.shape
    key_blocks = key_codes.shape[1] // BLOCK
    share = GROUP // heads_dev
    assert share == 2 and rows_dev == BLOCK
    core = head_place % share
    group = head_place // share
    groups = head_count // share
    kv_head = head_place * heads_dev // GROUP

    key_rows = lax.dynamic_index_in_dim(key_codes, kv_head, 0, keepdims=False)
    (
        key_rows,
        queries,
        positions,
        value_codes,
        scale_index,
        scale_table,
        block_lists,
    ) = lax.optimization_barrier(
        (key_rows, queries, positions, value_codes, scale_index, scale_table, block_lists)
    )
    value_rows = lax.dynamic_index_in_dim(value_codes, kv_head, 0, keepdims=False)
    index_rows = lax.dynamic_index_in_dim(scale_index, kv_head, 1, keepdims=False)
    matches = index_rows[:, :, None] == jnp.arange(scale_table.shape[1], dtype=jnp.int32)
    scales = jnp.sum(jnp.where(matches, scale_table[:, None, :], 0.0), axis=2)

    entries = scale_table.shape[1]
    labels = jnp.pad(
        jnp.broadcast_to(index_rows[0].astype(jnp.bfloat16), (entries, key_blocks)),
        ((0, 0), (0, head_width - key_blocks)),
    )
    far_keys = jnp.concatenate([key_rows, labels], axis=0)
    key_parts = []
    for _ in range(reach_hops):
        far_keys = sent(far_keys, 1, share)
        key_parts += [far_keys, swapped(far_keys, 1)]

    own_lists = lax.dynamic_index_in_dim(block_lists, cycle_place, 1, keepdims=False)
    lists = jnp.concatenate([own_lists, swapped(own_lists, 1)], axis=0)
    offset = jnp.mod(lists // key_blocks - cycle_place, cycle_size)
    above = offset <= reach_hops
    hops = jnp.where(above, offset, cycle_size - offset)
    place = 2 * hops - jnp.where(above == (core == 1), 1, 0)
    slots = lists % key_blocks + key_blocks * jnp.where(offset == 0, 0, place)

    def ordered(x):
        cut = x.reshape((groups, share, rows_dev // head_count) + x.shape[1:])
        taken = [
            lax.dynamic_slice(
                cut,
                (jnp.bitwise_xor(group, n), jnp.bitwise_xor(core, part)) + (0,) * x.ndim,
                (1, 1) + cut.shape[2:],
            )
            for part in range(share)
            for n in range(groups)
        ]
        return jnp.concatenate(taken, axis=0).reshape(x.shape)

    frequency = ROPE_BASE ** (
        -2.0 * (jnp.arange(head_width) // 2).astype(jnp.float32) / head_width
    )
    angles = ordered(positions).astype(jnp.float32)[:, None] * frequency[None, :]
    signs = jnp.where(jnp.arange(head_width) % 2 == 0, -1.0, 1.0)
    cosine = jnp.cos(angles)
    sine = jnp.sin(angles) * signs[None, :]

    own, sibling, near = turn_queries(
        jnp.transpose(ordered(queries), (1, 0, 2)), cosine, sine, key_rows, scales
    )
    values = scale_blocks(scales, value_rows, own, 1)
    value_steps = []
    far_values = values
    for _ in range(reach_hops):
        far_values = sent(far_values, 1, share)
        value_steps.append(far_values)
    weights, total = block_weights(
        slots, own, swapped(sibling, 1), near, scale_table[0][:, None], key_parts
    )

    *value_steps, weights = lax.optimization_barrier((*value_steps, weights))
    value_parts = [values]
    for step in value_steps:
        value_parts += [step, swapped(step, 1)]
    pieces = block_outputs(slots, weights, total, value_parts, groups)
    moved = [pieces[0]] + [swapped(pieces[n], n * share) for n in range(1, groups)]
    return join_pieces(moved, share)


def solution(mesh):
    placed = (
        P(("groups", "ctx"), "head", None),
        P(("groups", "ctx")),
        P("groups", "ctx", None),
        P("groups", "ctx", None),
        P("groups", None, "ctx"),
        P(),
        P(("groups", "head"), None, None),
    )
    return jax.shard_map(
        on_device,
        mesh=mesh,
        in_specs=placed,
        out_specs=P(("groups", "ctx", "head"), None),
        check_vma=False,
    )
```

```python
import functools
import math

import jax
import jax.numpy as jnp
from jax import lax
from jax.experimental import pallas as pl
from jax.experimental.pallas import tpu as pltpu
from jax.sharding import PartitionSpec as P

GROUP = 16
BLOCK = 128
ROPE_BASE = 500000.0
VMEM_GRANT = 16 * 2**20

in_vmem = pl.BlockSpec(memory_space=pltpu.VMEM)
granted = pltpu.CompilerParams(vmem_limit_bytes=VMEM_GRANT)


def sent(x, hop, share):
    cycle = lax.axis_size("ctx")
    heads = lax.axis_size("head")
    pairs = []
    for place in range(cycle):
        for head in range(heads):
            by = hop if head % share == 0 else -hop
            pairs.append((place * heads + head, (place + by) % cycle * heads + head))
    return lax.ppermute(x, ("ctx", "head"), pairs)


def swapped(x, mask):
    return lax.ppermute(x, "head", [(i, i ^ mask) for i in range(lax.axis_size("head"))])


def scale_kernel(scales_ref, codes_ref, _, out_ref, *, row):
    scales = scales_ref[...]
    for block in range(out_ref.shape[0]):
        codes = codes_ref[block * BLOCK : (block + 1) * BLOCK, :].astype(jnp.float32)
        out_ref[block] = (codes * scales[row, block]).astype(jnp.bfloat16)


def scale_blocks(scales, codes, before, row):
    keys_dev, width = codes.shape
    return pl.pallas_call(
        functools.partial(scale_kernel, row=row),
        in_specs=[in_vmem, in_vmem, pl.BlockSpec(memory_space=pl.ANY)],
        out_specs=in_vmem,
        out_shape=jax.ShapeDtypeStruct((keys_dev // BLOCK, BLOCK, width), jnp.bfloat16),
        compiler_params=granted,
        name="scale_values",
    )(scales, codes, before)


def scaled_keys(codes_ref, scales, blocks, store, at):
    for block in range(blocks):
        codes = codes_ref[block * BLOCK : (block + 1) * BLOCK, :].astype(jnp.float32)
        store[at + block] = (codes * scales[0, block]).T.astype(jnp.bfloat16)


def turn_kernel(queries_ref, cosine_ref, sine_ref, codes_ref, scales_ref, *outs):
    own_ref, sibling_ref, keys_ref = outs
    heads_dev, rows, width = own_ref.shape
    cosine = cosine_ref[...]
    sine = sine_ref[...]
    even = lax.rem(lax.broadcasted_iota(jnp.int32, cosine.shape, 1), 2) == 0
    for head in range(heads_dev):
        plain = queries_ref[head].astype(jnp.float32)
        other = jnp.where(even, pltpu.roll(plain, width - 1, 1), pltpu.roll(plain, 1, 1))
        turned = (plain * cosine + other * sine).astype(jnp.bfloat16)
        own_ref[head] = turned[:rows]
        sibling_ref[head] = turned[rows:]
    scaled_keys(codes_ref, scales_ref[...], keys_ref.shape[0], keys_ref, 0)


def turn_queries(queries, cosine, sine, codes, scales):
    heads_dev, rows, width = queries.shape
    half = jax.ShapeDtypeStruct((heads_dev, rows // 2, width), jnp.bfloat16)
    return pl.pallas_call(
        turn_kernel,
        in_specs=[in_vmem] * 5,
        out_specs=[in_vmem] * 3,
        out_shape=[
            half,
            half,
            jax.ShapeDtypeStruct((scales.shape[1], width, BLOCK), jnp.bfloat16),
        ],
        compiler_params=granted,
        name="turn_queries",
    )(queries, cosine, sine, codes, scales)


def score_kernel(slots_ref, own_ref, sibling_ref, near_ref, table_ref, *rest):
    *parts, weights_ref, total_ref, store = rest
    heads_dev, rows, width = own_ref.shape
    heads = slots_ref.shape[0]
    picks = slots_ref.shape[1]
    slots = slots_ref[...]
    factor = math.log2(math.e) / math.sqrt(width)
    blocks = near_ref.shape[0]
    store[:blocks] = near_ref[...]
    table = table_ref[...]
    entries = lax.broadcasted_iota(jnp.int32, (table.shape[0], width), 0).astype(jnp.float32)
    for n, part in enumerate(parts):
        index = part[blocks * BLOCK :, :].astype(jnp.float32)
        scales = jnp.sum(jnp.where(index == entries, table, 0.0), axis=0, keepdims=True)
        scaled_keys(part, scales, blocks, store, (n + 1) * blocks)
    for head in range(heads):
        turned = (own_ref if head < heads_dev else sibling_ref)[head % heads_dev]
        scores = [
            jnp.dot(turned, store[slots[head, i]], preferred_element_type=jnp.float32)
            for i in range(picks)
        ]
        top = scores[0]
        for i in range(1, picks):
            top = jnp.maximum(top, scores[i])
        top = jnp.max(top, axis=1, keepdims=True)
        total = jnp.zeros((rows, BLOCK), jnp.float32)
        for i in range(picks):
            weight = jnp.exp2((scores[i] - top) * factor)
            total = total + weight
            weights_ref[head, :, i * BLOCK : (i + 1) * BLOCK] = weight.astype(jnp.bfloat16)
        total = jnp.sum(total, axis=1, keepdims=True)
        total_ref[head] = jnp.broadcast_to(total, (rows, width))


def block_weights(slots, own, sibling, near, table, parts):
    _, rows, width = own.shape
    heads, picks = slots.shape
    blocks = near.shape[0] * (1 + len(parts))
    return pl.pallas_call(
        score_kernel,
        in_specs=[in_vmem] * (5 + len(parts)),
        out_specs=[in_vmem, in_vmem],
        out_shape=[
            jax.ShapeDtypeStruct((heads, rows, picks * BLOCK), jnp.bfloat16),
            jax.ShapeDtypeStruct((heads, rows, width), jnp.float32),
        ],
        scratch_shapes=[pltpu.VMEM((blocks, width, BLOCK), jnp.bfloat16)],
        compiler_params=granted,
        name="block_weights",
    )(slots, own, sibling, near, table, *parts)


def value_kernel(slots_ref, weights_ref, total_ref, *rest, inputs):
    parts = rest[:inputs]
    pieces = rest[inputs:-1]
    store = rest[-1]
    heads, _, width = total_ref.shape
    picks = slots_ref.shape[1]
    rows = pieces[0].shape[0]
    slots = slots_ref[...]
    at = 0
    for part in parts:
        store[at : at + part.shape[0]] = part[...]
        at += part.shape[0]
    for head in range(heads):
        picked = jnp.concatenate([store[slots[head, i]] for i in range(picks)], axis=0)
        out = jnp.dot(weights_ref[head], picked, preferred_element_type=jnp.float32)
        out = out / total_ref[head]
        for n, piece in enumerate(pieces):
            piece[:, head * width : (head + 1) * width] = out[n * rows : (n + 1) * rows].astype(
                jnp.bfloat16
            )


def block_outputs(slots, weights, total, parts, pieces):
    heads, rows, width = total.shape
    blocks = sum(part.shape[0] for part in parts)
    piece = jax.ShapeDtypeStruct((rows // pieces, heads * width), jnp.bfloat16)
    return pl.pallas_call(
        functools.partial(value_kernel, inputs=len(parts)),
        in_specs=[in_vmem] * (3 + len(parts)),
        out_specs=[in_vmem] * pieces,
        out_shape=[piece] * pieces,
        scratch_shapes=[pltpu.VMEM((blocks, BLOCK, width), jnp.bfloat16)],
        compiler_params=granted,
        name="block_outputs",
    )(slots, weights, total, *parts)


def join_kernel(*refs, share):
    *pieces, out_ref = refs
    place = lax.axis_index("head")
    width = pieces[0].shape[1] // share
    for n, piece in enumerate(pieces):
        for part in range(share):
            column = pl.multiple_of(jnp.bitwise_xor(place, n * share + part) * width, width)
            out_ref[:, pl.ds(column, width)] = piece[:, part * width : (part + 1) * width]


def join_pieces(pieces, share):
    rows, width = pieces[0].shape
    return pl.pallas_call(
        functools.partial(join_kernel, share=share),
        in_specs=[in_vmem] * len(pieces),
        out_specs=in_vmem,
        out_shape=jax.ShapeDtypeStruct((rows, width * len(pieces)), jnp.bfloat16),
        compiler_params=granted,
        name="join_pieces",
    )(*pieces)


def on_device(queries, positions, key_codes, value_codes, scale_index, scale_table, block_lists):
    cycle_size = lax.axis_size("ctx")
    cycle_place = lax.axis_index("ctx")
    head_count = lax.axis_size("head")
    head_place = lax.axis_index("head")
    reach_hops = min(3, (cycle_size - 1) // 2)
    rows_dev, heads_dev, head_width = queries.shape
    key_blocks = key_codes.shape[1] // BLOCK
    share = GROUP // heads_dev
    assert share == 2 and rows_dev == BLOCK
    core = head_place % share
    group = head_place // share
    groups = head_count // share
    kv_head = head_place * heads_dev // GROUP

    index_rows = lax.dynamic_index_in_dim(scale_index, kv_head, 1, keepdims=False)
    entries = scale_table.shape[1]
    labels = jnp.pad(
        jnp.broadcast_to(index_rows[0].astype(jnp.bfloat16), (entries, key_blocks)),
        ((0, 0), (0, head_width - key_blocks)),
    )
    labels, key_codes = lax.optimization_barrier((labels, key_codes))
    key_rows = lax.dynamic_index_in_dim(key_codes, kv_head, 0, keepdims=False)
    near_keys = jnp.concatenate([key_rows, labels], axis=0)
    near_keys, queries, positions, value_codes, scale_index, scale_table, block_lists = (
        lax.optimization_barrier(
            (near_keys, queries, positions, value_codes, scale_index, scale_table, block_lists)
        )
    )
    index_rows = lax.dynamic_index_in_dim(scale_index, kv_head, 1, keepdims=False)
    far_keys = near_keys
    key_parts = []
    for _ in range(reach_hops):
        far_keys = sent(far_keys, 1, share)
        key_parts += [far_keys, swapped(far_keys, 1)]

    value_rows = lax.dynamic_index_in_dim(value_codes, kv_head, 0, keepdims=False)
    matches = index_rows[:, :, None] == jnp.arange(entries, dtype=jnp.int32)
    scales = jnp.sum(jnp.where(matches, scale_table[:, None, :], 0.0), axis=2)

    own_lists = lax.dynamic_index_in_dim(block_lists, cycle_place, 1, keepdims=False)
    lists = jnp.concatenate([own_lists, swapped(own_lists, 1)], axis=0)
    offset = jnp.mod(lists // key_blocks - cycle_place, cycle_size)
    above = offset <= reach_hops
    hops = jnp.where(above, offset, cycle_size - offset)
    place = 2 * hops - jnp.where(above == (core == 1), 1, 0)
    slots = lists % key_blocks + key_blocks * jnp.where(offset == 0, 0, place)

    def ordered(x):
        cut = x.reshape((groups, share, rows_dev // head_count) + x.shape[1:])
        taken = [
            lax.dynamic_slice(
                cut,
                (jnp.bitwise_xor(group, n), jnp.bitwise_xor(core, part)) + (0,) * x.ndim,
                (1, 1) + cut.shape[2:],
            )
            for part in range(share)
            for n in range(groups)
        ]
        return jnp.concatenate(taken, axis=0).reshape(x.shape)

    frequency = ROPE_BASE ** (
        -2.0 * (jnp.arange(head_width) // 2).astype(jnp.float32) / head_width
    )
    angles = ordered(positions).astype(jnp.float32)[:, None] * frequency[None, :]
    signs = jnp.where(jnp.arange(head_width) % 2 == 0, -1.0, 1.0)
    cosine = jnp.cos(angles)
    sine = jnp.sin(angles) * signs[None, :]

    own, sibling, near = turn_queries(
        jnp.transpose(ordered(queries), (1, 0, 2)), cosine, sine, near_keys, scales
    )
    values = scale_blocks(scales, value_rows, near_keys, 1)
    value_steps = []
    far_values = values
    for _ in range(reach_hops):
        far_values = sent(far_values, 1, share)
        value_steps.append(far_values)
    weights, total = block_weights(
        slots, own, swapped(sibling, 1), near, scale_table[0][:, None], key_parts
    )

    *value_steps, weights = lax.optimization_barrier((*value_steps, weights))
    value_parts = [values]
    for step in value_steps:
        value_parts += [step, swapped(step, 1)]
    pieces = block_outputs(slots, weights, total, value_parts, groups)
    moved = [pieces[0]] + [swapped(pieces[n], n * share) for n in range(1, groups)]
    return join_pieces(moved, share)


def solution(mesh):
    placed = (
        P(("groups", "ctx"), "head", None),
        P(("groups", "ctx")),
        P("groups", "ctx", None),
        P("groups", "ctx", None),
        P("groups", None, "ctx"),
        P(),
        P(("groups", "head"), None, None),
    )
    return jax.shard_map(
        on_device,
        mesh=mesh,
        in_specs=placed,
        out_specs=P(("groups", "ctx", "head"), None),
        check_vma=False,
    )
```

```python
import functools
import math

import jax
import jax.numpy as jnp
from jax import lax
from jax.experimental import pallas as pl
from jax.experimental.pallas import tpu as pltpu
from jax.sharding import PartitionSpec as P

GROUP = 16
BLOCK = 128
ROW_TILE = 16
ROPE_BASE = 500000.0
VMEM_GRANT = 16 * 2**20

in_vmem = pl.BlockSpec(memory_space=pltpu.VMEM)
granted = pltpu.CompilerParams(vmem_limit_bytes=VMEM_GRANT)


def paired(cycle, hops):
    return hops == 1 and cycle % 2 == 0


def source(place, part, cycle, pairs):
    if pairs:
        return place + 1 if place % 2 == part else place - 1
    return place - 1 if part == 0 else place + 1


def sent(x, share, pairs):
    cycle = lax.axis_size("ctx")
    heads = lax.axis_size("head")
    moves = [
        (source(place, head % share, cycle, pairs) % cycle * heads + head, place * heads + head)
        for place in range(cycle)
        for head in range(heads)
    ]
    return lax.ppermute(x, ("ctx", "head"), moves)


def swapped(x, mask):
    return lax.ppermute(x, "head", [(i, i ^ mask) for i in range(lax.axis_size("head"))])


def scale_kernel(scales_ref, codes_ref, _, out_ref, *, row):
    scales = scales_ref[...]
    for block in range(out_ref.shape[0]):
        codes = codes_ref[block * BLOCK : (block + 1) * BLOCK, :].astype(jnp.float32)
        out_ref[block] = (codes * scales[row, block]).astype(jnp.bfloat16)


def scale_blocks(scales, codes, before, row):
    keys_dev, width = codes.shape
    return pl.pallas_call(
        functools.partial(scale_kernel, row=row),
        in_specs=[in_vmem, in_vmem, pl.BlockSpec(memory_space=pl.ANY)],
        out_specs=in_vmem,
        out_shape=jax.ShapeDtypeStruct((keys_dev // BLOCK, BLOCK, width), jnp.bfloat16),
        compiler_params=granted,
        name="scale_values",
    )(scales, codes, before)


def scaled_keys(codes_ref, scales, blocks, store, at):
    for block in range(blocks):
        codes = codes_ref[block * BLOCK : (block + 1) * BLOCK, :].astype(jnp.float32)
        store[at + block] = (codes * scales[0, block]).T.astype(jnp.bfloat16)


def turn_kernel(queries_ref, cosine_ref, sine_ref, codes_ref, scales_ref, lists_ref, *outs):
    own_ref, sibling_ref, keys_ref = outs
    heads_dev, rows, width = own_ref.shape
    cosine = cosine_ref[...]
    sine = sine_ref[...]
    even = lax.rem(lax.broadcasted_iota(jnp.int32, cosine.shape, 1), 2) == 0
    for head in range(heads_dev):
        plain = queries_ref[head].astype(jnp.float32)
        other = jnp.where(even, pltpu.roll(plain, width - 1, 1), pltpu.roll(plain, 1, 1))
        turned = (plain * cosine + other * sine).astype(jnp.bfloat16)
        own_ref[head] = turned[:rows]
        sibling_ref[head, :rows] = turned[rows:]
        sibling_ref[head, rows:] = jnp.broadcast_to(
            lists_ref[head : head + 1], sibling_ref[head, rows:].shape
        )
    scaled_keys(codes_ref, scales_ref[...], keys_ref.shape[0], keys_ref, 0)


def turn_queries(queries, cosine, sine, codes, scales, lists):
    heads_dev, rows, width = queries.shape
    half = (heads_dev, rows // 2, width)
    more = (heads_dev, rows // 2 + ROW_TILE, width)
    return pl.pallas_call(
        turn_kernel,
        in_specs=[in_vmem] * 6,
        out_specs=[in_vmem] * 3,
        out_shape=[
            jax.ShapeDtypeStruct(half, jnp.bfloat16),
            jax.ShapeDtypeStruct(more, jnp.bfloat16),
            jax.ShapeDtypeStruct((scales.shape[1], width, BLOCK), jnp.bfloat16),
        ],
        compiler_params=granted,
        name="turn_queries",
    )(queries, cosine, sine, codes, scales, lists)


def score_kernel(slots_ref, own_ref, sibling_ref, near_ref, table_ref, *rest):
    *parts, weights_ref, total_ref, store = rest
    heads_dev, rows, width = own_ref.shape
    heads = slots_ref.shape[0]
    picks = slots_ref.shape[1]
    slots = slots_ref[...]
    factor = math.log2(math.e) / math.sqrt(width)
    blocks = near_ref.shape[0]
    store[:blocks] = near_ref[...]
    table = table_ref[...]
    entries = lax.broadcasted_iota(jnp.int32, (table.shape[0], width), 0).astype(jnp.float32)
    for n, part in enumerate(parts):
        index = part[blocks * BLOCK :, :].astype(jnp.float32)
        scales = jnp.sum(jnp.where(index == entries, table, 0.0), axis=0, keepdims=True)
        scaled_keys(part, scales, blocks, store, (n + 1) * blocks)
    for head in range(heads):
        turned = (own_ref if head < heads_dev else sibling_ref)[head % heads_dev, :rows]
        scores = [
            jnp.dot(turned, store[slots[head, i]], preferred_element_type=jnp.float32)
            for i in range(picks)
        ]
        top = scores[0]
        for i in range(1, picks):
            top = jnp.maximum(top, scores[i])
        top = jnp.max(top, axis=1, keepdims=True)
        total = jnp.zeros((rows, BLOCK), jnp.float32)
        for i in range(picks):
            weight = jnp.exp2((scores[i] - top) * factor)
            total = total + weight
            weights_ref[head, :, i * BLOCK : (i + 1) * BLOCK] = weight.astype(jnp.bfloat16)
        total = jnp.sum(total, axis=1, keepdims=True)
        total_ref[head] = jnp.broadcast_to(total, (rows, width))


def block_weights(slots, own, sibling, near, table, parts):
    _, rows, width = own.shape
    heads, picks = slots.shape
    blocks = near.shape[0] * (1 + len(parts))
    return pl.pallas_call(
        score_kernel,
        in_specs=[in_vmem] * (5 + len(parts)),
        out_specs=[in_vmem, in_vmem],
        out_shape=[
            jax.ShapeDtypeStruct((heads, rows, picks * BLOCK), jnp.bfloat16),
            jax.ShapeDtypeStruct((heads, rows, width), jnp.float32),
        ],
        scratch_shapes=[pltpu.VMEM((blocks, width, BLOCK), jnp.bfloat16)],
        compiler_params=granted,
        name="block_weights",
    )(slots, own, sibling, near, table, *parts)


def value_kernel(slots_ref, weights_ref, total_ref, *rest, inputs):
    parts = rest[:inputs]
    pieces = rest[inputs:-1]
    store = rest[-1]
    heads, _, width = total_ref.shape
    picks = slots_ref.shape[1]
    rows = pieces[0].shape[0]
    slots = slots_ref[...]
    at = 0
    for part in parts:
        store[at : at + part.shape[0]] = part[...]
        at += part.shape[0]
    for head in range(heads):
        picked = jnp.concatenate([store[slots[head, i]] for i in range(picks)], axis=0)
        out = jnp.dot(weights_ref[head], picked, preferred_element_type=jnp.float32)
        out = out / total_ref[head]
        for n, piece in enumerate(pieces):
            piece[:, head * width : (head + 1) * width] = out[n * rows : (n + 1) * rows].astype(
                jnp.bfloat16
            )


def block_outputs(slots, weights, total, parts, pieces):
    heads, rows, width = total.shape
    blocks = sum(part.shape[0] for part in parts)
    piece = jax.ShapeDtypeStruct((rows // pieces, heads * width), jnp.bfloat16)
    return pl.pallas_call(
        functools.partial(value_kernel, inputs=len(parts)),
        in_specs=[in_vmem] * (3 + len(parts)),
        out_specs=[in_vmem] * pieces,
        out_shape=[piece] * pieces,
        scratch_shapes=[pltpu.VMEM((blocks, BLOCK, width), jnp.bfloat16)],
        compiler_params=granted,
        name="block_outputs",
    )(slots, weights, total, *parts)


def join_kernel(*refs, share):
    *pieces, out_ref = refs
    place = lax.axis_index("head")
    width = pieces[0].shape[1] // share
    for n, piece in enumerate(pieces):
        for part in range(share):
            column = pl.multiple_of(jnp.bitwise_xor(place, n * share + part) * width, width)
            out_ref[:, pl.ds(column, width)] = piece[:, part * width : (part + 1) * width]


def join_pieces(pieces, share):
    rows, width = pieces[0].shape
    return pl.pallas_call(
        functools.partial(join_kernel, share=share),
        in_specs=[in_vmem] * len(pieces),
        out_specs=in_vmem,
        out_shape=jax.ShapeDtypeStruct((rows, width * len(pieces)), jnp.bfloat16),
        compiler_params=granted,
        name="join_pieces",
    )(*pieces)


def on_device(queries, positions, key_codes, value_codes, scale_index, scale_table, block_lists):
    cycle_size = lax.axis_size("ctx")
    cycle_place = lax.axis_index("ctx")
    head_count = lax.axis_size("head")
    head_place = lax.axis_index("head")
    reach_hops = min(3, (cycle_size - 1) // 2)
    pairs = paired(cycle_size, reach_hops)
    rows_dev, heads_dev, head_width = queries.shape
    key_blocks = key_codes.shape[1] // BLOCK
    share = GROUP // heads_dev
    assert share == 2 and rows_dev == BLOCK
    core = head_place % share
    group = head_place // share
    groups = head_count // share
    kv_head = head_place * heads_dev // GROUP

    index_rows = lax.dynamic_index_in_dim(scale_index, kv_head, 1, keepdims=False)
    entries = scale_table.shape[1]
    labels = jnp.pad(
        jnp.broadcast_to(index_rows[0].astype(jnp.bfloat16), (entries, key_blocks)),
        ((0, 0), (0, head_width - key_blocks)),
    )
    labels, key_codes = lax.optimization_barrier((labels, key_codes))
    key_rows = lax.dynamic_index_in_dim(key_codes, kv_head, 0, keepdims=False)
    near_keys = jnp.concatenate([key_rows, labels], axis=0)
    near_keys, queries, positions, value_codes, scale_index, scale_table, block_lists = (
        lax.optimization_barrier(
            (near_keys, queries, positions, value_codes, scale_index, scale_table, block_lists)
        )
    )
    index_rows = lax.dynamic_index_in_dim(scale_index, kv_head, 1, keepdims=False)
    far_keys = near_keys
    key_parts = []
    for _ in range(reach_hops):
        far_keys = sent(far_keys, share, pairs)
        key_parts.append(far_keys)

    value_rows = lax.dynamic_index_in_dim(value_codes, kv_head, 0, keepdims=False)
    matches = index_rows[:, :, None] == jnp.arange(entries, dtype=jnp.int32)
    scales = jnp.sum(jnp.where(matches, scale_table[:, None, :], 0.0), axis=2)

    values = scale_blocks(scales, value_rows, near_keys, 1)
    values, queries, positions, block_lists = lax.optimization_barrier(
        (values, queries, positions, block_lists)
    )
    own_lists = lax.dynamic_index_in_dim(block_lists, cycle_place, 1, keepdims=False)
    def ordered(x):
        cut = x.reshape((groups, share, rows_dev // head_count) + x.shape[1:])
        taken = [
            lax.dynamic_slice(
                cut,
                (jnp.bitwise_xor(group, n), jnp.bitwise_xor(core, part)) + (0,) * x.ndim,
                (1, 1) + cut.shape[2:],
            )
            for part in range(share)
            for n in range(groups)
        ]
        return jnp.concatenate(taken, axis=0).reshape(x.shape)

    frequency = ROPE_BASE ** (
        -2.0 * (jnp.arange(head_width) // 2).astype(jnp.float32) / head_width
    )
    angles = ordered(positions).astype(jnp.float32)[:, None] * frequency[None, :]
    signs = jnp.where(jnp.arange(head_width) % 2 == 0, -1.0, 1.0)
    cosine = jnp.cos(angles)
    sine = jnp.sin(angles) * signs[None, :]

    picks = own_lists.shape[1]
    carried = jnp.pad(own_lists.astype(jnp.bfloat16), ((0, 0), (0, head_width - picks)))
    own, sibling, near = turn_queries(
        jnp.transpose(ordered(queries), (1, 0, 2)), cosine, sine, near_keys, scales, carried
    )
    sibling, key_parts[0] = lax.optimization_barrier((sibling, key_parts[0]))
    key_parts = [part for far in key_parts for part in (far, swapped(far, 1))]
    sibling = swapped(sibling, 1)
    sibling_lists = sibling[:, rows_dev // share, :picks].astype(jnp.int32)
    lists = jnp.concatenate([own_lists, sibling_lists], axis=0)
    offset = jnp.mod(lists // key_blocks - cycle_place, cycle_size)
    above = offset <= reach_hops
    hops = jnp.where(above, offset, cycle_size - offset)
    from_above = (cycle_place % 2 if pairs else 1) == core
    place = 2 * hops - jnp.where(above == from_above, 1, 0)
    slots = lists % key_blocks + key_blocks * jnp.where(offset == 0, 0, place)

    value_steps = []
    far_values = values
    for _ in range(reach_hops):
        far_values = sent(far_values, share, pairs)
        value_steps.append(far_values)
    weights, total = block_weights(
        slots, own, sibling, near, scale_table[0][:, None], key_parts
    )

    *value_steps, weights = lax.optimization_barrier((*value_steps, weights))
    value_parts = [values]
    for step in value_steps:
        value_parts += [step, swapped(step, 1)]
    pieces = block_outputs(slots, weights, total, value_parts, groups)
    moved = [pieces[0]] + [swapped(pieces[n], n * share) for n in range(1, groups)]
    return join_pieces(moved, share)


def solution(mesh):
    placed = (
        P(("groups", "ctx"), "head", None),
        P(("groups", "ctx")),
        P("groups", "ctx", None),
        P("groups", "ctx", None),
        P("groups", None, "ctx"),
        P(),
        P(("groups", "head"), None, None),
    )
    return jax.shard_map(
        on_device,
        mesh=mesh,
        in_specs=placed,
        out_specs=P(("groups", "ctx", "head"), None),
        check_vma=False,
    )
```

```python
import functools
import math

import jax
import jax.numpy as jnp
from jax import lax
from jax.experimental import pallas as pl
from jax.experimental.pallas import tpu as pltpu
from jax.sharding import PartitionSpec as P

GROUP = 16
BLOCK = 128
ROW_TILE = 16
ROPE_BASE = 500000.0
VMEM_GRANT = 16 * 2**20

in_vmem = pl.BlockSpec(memory_space=pltpu.VMEM)
granted = pltpu.CompilerParams(vmem_limit_bytes=VMEM_GRANT)


def paired(cycle, hops):
    return hops == 1 and cycle % 2 == 0


def source(place, part, cycle, pairs):
    if pairs:
        return place + 1 if place % 2 == part else place - 1
    return place - 1 if part == 0 else place + 1


def sent(x, share, pairs):
    cycle = lax.axis_size("ctx")
    heads = lax.axis_size("head")
    moves = [
        (source(place, head % share, cycle, pairs) % cycle * heads + head, place * heads + head)
        for place in range(cycle)
        for head in range(heads)
    ]
    return lax.ppermute(x, ("ctx", "head"), moves)


def swapped(x, mask):
    return lax.ppermute(x, "head", [(i, i ^ mask) for i in range(lax.axis_size("head"))])


def begin_kernel(index_hbm, table_hbm, keys_hbm, values_hbm, keys_ref, values_ref, *scratch):
    index_ref, table_ref, key_codes, value_codes, arrived = scratch
    groups = index_hbm.shape[1]
    kv_head = lax.axis_index("head") * groups // lax.axis_size("head")
    copies = [
        pltpu.make_async_copy(source, target, arrived.at[n])
        for n, (source, target) in enumerate(
            (
                (index_hbm, index_ref),
                (table_hbm, table_ref),
                (keys_hbm.at[kv_head], key_codes),
                (values_hbm.at[kv_head], value_codes),
            )
        )
    ]
    for copy in copies:
        copy.start()
    for copy in copies[:2]:
        copy.wait()
    blocks = keys_ref.shape[0]
    scales = [
        [table_ref[row, index_ref[row, kv_head, block]] for block in range(blocks)]
        for row in range(2)
    ]
    copies[2].wait()
    for block in range(blocks):
        codes = key_codes[block * BLOCK : (block + 1) * BLOCK, :].astype(jnp.float32)
        keys_ref[block] = (codes * scales[0][block]).T.astype(jnp.bfloat16)
    copies[3].wait()
    for block in range(blocks):
        codes = value_codes[block * BLOCK : (block + 1) * BLOCK, :].astype(jnp.float32)
        values_ref[block] = (codes * scales[1][block]).astype(jnp.bfloat16)


def begin(scale_index, scale_table, key_codes, value_codes):
    _, keys_dev, width = key_codes.shape
    blocks = keys_dev // BLOCK
    stay = functools.partial(pltpu.with_memory_space_constraint, memory_space=pltpu.HBM)
    return pl.pallas_call(
        begin_kernel,
        in_specs=[pl.BlockSpec(memory_space=pltpu.HBM)] * 4,
        out_specs=[in_vmem] * 2,
        out_shape=[
            pltpu.VMEM((blocks, width, BLOCK), jnp.bfloat16),
            pltpu.VMEM((blocks, BLOCK, width), jnp.bfloat16),
        ],
        scratch_shapes=[
            pltpu.SMEM(scale_index.shape, scale_index.dtype),
            pltpu.SMEM(scale_table.shape, scale_table.dtype),
            pltpu.VMEM((keys_dev, width), key_codes.dtype),
            pltpu.VMEM((keys_dev, width), value_codes.dtype),
            pltpu.SemaphoreType.DMA((4,)),
        ],
        compiler_params=granted,
        name="begin",
    )(stay(scale_index), stay(scale_table), stay(key_codes), stay(value_codes))


def turn_kernel(queries_ref, cosine_ref, sine_ref, lists_ref, own_ref, sibling_ref):
    heads_dev, rows, width = own_ref.shape
    cosine = cosine_ref[...]
    sine = sine_ref[...]
    even = lax.rem(lax.broadcasted_iota(jnp.int32, cosine.shape, 1), 2) == 0
    for head in range(heads_dev):
        plain = queries_ref[head].astype(jnp.float32)
        other = jnp.where(even, pltpu.roll(plain, width - 1, 1), pltpu.roll(plain, 1, 1))
        turned = (plain * cosine + other * sine).astype(jnp.bfloat16)
        own_ref[head] = turned[:rows]
        sibling_ref[head, :rows] = turned[rows:]
        sibling_ref[head, rows:] = jnp.broadcast_to(
            lists_ref[head : head + 1], sibling_ref[head, rows:].shape
        )


def turn_queries(queries, cosine, sine, lists):
    heads_dev, rows, width = queries.shape
    half = (heads_dev, rows // 2, width)
    more = (heads_dev, rows // 2 + ROW_TILE, width)
    return pl.pallas_call(
        turn_kernel,
        in_specs=[in_vmem] * 4,
        out_specs=[in_vmem] * 2,
        out_shape=[
            jax.ShapeDtypeStruct(half, jnp.bfloat16),
            jax.ShapeDtypeStruct(more, jnp.bfloat16),
        ],
        compiler_params=granted,
        name="turn_queries",
    )(queries, cosine, sine, lists)


def gather_parts(parts, store):
    at = 0
    for part in parts:
        store[at : at + part.shape[0]] = part[...]
        at += part.shape[0]


def score_kernel(slots_ref, own_ref, sibling_ref, _, *rest):
    *parts, weights_ref, total_ref, store = rest
    heads_dev, rows, width = own_ref.shape
    heads = slots_ref.shape[0]
    picks = slots_ref.shape[1]
    slots = slots_ref[...]
    factor = math.log2(math.e) / math.sqrt(width)
    gather_parts(parts, store)
    for head in range(heads):
        turned = (own_ref if head < heads_dev else sibling_ref)[head % heads_dev, :rows]
        scores = [
            jnp.dot(turned, store[slots[head, i]], preferred_element_type=jnp.float32)
            for i in range(picks)
        ]
        top = scores[0]
        for i in range(1, picks):
            top = jnp.maximum(top, scores[i])
        top = jnp.max(top, axis=1, keepdims=True)
        total = jnp.zeros((rows, BLOCK), jnp.float32)
        for i in range(picks):
            weight = jnp.exp2((scores[i] - top) * factor)
            total = total + weight
            weights_ref[head, :, i * BLOCK : (i + 1) * BLOCK] = weight.astype(jnp.bfloat16)
        total = jnp.sum(total, axis=1, keepdims=True)
        total_ref[head] = jnp.broadcast_to(total, (rows, width))


def block_weights(slots, own, sibling, extra, parts):
    _, rows, width = own.shape
    heads, picks = slots.shape
    blocks = sum(part.shape[0] for part in parts)
    return pl.pallas_call(
        score_kernel,
        in_specs=[in_vmem] * (4 + len(parts)),
        out_specs=[in_vmem, in_vmem],
        out_shape=[
            jax.ShapeDtypeStruct((heads, rows, picks * BLOCK), jnp.bfloat16),
            jax.ShapeDtypeStruct((heads, rows, width), jnp.float32),
        ],
        scratch_shapes=[pltpu.VMEM((blocks, width, BLOCK), jnp.bfloat16)],
        compiler_params=granted,
        name="block_weights",
    )(slots, own, sibling, extra, *parts)


def value_kernel(slots_ref, weights_ref, total_ref, *rest, inputs):
    parts = rest[:inputs]
    pieces = rest[inputs:-1]
    store = rest[-1]
    heads, _, width = total_ref.shape
    picks = slots_ref.shape[1]
    rows = pieces[0].shape[0]
    slots = slots_ref[...]
    gather_parts(parts, store)
    for head in range(heads):
        picked = jnp.concatenate([store[slots[head, i]] for i in range(picks)], axis=0)
        out = jnp.dot(weights_ref[head], picked, preferred_element_type=jnp.float32)
        out = out / total_ref[head]
        for n, piece in enumerate(pieces):
            piece[:, head * width : (head + 1) * width] = out[n * rows : (n + 1) * rows].astype(
                jnp.bfloat16
            )


def block_outputs(slots, weights, total, parts, pieces):
    heads, rows, width = total.shape
    blocks = sum(part.shape[0] for part in parts)
    piece = jax.ShapeDtypeStruct((rows // pieces, heads * width), jnp.bfloat16)
    return pl.pallas_call(
        functools.partial(value_kernel, inputs=len(parts)),
        in_specs=[in_vmem] * (3 + len(parts)),
        out_specs=[in_vmem] * pieces,
        out_shape=[piece] * pieces,
        scratch_shapes=[pltpu.VMEM((blocks, BLOCK, width), jnp.bfloat16)],
        compiler_params=granted,
        name="block_outputs",
    )(slots, weights, total, *parts)


def join_kernel(*refs, share):
    *pieces, out_ref = refs
    place = lax.axis_index("head")
    width = pieces[0].shape[1] // share
    for n, piece in enumerate(pieces):
        for part in range(share):
            column = pl.multiple_of(jnp.bitwise_xor(place, n * share + part) * width, width)
            out_ref[:, pl.ds(column, width)] = piece[:, part * width : (part + 1) * width]


def join_pieces(pieces, share):
    rows, width = pieces[0].shape
    return pl.pallas_call(
        functools.partial(join_kernel, share=share),
        in_specs=[in_vmem] * len(pieces),
        out_specs=in_vmem,
        out_shape=jax.ShapeDtypeStruct((rows, width * len(pieces)), jnp.bfloat16),
        compiler_params=granted,
        name="join_pieces",
    )(*pieces)


def on_device(queries, positions, key_codes, value_codes, scale_index, scale_table, block_lists):
    cycle_size = lax.axis_size("ctx")
    cycle_place = lax.axis_index("ctx")
    head_count = lax.axis_size("head")
    head_place = lax.axis_index("head")
    reach_hops = min(3, (cycle_size - 1) // 2)
    pairs = paired(cycle_size, reach_hops)
    rows_dev, heads_dev, head_width = queries.shape
    key_blocks = key_codes.shape[1] // BLOCK
    share = GROUP // heads_dev
    assert share == 2 and rows_dev == BLOCK
    core = head_place % share
    group = head_place // share
    groups = head_count // share

    keys, values = begin(scale_index, scale_table, key_codes, value_codes)
    far_keys = keys
    key_parts = []
    for _ in range(reach_hops):
        far_keys = sent(far_keys, share, pairs)
        key_parts.append(far_keys)
    values, queries, positions, block_lists = lax.optimization_barrier(
        (values, queries, positions, block_lists)
    )
    own_lists = lax.dynamic_index_in_dim(block_lists, cycle_place, 1, keepdims=False)
    def ordered(x):
        cut = x.reshape((groups, share, rows_dev // head_count) + x.shape[1:])
        taken = [
            lax.dynamic_slice(
                cut,
                (jnp.bitwise_xor(group, n), jnp.bitwise_xor(core, part)) + (0,) * x.ndim,
                (1, 1) + cut.shape[2:],
            )
            for part in range(share)
            for n in range(groups)
        ]
        return jnp.concatenate(taken, axis=0).reshape(x.shape)

    frequency = ROPE_BASE ** (
        -2.0 * (jnp.arange(head_width) // 2).astype(jnp.float32) / head_width
    )
    angles = ordered(positions).astype(jnp.float32)[:, None] * frequency[None, :]
    signs = jnp.where(jnp.arange(head_width) % 2 == 0, -1.0, 1.0)
    cosine = jnp.cos(angles)
    sine = jnp.sin(angles) * signs[None, :]

    picks = own_lists.shape[1]
    carried = jnp.pad(own_lists.astype(jnp.bfloat16), ((0, 0), (0, head_width - picks)))
    own, sibling = turn_queries(
        jnp.transpose(ordered(queries), (1, 0, 2)), cosine, sine, carried
    )
    sibling, key_parts[0] = lax.optimization_barrier((sibling, key_parts[0]))
    key_parts = [keys] + [part for far in key_parts for part in (far, swapped(far, 1))]
    sibling = swapped(sibling, 1)
    sibling_lists = sibling[:, rows_dev // share, :picks].astype(jnp.int32)
    lists = jnp.concatenate([own_lists, sibling_lists], axis=0)
    offset = jnp.mod(lists // key_blocks - cycle_place, cycle_size)
    above = offset <= reach_hops
    hops = jnp.where(above, offset, cycle_size - offset)
    from_above = (cycle_place % 2 if pairs else 1) == core
    place = 2 * hops - jnp.where(above == from_above, 1, 0)
    slots = lists % key_blocks + key_blocks * jnp.where(offset == 0, 0, place)

    value_steps = []
    far_values = values
    for _ in range(reach_hops):
        far_values = sent(far_values, share, pairs)
        value_steps.append(far_values)
    weights, total = block_weights(
        slots, own, sibling, scale_table[0][:, None], key_parts
    )

    *value_steps, weights = lax.optimization_barrier((*value_steps, weights))
    value_parts = [values]
    for step in value_steps:
        value_parts += [step, swapped(step, 1)]
    pieces = block_outputs(slots, weights, total, value_parts, groups)
    moved = [pieces[0]] + [swapped(pieces[n], n * share) for n in range(1, groups)]
    return join_pieces(moved, share)


def solution(mesh):
    placed = (
        P(("groups", "ctx"), "head", None),
        P(("groups", "ctx")),
        P("groups", "ctx", None),
        P("groups", "ctx", None),
        P("groups", None, "ctx"),
        P(),
        P(("groups", "head"), None, None),
    )
    return jax.shard_map(
        on_device,
        mesh=mesh,
        in_specs=placed,
        out_specs=P(("groups", "ctx", "head"), None),
        check_vma=False,
    )
```

```python
import functools
import math

import jax
import jax.numpy as jnp
from jax import lax
from jax.experimental import pallas as pl
from jax.experimental.pallas import tpu as pltpu
from jax.sharding import PartitionSpec as P

GROUP = 16
BLOCK = 128
ROW_TILE = 16
ROPE_BASE = 500000.0
VMEM_GRANT = 16 * 2**20

in_vmem = pl.BlockSpec(memory_space=pltpu.VMEM)
granted = pltpu.CompilerParams(vmem_limit_bytes=VMEM_GRANT)


def paired(cycle, hops):
    return hops == 1 and cycle % 2 == 0


def source(place, part, cycle, pairs):
    if pairs:
        return place + 1 if place % 2 == part else place - 1
    return place - 1 if part == 0 else place + 1


def sent(x, share, pairs):
    cycle = lax.axis_size("ctx")
    heads = lax.axis_size("head")
    moves = [
        (source(place, head % share, cycle, pairs) % cycle * heads + head, place * heads + head)
        for place in range(cycle)
        for head in range(heads)
    ]
    return lax.ppermute(x, ("ctx", "head"), moves)


def swapped(x, mask):
    return lax.ppermute(x, "head", [(i, i ^ mask) for i in range(lax.axis_size("head"))])


def lower_half(shape):
    return lax.broadcasted_iota(jnp.int32, shape, 1) < shape[1] // 2


def begin_kernel(index_hbm, table_hbm, keys_hbm, values_hbm, keys_ref, *rest):
    first_ref, second_ref, index_ref, table_ref, key_codes, value_codes, arrived = rest
    groups = index_hbm.shape[1]
    kv_head = lax.axis_index("head") * groups // lax.axis_size("head")
    copies = [
        pltpu.make_async_copy(source, target, arrived.at[n])
        for n, (source, target) in enumerate(
            (
                (index_hbm, index_ref),
                (table_hbm, table_ref),
                (keys_hbm.at[kv_head], key_codes),
                (values_hbm.at[kv_head], value_codes),
            )
        )
    ]
    for copy in copies:
        copy.start()
    for copy in copies[:2]:
        copy.wait()
    blocks = keys_ref.shape[0]
    scales = [
        [table_ref[row, index_ref[row, kv_head, block]] for block in range(blocks)]
        for row in range(2)
    ]
    copies[2].wait()
    for block in range(blocks):
        codes = key_codes[block * BLOCK : (block + 1) * BLOCK, :].astype(jnp.float32)
        keys_ref[block] = (codes * scales[0][block]).T.astype(jnp.bfloat16)
    copies[3].wait()
    pairs = first_ref.shape[0]
    width = value_codes.shape[1]
    low = lower_half((BLOCK, width))
    for pair in range(pairs):
        left, right = (
            value_codes[block * BLOCK : (block + 1) * BLOCK, :].astype(jnp.float32)
            * scales[1][block]
            for block in (pair, pair + pairs)
        )
        first = jnp.where(low, left, pltpu.roll(right, width // 2, 1))
        second = jnp.where(low, pltpu.roll(left, width // 2, 1), right)
        first_ref[pair] = first.astype(jnp.bfloat16)
        second_ref[pair] = second.astype(jnp.bfloat16)


def begin(scale_index, scale_table, key_codes, value_codes):
    _, keys_dev, width = key_codes.shape
    blocks = keys_dev // BLOCK
    stay = functools.partial(pltpu.with_memory_space_constraint, memory_space=pltpu.HBM)
    return pl.pallas_call(
        begin_kernel,
        in_specs=[pl.BlockSpec(memory_space=pltpu.HBM)] * 4,
        out_specs=[in_vmem] * 3,
        out_shape=[
            pltpu.VMEM((blocks, width, BLOCK), jnp.bfloat16),
            pltpu.VMEM((blocks // 2, BLOCK, width), jnp.bfloat16),
            pltpu.VMEM((blocks // 2, BLOCK, width), jnp.bfloat16),
        ],
        scratch_shapes=[
            pltpu.SMEM(scale_index.shape, scale_index.dtype),
            pltpu.SMEM(scale_table.shape, scale_table.dtype),
            pltpu.VMEM((keys_dev, width), key_codes.dtype),
            pltpu.VMEM((keys_dev, width), value_codes.dtype),
            pltpu.SemaphoreType.DMA((4,)),
        ],
        compiler_params=granted,
        name="begin",
    )(stay(scale_index), stay(scale_table), stay(key_codes), stay(value_codes))


def turn_kernel(queries_ref, cosine_ref, sine_ref, lists_ref, own_ref, sibling_ref):
    heads_dev, rows, width = own_ref.shape
    cosine = cosine_ref[...]
    sine = sine_ref[...]
    even = lax.rem(lax.broadcasted_iota(jnp.int32, cosine.shape, 1), 2) == 0
    for head in range(heads_dev):
        plain = queries_ref[head].astype(jnp.float32)
        other = jnp.where(even, pltpu.roll(plain, width - 1, 1), pltpu.roll(plain, 1, 1))
        turned = (plain * cosine + other * sine).astype(jnp.bfloat16)
        own_ref[head] = turned[:rows]
        sibling_ref[head, :rows] = turned[rows:]
        sibling_ref[head, rows:] = jnp.broadcast_to(
            lists_ref[head : head + 1], sibling_ref[head, rows:].shape
        )


def turn_queries(queries, cosine, sine, lists):
    heads_dev, rows, width = queries.shape
    half = (heads_dev, rows // 2, width)
    more = (heads_dev, rows // 2 + ROW_TILE, width)
    return pl.pallas_call(
        turn_kernel,
        in_specs=[in_vmem] * 4,
        out_specs=[in_vmem] * 2,
        out_shape=[
            jax.ShapeDtypeStruct(half, jnp.bfloat16),
            jax.ShapeDtypeStruct(more, jnp.bfloat16),
        ],
        compiler_params=granted,
        name="turn_queries",
    )(queries, cosine, sine, lists)


def gather_parts(parts, store):
    at = 0
    for part in parts:
        store[at : at + part.shape[0]] = part[...]
        at += part.shape[0]


def score_kernel(slots_ref, queries_ref, *rest, inputs):
    parts = rest[:inputs]
    weights_ref, total_ref, store = rest[-3:]
    heads, rows, width = total_ref.shape
    picks = slots_ref.shape[1]
    slots = slots_ref[...]
    factor = math.log2(math.e) / math.sqrt(width)
    gather_parts(parts, store)
    for head in range(heads):
        turned = queries_ref[head, :rows]
        scores = [
            jnp.dot(turned, store[slots[head, i]], preferred_element_type=jnp.float32)
            for i in range(picks)
        ]
        top = scores[0]
        for i in range(1, picks):
            top = jnp.maximum(top, scores[i])
        top = jnp.max(top, axis=1, keepdims=True)
        total = jnp.zeros((rows, BLOCK), jnp.float32)
        for i in range(picks):
            weight = jnp.exp2((scores[i] - top) * factor)
            total = total + weight
            weights_ref[head, :, i * BLOCK : (i + 1) * BLOCK] = weight.astype(jnp.bfloat16)
        total = jnp.sum(total, axis=1, keepdims=True)
        total_ref[head] = jnp.broadcast_to(1.0 / total, (rows, width))


def block_weights(slots, queries, parts, rows, *extra):
    width = queries.shape[2]
    heads, picks = slots.shape
    blocks = sum(part.shape[0] for part in parts)
    return pl.pallas_call(
        functools.partial(score_kernel, inputs=len(parts)),
        in_specs=[in_vmem] * (2 + len(parts) + len(extra)),
        out_specs=[in_vmem, in_vmem],
        out_shape=[
            jax.ShapeDtypeStruct((heads, rows, picks * BLOCK), jnp.bfloat16),
            jax.ShapeDtypeStruct((heads, rows, width), jnp.float32),
        ],
        scratch_shapes=[pltpu.VMEM((blocks, width, BLOCK), jnp.bfloat16)],
        compiler_params=granted,
        name="block_weights",
    )(slots, queries, *parts, *extra)


def value_kernel(slots_ref, *rest, inputs, flip, first, last):
    weights = rest[:2]
    totals = rest[2:4]
    parts = rest[4 : 4 + inputs]
    pieces = rest[4 + inputs : -1]
    store = rest[-1]
    heads_dev, _, width = totals[0].shape
    heads, picks = slots_ref.shape
    rows = pieces[0].shape[0]
    slots = slots_ref[...]
    half = store.shape[0] // 2
    at = 0
    for part in parts:
        for pair in range(part.shape[0]):
            block = part[pair]
            store[at] = block
            turned = pltpu.roll(block.astype(jnp.float32), width // 2, 1)
            store[half + at] = turned.astype(jnp.bfloat16)
            at += 1
    low = lower_half((last - first, width))
    for pair in range(heads // 2):
        both = []
        for head in (2 * pair, 2 * pair + 1):
            picked = jnp.concatenate([store[slots[head, i]] for i in range(picks)], axis=0)
            owner, place = divmod(head, heads_dev)
            weight = weights[owner][place, first:last]
            out = jnp.dot(weight, picked, preferred_element_type=jnp.float32)
            both.append(out * totals[owner][place, first:last])
        out = jnp.where(low, both[flip], both[1 - flip])
        for n, piece in enumerate(pieces):
            piece[:, pair * width : (pair + 1) * width] = out[n * rows : (n + 1) * rows].astype(
                jnp.bfloat16
            )


def block_outputs(slots, weights, totals, parts, pieces, flip, first, last):
    heads = slots.shape[0]
    _, rows, width = totals[0].shape
    pairs = sum(part.shape[0] for part in parts)
    rows //= pieces
    pieces = last - first
    piece = jax.ShapeDtypeStruct((rows, heads // 2 * width), jnp.bfloat16)
    return pl.pallas_call(
        functools.partial(
            value_kernel,
            inputs=len(parts),
            flip=flip,
            first=first * rows,
            last=last * rows,
        ),
        in_specs=[in_vmem] * (5 + len(parts)),
        out_specs=[in_vmem] * pieces,
        out_shape=[piece] * pieces,
        scratch_shapes=[pltpu.VMEM((2 * pairs, BLOCK, width), jnp.bfloat16)],
        compiler_params=granted,
        name="block_outputs",
    )(slots, *weights, *totals, *parts)


def join_kernel(*refs, share, width):
    *pieces, out_ref = refs
    place = lax.axis_index("head")
    chips = len(pieces) // 2
    rows = out_ref.shape[0]
    pairs = pieces[0].shape[1] // width // share
    low = lower_half((rows, width))
    for n in range(chips):
        for part in range(share):
            column = jnp.bitwise_xor(place, n * share + part) * (2 * pairs * width)
            for pair in range(pairs):
                at = (part * pairs + pair) * width
                first, second = (
                    piece[:, at : at + width].astype(jnp.float32)
                    for piece in (pieces[n], pieces[chips + n])
                )
                even = jnp.where(low, first, second)
                odd = pltpu.roll(jnp.where(low, second, first), width // 2, 1)
                for m, out in enumerate((even, odd)):
                    to = pl.multiple_of(column + (2 * pair + m) * width, width)
                    out_ref[:, pl.ds(to, width)] = out.astype(jnp.bfloat16)


def join_pieces(pieces, share, width):
    rows, across = pieces[0].shape
    return pl.pallas_call(
        functools.partial(join_kernel, share=share, width=width),
        in_specs=[in_vmem] * len(pieces),
        out_specs=in_vmem,
        out_shape=jax.ShapeDtypeStruct((rows, across * len(pieces)), jnp.bfloat16),
        compiler_params=granted,
        name="join_pieces",
    )(*pieces)


def on_device(queries, positions, key_codes, value_codes, scale_index, scale_table, block_lists):
    cycle_size = lax.axis_size("ctx")
    cycle_place = lax.axis_index("ctx")
    head_count = lax.axis_size("head")
    head_place = lax.axis_index("head")
    reach_hops = min(3, (cycle_size - 1) // 2)
    pairs = paired(cycle_size, reach_hops)
    rows_dev, heads_dev, head_width = queries.shape
    key_blocks = key_codes.shape[1] // BLOCK
    share = GROUP // heads_dev
    assert share == 2 and rows_dev == BLOCK
    core = head_place % share
    group = head_place // share
    groups = head_count // share

    keys, *values = begin(scale_index, scale_table, key_codes, value_codes)
    far_keys = keys
    key_parts = []
    for _ in range(reach_hops):
        far_keys = sent(far_keys, share, pairs)
        key_parts.append(far_keys)
    *values, queries, positions, block_lists = lax.optimization_barrier(
        (*values, queries, positions, block_lists)
    )
    own_lists = lax.dynamic_index_in_dim(block_lists, cycle_place, 1, keepdims=False)
    def ordered(x):
        cut = x.reshape((groups, share, rows_dev // head_count) + x.shape[1:])
        taken = [
            lax.dynamic_slice(
                cut,
                (jnp.bitwise_xor(group, n), jnp.bitwise_xor(core, part)) + (0,) * x.ndim,
                (1, 1) + cut.shape[2:],
            )
            for part in range(share)
            for n in range(groups)
        ]
        return jnp.concatenate(taken, axis=0).reshape(x.shape)

    frequency = ROPE_BASE ** (
        -2.0 * (jnp.arange(head_width) // 2).astype(jnp.float32) / head_width
    )
    angles = ordered(positions).astype(jnp.float32)[:, None] * frequency[None, :]
    signs = jnp.where(jnp.arange(head_width) % 2 == 0, -1.0, 1.0)
    cosine = jnp.cos(angles)
    sine = jnp.sin(angles) * signs[None, :]

    picks = own_lists.shape[1]
    carried = jnp.pad(own_lists.astype(jnp.bfloat16), ((0, 0), (0, head_width - picks)))
    own, sibling = turn_queries(
        jnp.transpose(ordered(queries), (1, 0, 2)), cosine, sine, carried
    )
    sibling, key_parts[0] = lax.optimization_barrier((sibling, key_parts[0]))
    key_parts = [keys] + [part for far in key_parts for part in (far, swapped(far, 1))]
    sibling = swapped(sibling, 1)
    sibling_lists = sibling[:, rows_dev // share, :picks].astype(jnp.int32)
    lists = jnp.concatenate([own_lists, sibling_lists], axis=0)
    offset = jnp.mod(lists // key_blocks - cycle_place, cycle_size)
    above = offset <= reach_hops
    hops = jnp.where(above, offset, cycle_size - offset)
    from_above = (cycle_place % 2 if pairs else 1) == core
    place = 2 * hops - jnp.where(above == from_above, 1, 0)
    slots = lists % key_blocks + key_blocks * jnp.where(offset == 0, 0, place)

    steps = []
    far_values = values
    for _ in range(reach_hops):
        far_values = [sent(half, share, pairs) for half in far_values]
        steps.append(far_values)
    rows = rows_dev // share
    own_weights, own_total = block_weights(slots[:heads_dev], own, key_parts, rows)
    sibling_weights, sibling_total = block_weights(slots[heads_dev:], sibling, key_parts, rows)
    weights = (own_weights, sibling_weights)
    totals = (own_total, sibling_total)

    inner = slots % key_blocks
    places = slots // key_blocks * (key_blocks // 2) + inner % (key_blocks // 2)
    parity = jnp.arange(slots.shape[0])[:, None] % 2
    turned_places = (2 * reach_hops + 1) * (key_blocks // 2)
    ready = own_weights
    moved = []
    for half in range(2):
        *far_values, ready = lax.optimization_barrier((*[step[half] for step in steps], ready))
        value_parts = [values[half]]
        for far in far_values:
            value_parts += [far, swapped(far, 1)]
        side = jnp.bitwise_xor(inner // (key_blocks // 2), jnp.bitwise_xor(parity, half))
        outputs = functools.partial(
            block_outputs,
            places + turned_places * side,
            weights,
            totals,
            value_parts,
            groups,
            half,
        )
        if half == 0 or groups == 1:
            pieces = outputs(0, groups)
        else:
            pieces = [None, *outputs(1, groups)]
        sent_pieces = [swapped(pieces[n], n * share) for n in range(1, groups)]
        if pieces[0] is None:
            pieces[0] = outputs(0, 1)[0]
        moved += [pieces[0], *sent_pieces]
        ready = pieces[0]
    return join_pieces(moved, share, head_width)


def solution(mesh):
    placed = (
        P(("groups", "ctx"), "head", None),
        P(("groups", "ctx")),
        P("groups", "ctx", None),
        P("groups", "ctx", None),
        P("groups", None, "ctx"),
        P(),
        P(("groups", "head"), None, None),
    )
    return jax.shard_map(
        on_device,
        mesh=mesh,
        in_specs=placed,
        out_specs=P(("groups", "ctx", "head"), None),
        check_vma=False,
    )
```

```python
import functools
import math

import jax
import jax.numpy as jnp
from jax import lax
from jax.experimental import pallas as pl
from jax.experimental.pallas import tpu as pltpu
from jax.sharding import PartitionSpec as P

GROUP = 16
BLOCK = 128
ROW_TILE = 16
ROPE_BASE = 500000.0
VMEM_GRANT = 16 * 2**20

in_vmem = pl.BlockSpec(memory_space=pltpu.VMEM)
granted = pltpu.CompilerParams(vmem_limit_bytes=VMEM_GRANT)


def paired(cycle, hops):
    return hops == 1 and cycle % 2 == 0


def source(place, part, cycle, pairs):
    if pairs:
        return place + 1 if place % 2 == part else place - 1
    return place - 1 if part == 0 else place + 1


def sent(x, share, pairs):
    cycle = lax.axis_size("ctx")
    heads = lax.axis_size("head")
    moves = [
        (source(place, head % share, cycle, pairs) % cycle * heads + head, place * heads + head)
        for place in range(cycle)
        for head in range(heads)
    ]
    return lax.ppermute(x, ("ctx", "head"), moves)


def across(n, share):
    return n * share ^ n % share


def swapped(x, mask):
    return lax.ppermute(x, "head", [(i, i ^ mask) for i in range(lax.axis_size("head"))])


def fetch(index_hbm, table_hbm, codes_hbm, index_ref, table_ref, codes_ref, arrived, row):
    groups = index_hbm.shape[1]
    kv_head = lax.axis_index("head") * groups // lax.axis_size("head")
    copies = [
        pltpu.make_async_copy(source, target, arrived.at[n])
        for n, (source, target) in enumerate(
            (
                (index_hbm, index_ref),
                (table_hbm, table_ref),
                (codes_hbm.at[kv_head], codes_ref),
            )
        )
    ]
    for copy in copies:
        copy.start()
    for copy in copies[:2]:
        copy.wait()
    scales = [
        table_ref[row, index_ref[row, kv_head, block]] for block in range(index_hbm.shape[2])
    ]
    copies[2].wait()
    return scales


def key_kernel(index_hbm, table_hbm, codes_hbm, out_ref, *scratch):
    codes_ref = scratch[2]
    for block, scale in enumerate(fetch(index_hbm, table_hbm, codes_hbm, *scratch, 0)):
        codes = codes_ref[block * BLOCK : (block + 1) * BLOCK, :].astype(jnp.float32)
        out_ref[block] = (codes * scale).T.astype(jnp.bfloat16)


def half_kernel(index_hbm, table_hbm, codes_hbm, _, *rest):
    *others, index_ref, table_ref, codes_ref, arrived = rest
    scratch = (index_ref, table_ref, codes_ref, arrived)
    count = len(others) // 2 - 1
    first_ref, second_ref = others[count : count + 2]
    copies = [
        pltpu.make_async_copy(others[n], others[count + 2 + n], arrived.at[3 + n])
        for n in range(count)
    ]
    for copy in copies:
        copy.start()
    scales = fetch(index_hbm, table_hbm, codes_hbm, *scratch, 1)
    pairs = first_ref.shape[0]
    width = codes_ref.shape[1]
    low = lower_half((BLOCK, width))
    for pair in range(pairs):
        left, right = (
            codes_ref[block * BLOCK : (block + 1) * BLOCK, :].astype(jnp.float32) * scales[block]
            for block in (pair, pair + pairs)
        )
        first = jnp.where(low, left, pltpu.roll(right, width // 2, 1))
        second = jnp.where(low, pltpu.roll(left, width // 2, 1), right)
        first_ref[pair] = first.astype(jnp.bfloat16)
        second_ref[pair] = second.astype(jnp.bfloat16)
    for copy in copies:
        copy.wait()


def lower_half(shape):
    return lax.broadcasted_iota(jnp.int32, shape, 1) < shape[1] // 2


def begin(kernel, scale_index, scale_table, codes, outputs, *after, others=()):
    _, keys_dev, width = codes.shape
    blocks = keys_dev // BLOCK // outputs
    stay = functools.partial(pltpu.with_memory_space_constraint, memory_space=pltpu.HBM)
    return pl.pallas_call(
        kernel,
        in_specs=[pl.BlockSpec(memory_space=pltpu.HBM)] * 3
        + [pl.BlockSpec(memory_space=pl.ANY)] * len(after)
        + [pl.BlockSpec(memory_space=pltpu.HBM)] * len(others),
        out_specs=[in_vmem] * (outputs + len(others)),
        out_shape=[pltpu.VMEM((blocks, BLOCK, width), jnp.bfloat16)] * outputs
        + [pltpu.VMEM(other.shape, other.dtype) for other in others],
        scratch_shapes=[
            pltpu.SMEM(scale_index.shape, scale_index.dtype),
            pltpu.SMEM(scale_table.shape, scale_table.dtype),
            pltpu.VMEM((keys_dev, width), codes.dtype),
            pltpu.SemaphoreType.DMA((3 + len(others),)),
        ],
        compiler_params=granted,
        name=kernel.__name__,
    )(
        stay(scale_index),
        stay(scale_table),
        stay(codes),
        *after,
        *[stay(other) for other in others],
    )


def turn_kernel(queries_ref, cosine_ref, sine_ref, lists_ref, own_ref, sibling_ref):
    heads_dev, rows, width = own_ref.shape
    cosine = cosine_ref[...]
    sine = sine_ref[...]
    even = lax.rem(lax.broadcasted_iota(jnp.int32, cosine.shape, 1), 2) == 0
    for head in range(heads_dev):
        plain = queries_ref[head].astype(jnp.float32)
        other = jnp.where(even, pltpu.roll(plain, width - 1, 1), pltpu.roll(plain, 1, 1))
        turned = (plain * cosine + other * sine).astype(jnp.bfloat16)
        own_ref[head] = turned[:rows]
        sibling_ref[head, :rows] = turned[rows:]
        sibling_ref[head, rows:] = jnp.broadcast_to(
            lists_ref[head : head + 1], sibling_ref[head, rows:].shape
        )


def turn_queries(queries, cosine, sine, lists):
    heads_dev, rows, width = queries.shape
    half = (heads_dev, rows // 2, width)
    more = (heads_dev, rows // 2 + ROW_TILE, width)
    return pl.pallas_call(
        turn_kernel,
        in_specs=[in_vmem] * 4,
        out_specs=[in_vmem] * 2,
        out_shape=[
            jax.ShapeDtypeStruct(half, jnp.bfloat16),
            jax.ShapeDtypeStruct(more, jnp.bfloat16),
        ],
        compiler_params=granted,
        name="turn_queries",
    )(queries, cosine, sine, lists)


def gather_parts(parts, store):
    at = 0
    for part in parts:
        store[at : at + part.shape[0]] = part[...]
        at += part.shape[0]


def score_kernel(slots_ref, queries_ref, *rest, inputs):
    parts = rest[:inputs]
    weights_ref, total_ref, store = rest[-3:]
    heads, rows, width = total_ref.shape
    picks = slots_ref.shape[1]
    slots = slots_ref[...]
    factor = math.log2(math.e) / math.sqrt(width)
    gather_parts(parts, store)
    for head in range(heads):
        turned = queries_ref[head, :rows]
        scores = [
            jnp.dot(turned, store[slots[head, i]], preferred_element_type=jnp.float32)
            for i in range(picks)
        ]
        top = scores[0]
        for i in range(1, picks):
            top = jnp.maximum(top, scores[i])
        top = jnp.max(top, axis=1, keepdims=True)
        total = jnp.zeros((rows, BLOCK), jnp.float32)
        for i in range(picks):
            weight = jnp.exp2((scores[i] - top) * factor)
            total = total + weight
            weights_ref[head, :, i * BLOCK : (i + 1) * BLOCK] = weight.astype(jnp.bfloat16)
        total = jnp.sum(total, axis=1, keepdims=True)
        total_ref[head] = jnp.broadcast_to(1.0 / total, (rows, width))


def block_weights(slots, queries, parts, rows, *extra):
    width = queries.shape[2]
    heads, picks = slots.shape
    blocks = sum(part.shape[0] for part in parts)
    return pl.pallas_call(
        functools.partial(score_kernel, inputs=len(parts)),
        in_specs=[in_vmem] * (2 + len(parts) + len(extra)),
        out_specs=[in_vmem, in_vmem],
        out_shape=[
            jax.ShapeDtypeStruct((heads, rows, picks * BLOCK), jnp.bfloat16),
            jax.ShapeDtypeStruct((heads, rows, width), jnp.float32),
        ],
        scratch_shapes=[pltpu.VMEM((blocks, width, BLOCK), jnp.bfloat16)],
        compiler_params=granted,
        name="block_weights",
    )(slots, queries, *parts, *extra)


def value_kernel(slots_ref, *rest, inputs, flip, first, last):
    weights = rest[:2]
    totals = rest[2:4]
    parts = rest[4 : 4 + inputs]
    pieces = rest[4 + inputs : -1]
    store = rest[-1]
    heads_dev, _, width = totals[0].shape
    heads, picks = slots_ref.shape
    rows = pieces[0].shape[0]
    slots = slots_ref[...]
    half = store.shape[0] // 2
    at = 0
    for part in parts:
        for pair in range(part.shape[0]):
            block = part[pair]
            store[at] = block
            turned = pltpu.roll(block.astype(jnp.float32), width // 2, 1)
            store[half + at] = turned.astype(jnp.bfloat16)
            at += 1
    low = lower_half((last - first, width))
    for pair in range(heads // 2):
        both = []
        for head in (2 * pair, 2 * pair + 1):
            picked = jnp.concatenate([store[slots[head, i]] for i in range(picks)], axis=0)
            owner, place = divmod(head, heads_dev)
            weight = weights[owner][place, first:last]
            out = jnp.dot(weight, picked, preferred_element_type=jnp.float32)
            both.append(out * totals[owner][place, first:last])
        out = jnp.where(low, both[flip], both[1 - flip])
        for n, piece in enumerate(pieces):
            piece[:, pair * width : (pair + 1) * width] = out[n * rows : (n + 1) * rows].astype(
                jnp.bfloat16
            )


def block_outputs(slots, weights, totals, parts, pieces, flip, first, last):
    heads = slots.shape[0]
    _, rows, width = totals[0].shape
    pairs = sum(part.shape[0] for part in parts)
    rows //= pieces
    pieces = last - first
    piece = jax.ShapeDtypeStruct((rows, heads // 2 * width), jnp.bfloat16)
    return pl.pallas_call(
        functools.partial(
            value_kernel,
            inputs=len(parts),
            flip=flip,
            first=first * rows,
            last=last * rows,
        ),
        in_specs=[in_vmem] * (5 + len(parts)),
        out_specs=[in_vmem] * pieces,
        out_shape=[piece] * pieces,
        scratch_shapes=[pltpu.VMEM((2 * pairs, BLOCK, width), jnp.bfloat16)],
        compiler_params=granted,
        name="block_outputs",
    )(slots, *weights, *totals, *parts)


def join_kernel(*refs, share, width):
    *pieces, out_ref = refs
    place = lax.axis_index("head")
    chips = len(pieces) // 2
    rows = out_ref.shape[0]
    pairs = pieces[0].shape[1] // width // share
    low = lower_half((rows, width))
    for n in range(chips):
        for part in range(share):
            column = jnp.bitwise_xor(place, across(n, share) ^ part) * (2 * pairs * width)
            for pair in range(pairs):
                at = (part * pairs + pair) * width
                first, second = (
                    piece[:, at : at + width].astype(jnp.float32)
                    for piece in (pieces[n], pieces[chips + n])
                )
                even = jnp.where(low, first, second)
                odd = pltpu.roll(jnp.where(low, second, first), width // 2, 1)
                for m, out in enumerate((even, odd)):
                    to = pl.multiple_of(column + (2 * pair + m) * width, width)
                    out_ref[:, pl.ds(to, width)] = out.astype(jnp.bfloat16)


def join_pieces(pieces, share, width):
    rows, across = pieces[0].shape
    return pl.pallas_call(
        functools.partial(join_kernel, share=share, width=width),
        in_specs=[in_vmem] * len(pieces),
        out_specs=in_vmem,
        out_shape=jax.ShapeDtypeStruct((rows, across * len(pieces)), jnp.bfloat16),
        compiler_params=granted,
        name="join_pieces",
    )(*pieces)


def on_device(queries, positions, key_codes, value_codes, scale_index, scale_table, block_lists):
    cycle_size = lax.axis_size("ctx")
    cycle_place = lax.axis_index("ctx")
    head_count = lax.axis_size("head")
    head_place = lax.axis_index("head")
    reach_hops = min(3, (cycle_size - 1) // 2)
    pairs = paired(cycle_size, reach_hops)
    rows_dev, heads_dev, head_width = queries.shape
    key_blocks = key_codes.shape[1] // BLOCK
    share = GROUP // heads_dev
    assert share == 2 and rows_dev == BLOCK
    core = head_place % share
    group = head_place // share
    groups = head_count // share

    (keys,) = begin(key_kernel, scale_index, scale_table, key_codes, 1)
    *values, queries, positions, block_lists = begin(
        half_kernel,
        scale_index,
        scale_table,
        value_codes,
        2,
        keys,
        others=(queries, positions, block_lists),
    )
    far_keys = keys
    key_parts = []
    for _ in range(reach_hops):
        far_keys = sent(far_keys, share, pairs)
        key_parts.append(far_keys)
    own_lists = lax.dynamic_index_in_dim(block_lists, cycle_place, 1, keepdims=False)
    def ordered(x):
        cut = x.reshape((groups, share, rows_dev // head_count) + x.shape[1:])
        taken = [
            lax.dynamic_slice(
                cut,
                (jnp.bitwise_xor(group, n), jnp.bitwise_xor(core, part ^ n % share))
                + (0,) * x.ndim,
                (1, 1) + cut.shape[2:],
            )
            for part in range(share)
            for n in range(groups)
        ]
        return jnp.concatenate(taken, axis=0).reshape(x.shape)

    frequency = ROPE_BASE ** (
        -2.0 * (jnp.arange(head_width) // 2).astype(jnp.float32) / head_width
    )
    angles = ordered(positions).astype(jnp.float32)[:, None] * frequency[None, :]
    signs = jnp.where(jnp.arange(head_width) % 2 == 0, -1.0, 1.0)
    cosine = jnp.cos(angles)
    sine = jnp.sin(angles) * signs[None, :]

    picks = own_lists.shape[1]
    carried = jnp.pad(own_lists.astype(jnp.bfloat16), ((0, 0), (0, head_width - picks)))
    own, sibling = turn_queries(
        jnp.transpose(ordered(queries), (1, 0, 2)), cosine, sine, carried
    )
    sibling, key_parts[0] = lax.optimization_barrier((sibling, key_parts[0]))
    key_parts = [keys] + [part for far in key_parts for part in (far, swapped(far, 1))]
    sibling = swapped(sibling, 1)
    sibling_lists = sibling[:, rows_dev // share, :picks].astype(jnp.int32)
    lists = jnp.concatenate([own_lists, sibling_lists], axis=0)
    offset = jnp.mod(lists // key_blocks - cycle_place, cycle_size)
    above = offset <= reach_hops
    hops = jnp.where(above, offset, cycle_size - offset)
    from_above = (cycle_place % 2 if pairs else 1) == core
    place = 2 * hops - jnp.where(above == from_above, 1, 0)
    slots = lists % key_blocks + key_blocks * jnp.where(offset == 0, 0, place)

    steps = []
    far_values = values
    for _ in range(reach_hops):
        far_values = [sent(half, share, pairs) for half in far_values]
        steps.append(far_values)
    rows = rows_dev // share
    own_weights, own_total = block_weights(slots[:heads_dev], own, key_parts, rows)
    sibling_weights, sibling_total = block_weights(slots[heads_dev:], sibling, key_parts, rows)
    weights = (own_weights, sibling_weights)
    totals = (own_total, sibling_total)

    inner = slots % key_blocks
    places = slots // key_blocks * (key_blocks // 2) + inner % (key_blocks // 2)
    parity = jnp.arange(slots.shape[0])[:, None] % 2
    turned_places = (2 * reach_hops + 1) * (key_blocks // 2)
    ready = own_weights
    moved = []
    for half in range(2):
        *far_values, ready = lax.optimization_barrier((*[step[half] for step in steps], ready))
        value_parts = [values[half]]
        for far in far_values:
            value_parts += [far, swapped(far, 1)]
        side = jnp.bitwise_xor(inner // (key_blocks // 2), jnp.bitwise_xor(parity, half))
        outputs = functools.partial(
            block_outputs,
            places + turned_places * side,
            weights,
            totals,
            value_parts,
            groups,
            half,
        )
        if half == 0 or groups == 1:
            pieces = outputs(0, groups)
        else:
            pieces = [None, *outputs(1, groups)]
        sent_pieces = [swapped(pieces[n], across(n, share)) for n in range(1, groups)]
        if pieces[0] is None:
            pieces[0] = outputs(0, 1)[0]
        moved += [pieces[0], *sent_pieces]
        ready = pieces[0]
    return join_pieces(moved, share, head_width)


def solution(mesh):
    placed = (
        P(("groups", "ctx"), "head", None),
        P(("groups", "ctx")),
        P("groups", "ctx", None),
        P("groups", "ctx", None),
        P("groups", None, "ctx"),
        P(),
        P(("groups", "head"), None, None),
    )
    return jax.shard_map(
        on_device,
        mesh=mesh,
        in_specs=placed,
        out_specs=P(("groups", "ctx", "head"), None),
        check_vma=False,
    )
```

```python
import functools
import math

import jax
import jax.numpy as jnp
from jax import lax
from jax.experimental import pallas as pl
from jax.experimental.pallas import tpu as pltpu
from jax.sharding import PartitionSpec as P

GROUP = 16
BLOCK = 128
ROW_TILE = 16
ABREAST = 2
ROPE_BASE = 500000.0
VMEM_GRANT = 16 * 2**20

in_vmem = pl.BlockSpec(memory_space=pltpu.VMEM)
granted = pltpu.CompilerParams(vmem_limit_bytes=VMEM_GRANT)


def paired(cycle, hops):
    return hops == 1 and cycle % 2 == 0


def source(place, part, cycle, pairs):
    if pairs:
        return place + 1 if place % 2 == part else place - 1
    return place - 1 if part == 0 else place + 1


def sent(x, share, pairs):
    cycle = lax.axis_size("ctx")
    heads = lax.axis_size("head")
    moves = [
        (source(place, head % share, cycle, pairs) % cycle * heads + head, place * heads + head)
        for place in range(cycle)
        for head in range(heads)
    ]
    return lax.ppermute(x, ("ctx", "head"), moves)


def across(n, share):
    return n * share ^ n % share


def swapped(x, mask):
    return lax.ppermute(x, "head", [(i, i ^ mask) for i in range(lax.axis_size("head"))])


def fetch(index_hbm, table_hbm, codes_hbm, index_ref, table_ref, codes_ref, arrived, row):
    groups = index_hbm.shape[1]
    kv_head = lax.axis_index("head") * groups // lax.axis_size("head")
    copies = [
        pltpu.make_async_copy(source, target, arrived.at[n])
        for n, (source, target) in enumerate(
            (
                (index_hbm, index_ref),
                (table_hbm, table_ref),
                (codes_hbm.at[kv_head], codes_ref),
            )
        )
    ]
    for copy in copies:
        copy.start()
    for copy in copies[:2]:
        copy.wait()
    scales = [
        table_ref[row, index_ref[row, kv_head, block]] for block in range(index_hbm.shape[2])
    ]
    copies[2].wait()
    return scales


def key_kernel(index_hbm, table_hbm, codes_hbm, out_ref, *scratch):
    codes_ref = scratch[2]
    for block, scale in enumerate(fetch(index_hbm, table_hbm, codes_hbm, *scratch, 0)):
        codes = codes_ref[block * BLOCK : (block + 1) * BLOCK, :].astype(jnp.float32)
        out_ref[block] = (codes * scale).T.astype(jnp.bfloat16)


def half_kernel(index_hbm, table_hbm, codes_hbm, _, *rest):
    *others, index_ref, table_ref, codes_ref, arrived = rest
    scratch = (index_ref, table_ref, codes_ref, arrived)
    count = len(others) // 2 - 1
    first_ref, second_ref = others[count : count + 2]
    copies = [
        pltpu.make_async_copy(others[n], others[count + 2 + n], arrived.at[3 + n])
        for n in range(count)
    ]
    for copy in copies:
        copy.start()
    scales = fetch(index_hbm, table_hbm, codes_hbm, *scratch, 1)
    pairs = first_ref.shape[0]
    width = codes_ref.shape[1]
    low = lower_half((BLOCK, width))
    for pair in range(pairs):
        left, right = (
            codes_ref[block * BLOCK : (block + 1) * BLOCK, :].astype(jnp.float32) * scales[block]
            for block in (pair, pair + pairs)
        )
        first = jnp.where(low, left, pltpu.roll(right, width // 2, 1))
        second = jnp.where(low, pltpu.roll(left, width // 2, 1), right)
        first_ref[pair] = first.astype(jnp.bfloat16)
        second_ref[pair] = second.astype(jnp.bfloat16)
    for copy in copies:
        copy.wait()


def lower_half(shape):
    return lax.broadcasted_iota(jnp.int32, shape, 1) < shape[1] // 2


def begin(kernel, scale_index, scale_table, codes, outputs, *after, others=()):
    _, keys_dev, width = codes.shape
    blocks = keys_dev // BLOCK // outputs
    stay = functools.partial(pltpu.with_memory_space_constraint, memory_space=pltpu.HBM)
    return pl.pallas_call(
        kernel,
        in_specs=[pl.BlockSpec(memory_space=pltpu.HBM)] * 3
        + [pl.BlockSpec(memory_space=pl.ANY)] * len(after)
        + [pl.BlockSpec(memory_space=pltpu.HBM)] * len(others),
        out_specs=[in_vmem] * (outputs + len(others)),
        out_shape=[pltpu.VMEM((blocks, BLOCK, width), jnp.bfloat16)] * outputs
        + [pltpu.VMEM(other.shape, other.dtype) for other in others],
        scratch_shapes=[
            pltpu.SMEM(scale_index.shape, scale_index.dtype),
            pltpu.SMEM(scale_table.shape, scale_table.dtype),
            pltpu.VMEM((keys_dev, width), codes.dtype),
            pltpu.SemaphoreType.DMA((3 + len(others),)),
        ],
        compiler_params=granted,
        name=kernel.__name__,
    )(
        stay(scale_index),
        stay(scale_table),
        stay(codes),
        *after,
        *[stay(other) for other in others],
    )


def turn_kernel(queries_ref, cosine_ref, sine_ref, lists_ref, own_ref, sibling_ref):
    heads_dev, rows, width = own_ref.shape
    cosine = cosine_ref[...]
    sine = sine_ref[...]
    even = lax.rem(lax.broadcasted_iota(jnp.int32, cosine.shape, 1), 2) == 0
    for head in range(heads_dev):
        plain = queries_ref[head].astype(jnp.float32)
        other = jnp.where(even, pltpu.roll(plain, width - 1, 1), pltpu.roll(plain, 1, 1))
        turned = (plain * cosine + other * sine).astype(jnp.bfloat16)
        own_ref[head] = turned[:rows]
        sibling_ref[head, :rows] = turned[rows:]
        sibling_ref[head, rows:] = jnp.broadcast_to(
            lists_ref[head : head + 1], sibling_ref[head, rows:].shape
        )


def turn_queries(queries, cosine, sine, lists):
    heads_dev, rows, width = queries.shape
    half = (heads_dev, rows // 2, width)
    more = (heads_dev, rows // 2 + ROW_TILE, width)
    return pl.pallas_call(
        turn_kernel,
        in_specs=[in_vmem] * 4,
        out_specs=[in_vmem] * 2,
        out_shape=[
            jax.ShapeDtypeStruct(half, jnp.bfloat16),
            jax.ShapeDtypeStruct(more, jnp.bfloat16),
        ],
        compiler_params=granted,
        name="turn_queries",
    )(queries, cosine, sine, lists)


def gather_parts(parts, store):
    at = 0
    for part in parts:
        store[at : at + part.shape[0]] = part[...]
        at += part.shape[0]


def score_kernel(slots_ref, queries_ref, *rest, inputs):
    parts = rest[:inputs]
    weights_ref, total_ref, store = rest[-3:]
    heads, rows, width = total_ref.shape
    picks = slots_ref.shape[1]
    slots = slots_ref[...]
    factor = math.log2(math.e) / math.sqrt(width)
    gather_parts(parts, store)
    for head in range(heads):
        turned = queries_ref[head, :rows]
        scores = []
        for i in range(0, picks, ABREAST):
            wide = jnp.concatenate([store[slots[head, i + j]] for j in range(ABREAST)], axis=1)
            wide = jnp.dot(turned, wide, preferred_element_type=jnp.float32)
            scores += [wide[:, j * BLOCK : (j + 1) * BLOCK] for j in range(ABREAST)]
        top = scores[0]
        for i in range(1, picks):
            top = jnp.maximum(top, scores[i])
        top = jnp.max(top, axis=1, keepdims=True)
        total = jnp.zeros((rows, BLOCK), jnp.float32)
        for i in range(picks):
            weight = jnp.exp2((scores[i] - top) * factor)
            total = total + weight
            weights_ref[head, :, i * BLOCK : (i + 1) * BLOCK] = weight.astype(jnp.bfloat16)
        total = jnp.sum(total, axis=1, keepdims=True)
        total_ref[head] = jnp.broadcast_to(1.0 / total, (rows, width))


def block_weights(slots, queries, parts, rows, *extra):
    width = queries.shape[2]
    heads, picks = slots.shape
    blocks = sum(part.shape[0] for part in parts)
    return pl.pallas_call(
        functools.partial(score_kernel, inputs=len(parts)),
        in_specs=[in_vmem] * (2 + len(parts) + len(extra)),
        out_specs=[in_vmem, in_vmem],
        out_shape=[
            jax.ShapeDtypeStruct((heads, rows, picks * BLOCK), jnp.bfloat16),
            jax.ShapeDtypeStruct((heads, rows, width), jnp.float32),
        ],
        scratch_shapes=[pltpu.VMEM((blocks, width, BLOCK), jnp.bfloat16)],
        compiler_params=granted,
        name="block_weights",
    )(slots, queries, *parts, *extra)


def value_kernel(slots_ref, *rest, inputs, flip, first, last):
    weights = rest[:2]
    totals = rest[2:4]
    parts = rest[4 : 4 + inputs]
    pieces = rest[4 + inputs : -1]
    store = rest[-1]
    heads_dev, _, width = totals[0].shape
    heads, picks = slots_ref.shape
    rows = pieces[0].shape[0]
    slots = slots_ref[...]
    half = store.shape[0] // 2
    at = 0
    for part in parts:
        for pair in range(part.shape[0]):
            block = part[pair]
            store[at] = block
            turned = pltpu.roll(block.astype(jnp.float32), width // 2, 1)
            store[half + at] = turned.astype(jnp.bfloat16)
            at += 1
    low = lower_half((last - first, width))
    for pair in range(heads // 2):
        both = []
        for head in (2 * pair, 2 * pair + 1):
            picked = jnp.concatenate([store[slots[head, i]] for i in range(picks)], axis=0)
            owner, place = divmod(head, heads_dev)
            weight = weights[owner][place, first:last]
            out = jnp.dot(weight, picked, preferred_element_type=jnp.float32)
            both.append(out * totals[owner][place, first:last])
        out = jnp.where(low, both[flip], both[1 - flip])
        for n, piece in enumerate(pieces):
            piece[:, pair * width : (pair + 1) * width] = out[n * rows : (n + 1) * rows].astype(
                jnp.bfloat16
            )


def block_outputs(slots, weights, totals, parts, pieces, flip, first, last):
    heads = slots.shape[0]
    _, rows, width = totals[0].shape
    pairs = sum(part.shape[0] for part in parts)
    rows //= pieces
    pieces = last - first
    piece = jax.ShapeDtypeStruct((rows, heads // 2 * width), jnp.bfloat16)
    return pl.pallas_call(
        functools.partial(
            value_kernel,
            inputs=len(parts),
            flip=flip,
            first=first * rows,
            last=last * rows,
        ),
        in_specs=[in_vmem] * (5 + len(parts)),
        out_specs=[in_vmem] * pieces,
        out_shape=[piece] * pieces,
        scratch_shapes=[pltpu.VMEM((2 * pairs, BLOCK, width), jnp.bfloat16)],
        compiler_params=granted,
        name="block_outputs",
    )(slots, *weights, *totals, *parts)


def join_kernel(*refs, share, width):
    *pieces, out_ref = refs
    place = lax.axis_index("head")
    chips = len(pieces) // 2
    rows = out_ref.shape[0]
    pairs = pieces[0].shape[1] // width // share
    low = lower_half((rows, width))
    for n in range(chips):
        for part in range(share):
            column = jnp.bitwise_xor(place, across(n, share) ^ part) * (2 * pairs * width)
            for pair in range(pairs):
                at = (part * pairs + pair) * width
                first, second = (
                    piece[:, at : at + width].astype(jnp.float32)
                    for piece in (pieces[n], pieces[chips + n])
                )
                even = jnp.where(low, first, second)
                odd = pltpu.roll(jnp.where(low, second, first), width // 2, 1)
                for m, out in enumerate((even, odd)):
                    to = pl.multiple_of(column + (2 * pair + m) * width, width)
                    out_ref[:, pl.ds(to, width)] = out.astype(jnp.bfloat16)


def join_pieces(pieces, share, width):
    rows, across = pieces[0].shape
    return pl.pallas_call(
        functools.partial(join_kernel, share=share, width=width),
        in_specs=[in_vmem] * len(pieces),
        out_specs=in_vmem,
        out_shape=jax.ShapeDtypeStruct((rows, across * len(pieces)), jnp.bfloat16),
        compiler_params=granted,
        name="join_pieces",
    )(*pieces)


def on_device(queries, positions, key_codes, value_codes, scale_index, scale_table, block_lists):
    cycle_size = lax.axis_size("ctx")
    cycle_place = lax.axis_index("ctx")
    head_count = lax.axis_size("head")
    head_place = lax.axis_index("head")
    reach_hops = min(3, (cycle_size - 1) // 2)
    pairs = paired(cycle_size, reach_hops)
    rows_dev, heads_dev, head_width = queries.shape
    key_blocks = key_codes.shape[1] // BLOCK
    share = GROUP // heads_dev
    assert share == 2 and rows_dev == BLOCK
    core = head_place % share
    group = head_place // share
    groups = head_count // share

    (keys,) = begin(key_kernel, scale_index, scale_table, key_codes, 1)
    *values, queries, positions, block_lists = begin(
        half_kernel,
        scale_index,
        scale_table,
        value_codes,
        2,
        keys,
        others=(queries, positions, block_lists),
    )
    far_keys = keys
    key_parts = []
    for _ in range(reach_hops):
        far_keys = sent(far_keys, share, pairs)
        key_parts.append(far_keys)
    own_lists = lax.dynamic_index_in_dim(block_lists, cycle_place, 1, keepdims=False)
    def ordered(x):
        cut = x.reshape((groups, share, rows_dev // head_count) + x.shape[1:])
        taken = [
            lax.dynamic_slice(
                cut,
                (jnp.bitwise_xor(group, n), jnp.bitwise_xor(core, part ^ n % share))
                + (0,) * x.ndim,
                (1, 1) + cut.shape[2:],
            )
            for part in range(share)
            for n in range(groups)
        ]
        return jnp.concatenate(taken, axis=0).reshape(x.shape)

    frequency = ROPE_BASE ** (
        -2.0 * (jnp.arange(head_width) // 2).astype(jnp.float32) / head_width
    )
    angles = ordered(positions).astype(jnp.float32)[:, None] * frequency[None, :]
    signs = jnp.where(jnp.arange(head_width) % 2 == 0, -1.0, 1.0)
    cosine = jnp.cos(angles)
    sine = jnp.sin(angles) * signs[None, :]

    picks = own_lists.shape[1]
    carried = jnp.pad(own_lists.astype(jnp.bfloat16), ((0, 0), (0, head_width - picks)))
    own, sibling = turn_queries(
        jnp.transpose(ordered(queries), (1, 0, 2)), cosine, sine, carried
    )
    sibling, key_parts[0] = lax.optimization_barrier((sibling, key_parts[0]))
    key_parts = [keys] + [part for far in key_parts for part in (far, swapped(far, 1))]
    sibling = swapped(sibling, 1)
    sibling_lists = sibling[:, rows_dev // share, :picks].astype(jnp.int32)
    lists = jnp.concatenate([own_lists, sibling_lists], axis=0)
    offset = jnp.mod(lists // key_blocks - cycle_place, cycle_size)
    above = offset <= reach_hops
    hops = jnp.where(above, offset, cycle_size - offset)
    from_above = (cycle_place % 2 if pairs else 1) == core
    place = 2 * hops - jnp.where(above == from_above, 1, 0)
    slots = lists % key_blocks + key_blocks * jnp.where(offset == 0, 0, place)

    steps = []
    far_values = values
    for _ in range(reach_hops):
        far_values = [sent(half, share, pairs) for half in far_values]
        steps.append(far_values)
    rows = rows_dev // share
    own_weights, own_total = block_weights(slots[:heads_dev], own, key_parts, rows)
    sibling_weights, sibling_total = block_weights(slots[heads_dev:], sibling, key_parts, rows)
    weights = (own_weights, sibling_weights)
    totals = (own_total, sibling_total)

    inner = slots % key_blocks
    places = slots // key_blocks * (key_blocks // 2) + inner % (key_blocks // 2)
    parity = jnp.arange(slots.shape[0])[:, None] % 2
    turned_places = (2 * reach_hops + 1) * (key_blocks // 2)
    ready = own_weights
    moved = []
    for half in range(2):
        *far_values, ready = lax.optimization_barrier((*[step[half] for step in steps], ready))
        value_parts = [values[half]]
        for far in far_values:
            value_parts += [far, swapped(far, 1)]
        side = jnp.bitwise_xor(inner // (key_blocks // 2), jnp.bitwise_xor(parity, half))
        outputs = functools.partial(
            block_outputs,
            places + turned_places * side,
            weights,
            totals,
            value_parts,
            groups,
            half,
        )
        if half == 0 or groups == 1:
            pieces = outputs(0, groups)
        else:
            pieces = [None, *outputs(1, groups)]
        sent_pieces = [swapped(pieces[n], across(n, share)) for n in range(1, groups)]
        if pieces[0] is None:
            pieces[0] = outputs(0, 1)[0]
        moved += [pieces[0], *sent_pieces]
        ready = pieces[0]
    return join_pieces(moved, share, head_width)


def solution(mesh):
    placed = (
        P(("groups", "ctx"), "head", None),
        P(("groups", "ctx")),
        P("groups", "ctx", None),
        P("groups", "ctx", None),
        P("groups", None, "ctx"),
        P(),
        P(("groups", "head"), None, None),
    )
    return jax.shard_map(
        on_device,
        mesh=mesh,
        in_specs=placed,
        out_specs=P(("groups", "ctx", "head"), None),
        check_vma=False,
    )
```

```python
import functools
import math

import jax
import jax.numpy as jnp
from jax import lax
from jax.experimental import pallas as pl
from jax.experimental.pallas import tpu as pltpu
from jax.sharding import PartitionSpec as P

GROUP = 16
BLOCK = 128
ROW_TILE = 16
ABREAST = 2
ROPE_BASE = 500000.0
VMEM_GRANT = 16 * 2**20

in_vmem = pl.BlockSpec(memory_space=pltpu.VMEM)
granted = pltpu.CompilerParams(vmem_limit_bytes=VMEM_GRANT)


def paired(cycle, hops):
    return hops == 1 and cycle % 2 == 0


def source(place, part, cycle, pairs):
    if pairs:
        return place + 1 if place % 2 == part else place - 1
    return place - 1 if part == 0 else place + 1


def sent(x, share, pairs):
    cycle = lax.axis_size("ctx")
    heads = lax.axis_size("head")
    moves = [
        (source(place, head % share, cycle, pairs) % cycle * heads + head, place * heads + head)
        for place in range(cycle)
        for head in range(heads)
    ]
    return lax.ppermute(x, ("ctx", "head"), moves)


def across(n, share):
    return n * share ^ n % share


def swapped(x, mask):
    return lax.ppermute(x, "head", [(i, i ^ mask) for i in range(lax.axis_size("head"))])


def fetch(index_hbm, table_hbm, codes_hbm, index_ref, table_ref, codes_ref, arrived, row):
    groups = index_hbm.shape[1]
    kv_head = lax.axis_index("head") * groups // lax.axis_size("head")
    copies = [
        pltpu.make_async_copy(source, target, arrived.at[n])
        for n, (source, target) in enumerate(
            (
                (index_hbm, index_ref),
                (table_hbm, table_ref),
                (codes_hbm.at[kv_head], codes_ref),
            )
        )
    ]
    for copy in copies:
        copy.start()
    for copy in copies[:2]:
        copy.wait()
    scales = [
        table_ref[row, index_ref[row, kv_head, block]] for block in range(index_hbm.shape[2])
    ]
    copies[2].wait()
    return scales


def key_kernel(index_hbm, table_hbm, codes_hbm, out_ref, *scratch):
    codes_ref = scratch[2]
    for block, scale in enumerate(fetch(index_hbm, table_hbm, codes_hbm, *scratch, 0)):
        codes = codes_ref[block * BLOCK : (block + 1) * BLOCK, :].astype(jnp.float32)
        out_ref[block] = (codes * scale).astype(jnp.bfloat16)


def half_kernel(index_hbm, table_hbm, codes_hbm, _, *rest):
    *others, index_ref, table_ref, codes_ref, arrived = rest
    scratch = (index_ref, table_ref, codes_ref, arrived)
    count = len(others) // 2 - 1
    first_ref, second_ref = others[count : count + 2]
    copies = [
        pltpu.make_async_copy(others[n], others[count + 2 + n], arrived.at[3 + n])
        for n in range(count)
    ]
    for copy in copies:
        copy.start()
    scales = fetch(index_hbm, table_hbm, codes_hbm, *scratch, 1)
    pairs = first_ref.shape[0]
    width = codes_ref.shape[1]
    low = lower_half((BLOCK, width))
    for pair in range(pairs):
        left, right = (
            codes_ref[block * BLOCK : (block + 1) * BLOCK, :].astype(jnp.float32) * scales[block]
            for block in (pair, pair + pairs)
        )
        first = jnp.where(low, left, pltpu.roll(right, width // 2, 1))
        second = jnp.where(low, pltpu.roll(left, width // 2, 1), right)
        first_ref[pair] = first.astype(jnp.bfloat16)
        second_ref[pair] = second.astype(jnp.bfloat16)
    for copy in copies:
        copy.wait()


def lower_half(shape):
    return lax.broadcasted_iota(jnp.int32, shape, 1) < shape[1] // 2


def begin(kernel, scale_index, scale_table, codes, outputs, *after, others=()):
    _, keys_dev, width = codes.shape
    blocks = keys_dev // BLOCK // outputs
    stay = functools.partial(pltpu.with_memory_space_constraint, memory_space=pltpu.HBM)
    return pl.pallas_call(
        kernel,
        in_specs=[pl.BlockSpec(memory_space=pltpu.HBM)] * 3
        + [pl.BlockSpec(memory_space=pl.ANY)] * len(after)
        + [pl.BlockSpec(memory_space=pltpu.HBM)] * len(others),
        out_specs=[in_vmem] * (outputs + len(others)),
        out_shape=[pltpu.VMEM((blocks, BLOCK, width), jnp.bfloat16)] * outputs
        + [pltpu.VMEM(other.shape, other.dtype) for other in others],
        scratch_shapes=[
            pltpu.SMEM(scale_index.shape, scale_index.dtype),
            pltpu.SMEM(scale_table.shape, scale_table.dtype),
            pltpu.VMEM((keys_dev, width), codes.dtype),
            pltpu.SemaphoreType.DMA((3 + len(others),)),
        ],
        compiler_params=granted,
        name=kernel.__name__,
    )(
        stay(scale_index),
        stay(scale_table),
        stay(codes),
        *after,
        *[stay(other) for other in others],
    )


def turn_kernel(queries_ref, cosine_ref, sine_ref, lists_ref, own_ref, sibling_ref):
    heads_dev, rows, width = own_ref.shape
    cosine = cosine_ref[...]
    sine = sine_ref[...]
    even = lax.rem(lax.broadcasted_iota(jnp.int32, cosine.shape, 1), 2) == 0
    for head in range(heads_dev):
        plain = queries_ref[head].astype(jnp.float32)
        other = jnp.where(even, pltpu.roll(plain, width - 1, 1), pltpu.roll(plain, 1, 1))
        turned = (plain * cosine + other * sine).astype(jnp.bfloat16)
        own_ref[head] = turned[:rows]
        sibling_ref[head, :rows] = turned[rows:]
        sibling_ref[head, rows:] = jnp.broadcast_to(
            lists_ref[head : head + 1], sibling_ref[head, rows:].shape
        )


def turn_queries(queries, cosine, sine, lists):
    heads_dev, rows, width = queries.shape
    half = (heads_dev, rows // 2, width)
    more = (heads_dev, rows // 2 + ROW_TILE, width)
    return pl.pallas_call(
        turn_kernel,
        in_specs=[in_vmem] * 4,
        out_specs=[in_vmem] * 2,
        out_shape=[
            jax.ShapeDtypeStruct(half, jnp.bfloat16),
            jax.ShapeDtypeStruct(more, jnp.bfloat16),
        ],
        compiler_params=granted,
        name="turn_queries",
    )(queries, cosine, sine, lists)


def score_kernel(slots_ref, queries_ref, *rest, inputs):
    parts = rest[:inputs]
    weights_ref, total_ref, store = rest[inputs : inputs + 3]
    heads, rows, width = total_ref.shape
    picks = slots_ref.shape[1]
    slots = slots_ref[...]
    factor = math.log2(math.e) / math.sqrt(width)
    at = 0
    for part in parts:
        for block in range(part.shape[0]):
            store[at] = part[block].astype(jnp.float32).T.astype(jnp.bfloat16)
            at += 1
    for head in range(heads):
        turned = queries_ref[head, :rows]
        scores = []
        for i in range(0, picks, ABREAST):
            wide = jnp.concatenate([store[slots[head, i + j]] for j in range(ABREAST)], axis=1)
            wide = jnp.dot(turned, wide, preferred_element_type=jnp.float32)
            scores += [wide[:, j * BLOCK : (j + 1) * BLOCK] for j in range(ABREAST)]
        top = scores[0]
        for i in range(1, picks):
            top = jnp.maximum(top, scores[i])
        top = jnp.max(top, axis=1, keepdims=True)
        total = jnp.zeros((rows, BLOCK), jnp.float32)
        for i in range(picks):
            weight = jnp.exp2((scores[i] - top) * factor)
            total = total + weight
            weights_ref[head, :, i * BLOCK : (i + 1) * BLOCK] = weight.astype(jnp.bfloat16)
        total = jnp.sum(total, axis=1, keepdims=True)
        total_ref[head] = jnp.broadcast_to(1.0 / total, (rows, width))


def held_kernel(slots_ref, queries_ref, store, weights_ref, total_ref):
    score_kernel(slots_ref, queries_ref, weights_ref, total_ref, store, inputs=0)


def block_weights(slots, queries, parts, rows):
    width = queries.shape[2]
    heads, picks = slots.shape
    blocks = sum(part.shape[0] for part in parts)
    outputs = [
        jax.ShapeDtypeStruct((heads, rows, picks * BLOCK), jnp.bfloat16),
        jax.ShapeDtypeStruct((heads, rows, width), jnp.float32),
    ]
    if len(parts) > 1:
        outputs.append(jax.ShapeDtypeStruct((blocks, width, BLOCK), jnp.bfloat16))
    return pl.pallas_call(
        functools.partial(score_kernel, inputs=len(parts)) if len(parts) > 1 else held_kernel,
        in_specs=[in_vmem] * (2 + len(parts)),
        out_specs=[in_vmem] * len(outputs),
        out_shape=outputs,
        compiler_params=granted,
        name="block_weights",
    )(slots, queries, *parts)


def value_kernel(slots_ref, *rest, inputs, flip, first, last):
    weights = rest[:2]
    totals = rest[2:4]
    parts = rest[4 : 4 + inputs]
    pieces = rest[4 + inputs : -1]
    store = rest[-1]
    heads_dev, _, width = totals[0].shape
    heads, picks = slots_ref.shape
    rows = pieces[0].shape[0]
    slots = slots_ref[...]
    half = store.shape[0] // 2
    at = 0
    for part in parts:
        for pair in range(part.shape[0]):
            block = part[pair]
            store[at] = block
            turned = pltpu.roll(block.astype(jnp.float32), width // 2, 1)
            store[half + at] = turned.astype(jnp.bfloat16)
            at += 1
    low = lower_half((last - first, width))
    for pair in range(heads // 2):
        both = []
        for head in (2 * pair, 2 * pair + 1):
            picked = jnp.concatenate([store[slots[head, i]] for i in range(picks)], axis=0)
            owner, place = divmod(head, heads_dev)
            weight = weights[owner][place, first:last]
            out = jnp.dot(weight, picked, preferred_element_type=jnp.float32)
            both.append(out * totals[owner][place, first:last])
        out = jnp.where(low, both[flip], both[1 - flip])
        for n, piece in enumerate(pieces):
            piece[:, pair * width : (pair + 1) * width] = out[n * rows : (n + 1) * rows].astype(
                jnp.bfloat16
            )


def block_outputs(slots, weights, totals, parts, pieces, flip, first, last):
    heads = slots.shape[0]
    _, rows, width = totals[0].shape
    pairs = sum(part.shape[0] for part in parts)
    rows //= pieces
    pieces = last - first
    piece = jax.ShapeDtypeStruct((rows, heads // 2 * width), jnp.bfloat16)
    return pl.pallas_call(
        functools.partial(
            value_kernel,
            inputs=len(parts),
            flip=flip,
            first=first * rows,
            last=last * rows,
        ),
        in_specs=[in_vmem] * (5 + len(parts)),
        out_specs=[in_vmem] * pieces,
        out_shape=[piece] * pieces,
        scratch_shapes=[pltpu.VMEM((2 * pairs, BLOCK, width), jnp.bfloat16)],
        compiler_params=granted,
        name="block_outputs",
    )(slots, *weights, *totals, *parts)


def join_kernel(*refs, share, width):
    *pieces, out_ref = refs
    place = lax.axis_index("head")
    chips = len(pieces) // 2
    rows = out_ref.shape[0]
    pairs = pieces[0].shape[1] // width // share
    low = lower_half((rows, width))
    for n in range(chips):
        for part in range(share):
            column = jnp.bitwise_xor(place, across(n, share) ^ part) * (2 * pairs * width)
            for pair in range(pairs):
                at = (part * pairs + pair) * width
                first, second = (
                    piece[:, at : at + width].astype(jnp.float32)
                    for piece in (pieces[n], pieces[chips + n])
                )
                even = jnp.where(low, first, second)
                odd = pltpu.roll(jnp.where(low, second, first), width // 2, 1)
                for m, out in enumerate((even, odd)):
                    to = pl.multiple_of(column + (2 * pair + m) * width, width)
                    out_ref[:, pl.ds(to, width)] = out.astype(jnp.bfloat16)


def join_pieces(pieces, share, width):
    rows, across = pieces[0].shape
    return pl.pallas_call(
        functools.partial(join_kernel, share=share, width=width),
        in_specs=[in_vmem] * len(pieces),
        out_specs=in_vmem,
        out_shape=jax.ShapeDtypeStruct((rows, across * len(pieces)), jnp.bfloat16),
        compiler_params=granted,
        name="join_pieces",
    )(*pieces)


def on_device(queries, positions, key_codes, value_codes, scale_index, scale_table, block_lists):
    cycle_size = lax.axis_size("ctx")
    cycle_place = lax.axis_index("ctx")
    head_count = lax.axis_size("head")
    head_place = lax.axis_index("head")
    reach_hops = min(3, (cycle_size - 1) // 2)
    pairs = paired(cycle_size, reach_hops)
    rows_dev, heads_dev, head_width = queries.shape
    key_blocks = key_codes.shape[1] // BLOCK
    share = GROUP // heads_dev
    assert share == 2 and rows_dev == BLOCK
    core = head_place % share
    group = head_place // share
    groups = head_count // share

    (keys,) = begin(key_kernel, scale_index, scale_table, key_codes, 1)
    *values, queries, positions, block_lists = begin(
        half_kernel,
        scale_index,
        scale_table,
        value_codes,
        2,
        keys,
        others=(queries, positions, block_lists),
    )
    far_keys = keys
    key_parts = []
    for _ in range(reach_hops):
        far_keys = sent(far_keys, share, pairs)
        key_parts.append(far_keys)
    own_lists = lax.dynamic_index_in_dim(block_lists, cycle_place, 1, keepdims=False)
    def ordered(x):
        cut = x.reshape((groups, share, rows_dev // head_count) + x.shape[1:])
        taken = [
            lax.dynamic_slice(
                cut,
                (jnp.bitwise_xor(group, n), jnp.bitwise_xor(core, part ^ n % share))
                + (0,) * x.ndim,
                (1, 1) + cut.shape[2:],
            )
            for part in range(share)
            for n in range(groups)
        ]
        return jnp.concatenate(taken, axis=0).reshape(x.shape)

    frequency = ROPE_BASE ** (
        -2.0 * (jnp.arange(head_width) // 2).astype(jnp.float32) / head_width
    )
    angles = ordered(positions).astype(jnp.float32)[:, None] * frequency[None, :]
    signs = jnp.where(jnp.arange(head_width) % 2 == 0, -1.0, 1.0)
    cosine = jnp.cos(angles)
    sine = jnp.sin(angles) * signs[None, :]

    picks = own_lists.shape[1]
    carried = jnp.pad(own_lists.astype(jnp.bfloat16), ((0, 0), (0, head_width - picks)))
    own, sibling = turn_queries(
        jnp.transpose(ordered(queries), (1, 0, 2)), cosine, sine, carried
    )
    sibling, key_parts[0] = lax.optimization_barrier((sibling, key_parts[0]))
    key_parts = [keys] + [part for far in key_parts for part in (far, swapped(far, 1))]
    sibling = swapped(sibling, 1)
    sibling_lists = sibling[:, rows_dev // share, :picks].astype(jnp.int32)
    lists = jnp.concatenate([own_lists, sibling_lists], axis=0)
    offset = jnp.mod(lists // key_blocks - cycle_place, cycle_size)
    above = offset <= reach_hops
    hops = jnp.where(above, offset, cycle_size - offset)
    from_above = (cycle_place % 2 if pairs else 1) == core
    place = 2 * hops - jnp.where(above == from_above, 1, 0)
    slots = lists % key_blocks + key_blocks * jnp.where(offset == 0, 0, place)

    steps = []
    far_values = values
    for _ in range(reach_hops):
        far_values = [sent(half, share, pairs) for half in far_values]
        steps.append(far_values)
    rows = rows_dev // share
    own_weights, own_total, held = block_weights(slots[:heads_dev], own, key_parts, rows)
    sibling_weights, sibling_total = block_weights(slots[heads_dev:], sibling, [held], rows)
    weights = (own_weights, sibling_weights)
    totals = (own_total, sibling_total)

    inner = slots % key_blocks
    places = slots // key_blocks * (key_blocks // 2) + inner % (key_blocks // 2)
    parity = jnp.arange(slots.shape[0])[:, None] % 2
    turned_places = (2 * reach_hops + 1) * (key_blocks // 2)
    ready = own_weights
    moved = []
    for half in range(2):
        *far_values, ready = lax.optimization_barrier((*[step[half] for step in steps], ready))
        value_parts = [values[half]]
        for far in far_values:
            value_parts += [far, swapped(far, 1)]
        side = jnp.bitwise_xor(inner // (key_blocks // 2), jnp.bitwise_xor(parity, half))
        outputs = functools.partial(
            block_outputs,
            places + turned_places * side,
            weights,
            totals,
            value_parts,
            groups,
            half,
        )
        if half == 0 or groups == 1:
            pieces = outputs(0, groups)
        else:
            pieces = [None, *outputs(1, groups)]
        sent_pieces = [swapped(pieces[n], across(n, share)) for n in range(1, groups)]
        if pieces[0] is None:
            pieces[0] = outputs(0, 1)[0]
        moved += [pieces[0], *sent_pieces]
        ready = pieces[0]
    return join_pieces(moved, share, head_width)


def solution(mesh):
    placed = (
        P(("groups", "ctx"), "head", None),
        P(("groups", "ctx")),
        P("groups", "ctx", None),
        P("groups", "ctx", None),
        P("groups", None, "ctx"),
        P(),
        P(("groups", "head"), None, None),
    )
    return jax.shard_map(
        on_device,
        mesh=mesh,
        in_specs=placed,
        out_specs=P(("groups", "ctx", "head"), None),
        check_vma=False,
    )
```

```python
import functools
import math

import jax
import jax.numpy as jnp
from jax import lax
from jax.experimental import pallas as pl
from jax.experimental.pallas import tpu as pltpu
from jax.sharding import PartitionSpec as P

GROUP = 16
BLOCK = 128
ROW_TILE = 16
ABREAST = 2
ROPE_BASE = 500000.0
VMEM_GRANT = 16 * 2**20

in_vmem = pl.BlockSpec(memory_space=pltpu.VMEM)
granted = pltpu.CompilerParams(vmem_limit_bytes=VMEM_GRANT)


def paired(cycle, hops):
    return hops == 1 and cycle % 2 == 0


def source(place, part, cycle, pairs):
    if not pairs:
        return (place + (1 if part else -1)) % cycle, part
    outer = place % 4 in (0, 3)
    odd = part == outer
    other = (place + (1 if place % 2 == odd else -1)) % cycle
    return other, int((other % 4 in (0, 3)) == odd)


def sent(x, share, pairs):
    cycle = lax.axis_size("ctx")
    heads = lax.axis_size("head")
    moves = []
    for place in range(cycle):
        for head in range(heads):
            part = head % share
            other, core = source(place, part, cycle, pairs)
            moves.append((other * heads + head - part + core, place * heads + head))
    return lax.ppermute(x, ("ctx", "head"), moves)


def across(n, share):
    return n * share ^ n % share


def swapped(x, mask):
    return lax.ppermute(x, "head", [(i, i ^ mask) for i in range(lax.axis_size("head"))])


def fetch(index_hbm, table_hbm, codes_hbm, index_ref, table_ref, codes_ref, arrived, row):
    groups = index_hbm.shape[1]
    kv_head = lax.axis_index("head") * groups // lax.axis_size("head")
    copies = [
        pltpu.make_async_copy(source, target, arrived.at[n])
        for n, (source, target) in enumerate(
            (
                (index_hbm, index_ref),
                (table_hbm, table_ref),
                (codes_hbm.at[kv_head], codes_ref),
            )
        )
    ]
    for copy in copies:
        copy.start()
    for copy in copies[:2]:
        copy.wait()
    scales = [
        table_ref[row, index_ref[row, kv_head, block]] for block in range(index_hbm.shape[2])
    ]
    copies[2].wait()
    return scales


def key_kernel(index_hbm, table_hbm, codes_hbm, out_ref, *scratch):
    codes_ref = scratch[2]
    for block, scale in enumerate(fetch(index_hbm, table_hbm, codes_hbm, *scratch, 0)):
        codes = codes_ref[block * BLOCK : (block + 1) * BLOCK, :].astype(jnp.float32)
        out_ref[block] = (codes * scale).astype(jnp.bfloat16)


def half_kernel(index_hbm, table_hbm, codes_hbm, _, *rest):
    *others, index_ref, table_ref, codes_ref, arrived = rest
    scratch = (index_ref, table_ref, codes_ref, arrived)
    count = len(others) // 2 - 1
    first_ref, second_ref = others[count : count + 2]
    copies = [
        pltpu.make_async_copy(others[n], others[count + 2 + n], arrived.at[3 + n])
        for n in range(count)
    ]
    for copy in copies:
        copy.start()
    scales = fetch(index_hbm, table_hbm, codes_hbm, *scratch, 1)
    pairs = first_ref.shape[0]
    width = codes_ref.shape[1]
    low = lower_half((BLOCK, width))
    for pair in range(pairs):
        left, right = (
            codes_ref[block * BLOCK : (block + 1) * BLOCK, :].astype(jnp.float32) * scales[block]
            for block in (pair, pair + pairs)
        )
        first = jnp.where(low, left, pltpu.roll(right, width // 2, 1))
        second = jnp.where(low, pltpu.roll(left, width // 2, 1), right)
        first_ref[pair] = first.astype(jnp.bfloat16)
        second_ref[pair] = second.astype(jnp.bfloat16)
    for copy in copies:
        copy.wait()


def lower_half(shape):
    return lax.broadcasted_iota(jnp.int32, shape, 1) < shape[1] // 2


def begin(kernel, scale_index, scale_table, codes, outputs, *after, others=()):
    _, keys_dev, width = codes.shape
    blocks = keys_dev // BLOCK // outputs
    stay = functools.partial(pltpu.with_memory_space_constraint, memory_space=pltpu.HBM)
    return pl.pallas_call(
        kernel,
        in_specs=[pl.BlockSpec(memory_space=pltpu.HBM)] * 3
        + [pl.BlockSpec(memory_space=pl.ANY)] * len(after)
        + [pl.BlockSpec(memory_space=pltpu.HBM)] * len(others),
        out_specs=[in_vmem] * (outputs + len(others)),
        out_shape=[pltpu.VMEM((blocks, BLOCK, width), jnp.bfloat16)] * outputs
        + [pltpu.VMEM(other.shape, other.dtype) for other in others],
        scratch_shapes=[
            pltpu.SMEM(scale_index.shape, scale_index.dtype),
            pltpu.SMEM(scale_table.shape, scale_table.dtype),
            pltpu.VMEM((keys_dev, width), codes.dtype),
            pltpu.SemaphoreType.DMA((3 + len(others),)),
        ],
        compiler_params=granted,
        name=kernel.__name__,
    )(
        stay(scale_index),
        stay(scale_table),
        stay(codes),
        *after,
        *[stay(other) for other in others],
    )


def turn_kernel(queries_ref, cosine_ref, sine_ref, lists_ref, own_ref, sibling_ref):
    heads_dev, rows, width = own_ref.shape
    cosine = cosine_ref[...]
    sine = sine_ref[...]
    even = lax.rem(lax.broadcasted_iota(jnp.int32, cosine.shape, 1), 2) == 0
    for head in range(heads_dev):
        plain = queries_ref[head].astype(jnp.float32)
        other = jnp.where(even, pltpu.roll(plain, width - 1, 1), pltpu.roll(plain, 1, 1))
        turned = (plain * cosine + other * sine).astype(jnp.bfloat16)
        own_ref[head] = turned[:rows]
        sibling_ref[head, :rows] = turned[rows:]
        sibling_ref[head, rows:] = jnp.broadcast_to(
            lists_ref[head : head + 1], sibling_ref[head, rows:].shape
        )


def turn_queries(queries, cosine, sine, lists):
    heads_dev, rows, width = queries.shape
    half = (heads_dev, rows // 2, width)
    more = (heads_dev, rows // 2 + ROW_TILE, width)
    return pl.pallas_call(
        turn_kernel,
        in_specs=[in_vmem] * 4,
        out_specs=[in_vmem] * 2,
        out_shape=[
            jax.ShapeDtypeStruct(half, jnp.bfloat16),
            jax.ShapeDtypeStruct(more, jnp.bfloat16),
        ],
        compiler_params=granted,
        name="turn_queries",
    )(queries, cosine, sine, lists)


def score_kernel(slots_ref, queries_ref, *rest, inputs):
    parts = rest[:inputs]
    weights_ref, total_ref, store = rest[inputs : inputs + 3]
    heads, rows, width = total_ref.shape
    picks = slots_ref.shape[1]
    slots = slots_ref[...]
    factor = math.log2(math.e) / math.sqrt(width)
    at = 0
    for part in parts:
        for block in range(part.shape[0]):
            store[at] = part[block].astype(jnp.float32).T.astype(jnp.bfloat16)
            at += 1
    for head in range(heads):
        turned = queries_ref[head, :rows]
        scores = []
        for i in range(0, picks, ABREAST):
            wide = jnp.concatenate([store[slots[head, i + j]] for j in range(ABREAST)], axis=1)
            wide = jnp.dot(turned, wide, preferred_element_type=jnp.float32)
            scores += [wide[:, j * BLOCK : (j + 1) * BLOCK] for j in range(ABREAST)]
        top = scores[0]
        for i in range(1, picks):
            top = jnp.maximum(top, scores[i])
        top = jnp.max(top, axis=1, keepdims=True)
        total = jnp.zeros((rows, BLOCK), jnp.float32)
        for i in range(picks):
            weight = jnp.exp2((scores[i] - top) * factor)
            total = total + weight
            weights_ref[head, :, i * BLOCK : (i + 1) * BLOCK] = weight.astype(jnp.bfloat16)
        total = jnp.sum(total, axis=1, keepdims=True)
        total_ref[head] = jnp.broadcast_to(1.0 / total, (rows, width))


def held_kernel(slots_ref, queries_ref, store, weights_ref, total_ref):
    score_kernel(slots_ref, queries_ref, weights_ref, total_ref, store, inputs=0)


def block_weights(slots, queries, parts, rows):
    width = queries.shape[2]
    heads, picks = slots.shape
    blocks = sum(part.shape[0] for part in parts)
    outputs = [
        jax.ShapeDtypeStruct((heads, rows, picks * BLOCK), jnp.bfloat16),
        jax.ShapeDtypeStruct((heads, rows, width), jnp.float32),
    ]
    if len(parts) > 1:
        outputs.append(jax.ShapeDtypeStruct((blocks, width, BLOCK), jnp.bfloat16))
    return pl.pallas_call(
        functools.partial(score_kernel, inputs=len(parts)) if len(parts) > 1 else held_kernel,
        in_specs=[in_vmem] * (2 + len(parts)),
        out_specs=[in_vmem] * len(outputs),
        out_shape=outputs,
        compiler_params=granted,
        name="block_weights",
    )(slots, queries, *parts)


def value_kernel(slots_ref, *rest, inputs, flip, first, last):
    weights = rest[:2]
    totals = rest[2:4]
    parts = rest[4 : 4 + inputs]
    pieces = rest[4 + inputs : -1]
    store = rest[-1]
    heads_dev, _, width = totals[0].shape
    heads, picks = slots_ref.shape
    rows = pieces[0].shape[0]
    slots = slots_ref[...]
    half = store.shape[0] // 2
    at = 0
    for part in parts:
        for pair in range(part.shape[0]):
            block = part[pair]
            store[at] = block
            turned = pltpu.roll(block.astype(jnp.float32), width // 2, 1)
            store[half + at] = turned.astype(jnp.bfloat16)
            at += 1
    low = lower_half((last - first, width))
    for pair in range(heads // 2):
        both = []
        for head in (2 * pair, 2 * pair + 1):
            picked = jnp.concatenate([store[slots[head, i]] for i in range(picks)], axis=0)
            owner, place = divmod(head, heads_dev)
            weight = weights[owner][place, first:last]
            out = jnp.dot(weight, picked, preferred_element_type=jnp.float32)
            both.append(out * totals[owner][place, first:last])
        out = jnp.where(low, both[flip], both[1 - flip])
        for n, piece in enumerate(pieces):
            piece[:, pair * width : (pair + 1) * width] = out[n * rows : (n + 1) * rows].astype(
                jnp.bfloat16
            )


def block_outputs(slots, weights, totals, parts, pieces, flip, first, last):
    heads = slots.shape[0]
    _, rows, width = totals[0].shape
    pairs = sum(part.shape[0] for part in parts)
    rows //= pieces
    pieces = last - first
    piece = jax.ShapeDtypeStruct((rows, heads // 2 * width), jnp.bfloat16)
    return pl.pallas_call(
        functools.partial(
            value_kernel,
            inputs=len(parts),
            flip=flip,
            first=first * rows,
            last=last * rows,
        ),
        in_specs=[in_vmem] * (5 + len(parts)),
        out_specs=[in_vmem] * pieces,
        out_shape=[piece] * pieces,
        scratch_shapes=[pltpu.VMEM((2 * pairs, BLOCK, width), jnp.bfloat16)],
        compiler_params=granted,
        name="block_outputs",
    )(slots, *weights, *totals, *parts)


def join_kernel(*refs, share, width):
    *pieces, out_ref = refs
    place = lax.axis_index("head")
    chips = len(pieces) // 2
    rows = out_ref.shape[0]
    pairs = pieces[0].shape[1] // width // share
    low = lower_half((rows, width))
    for n in range(chips):
        for part in range(share):
            column = jnp.bitwise_xor(place, across(n, share) ^ part) * (2 * pairs * width)
            for pair in range(pairs):
                at = (part * pairs + pair) * width
                first, second = (
                    piece[:, at : at + width].astype(jnp.float32)
                    for piece in (pieces[n], pieces[chips + n])
                )
                even = jnp.where(low, first, second)
                odd = pltpu.roll(jnp.where(low, second, first), width // 2, 1)
                for m, out in enumerate((even, odd)):
                    to = pl.multiple_of(column + (2 * pair + m) * width, width)
                    out_ref[:, pl.ds(to, width)] = out.astype(jnp.bfloat16)


def join_pieces(pieces, share, width):
    rows, across = pieces[0].shape
    return pl.pallas_call(
        functools.partial(join_kernel, share=share, width=width),
        in_specs=[in_vmem] * len(pieces),
        out_specs=in_vmem,
        out_shape=jax.ShapeDtypeStruct((rows, across * len(pieces)), jnp.bfloat16),
        compiler_params=granted,
        name="join_pieces",
    )(*pieces)


def on_device(queries, positions, key_codes, value_codes, scale_index, scale_table, block_lists):
    cycle_size = lax.axis_size("ctx")
    cycle_place = lax.axis_index("ctx")
    head_count = lax.axis_size("head")
    head_place = lax.axis_index("head")
    reach_hops = min(3, (cycle_size - 1) // 2)
    pairs = paired(cycle_size, reach_hops)
    rows_dev, heads_dev, head_width = queries.shape
    key_blocks = key_codes.shape[1] // BLOCK
    share = GROUP // heads_dev
    assert share == 2 and rows_dev == BLOCK
    core = head_place % share
    group = head_place // share
    groups = head_count // share

    (keys,) = begin(key_kernel, scale_index, scale_table, key_codes, 1)
    *values, queries, positions, block_lists = begin(
        half_kernel,
        scale_index,
        scale_table,
        value_codes,
        2,
        keys,
        others=(queries, positions, block_lists),
    )
    far_keys = keys
    key_parts = []
    for _ in range(reach_hops):
        far_keys = sent(far_keys, share, pairs)
        key_parts.append(far_keys)
    own_lists = lax.dynamic_index_in_dim(block_lists, cycle_place, 1, keepdims=False)
    def ordered(x):
        cut = x.reshape((groups, share, rows_dev // head_count) + x.shape[1:])
        taken = [
            lax.dynamic_slice(
                cut,
                (jnp.bitwise_xor(group, n), jnp.bitwise_xor(core, part ^ n % share))
                + (0,) * x.ndim,
                (1, 1) + cut.shape[2:],
            )
            for part in range(share)
            for n in range(groups)
        ]
        return jnp.concatenate(taken, axis=0).reshape(x.shape)

    frequency = ROPE_BASE ** (
        -2.0 * (jnp.arange(head_width) // 2).astype(jnp.float32) / head_width
    )
    angles = ordered(positions).astype(jnp.float32)[:, None] * frequency[None, :]
    signs = jnp.where(jnp.arange(head_width) % 2 == 0, -1.0, 1.0)
    cosine = jnp.cos(angles)
    sine = jnp.sin(angles) * signs[None, :]

    picks = own_lists.shape[1]
    carried = jnp.pad(own_lists.astype(jnp.bfloat16), ((0, 0), (0, head_width - picks)))
    own, sibling = turn_queries(
        jnp.transpose(ordered(queries), (1, 0, 2)), cosine, sine, carried
    )
    sibling, key_parts[0] = lax.optimization_barrier((sibling, key_parts[0]))
    key_parts = [keys] + [part for far in key_parts for part in (far, swapped(far, 1))]
    sibling = swapped(sibling, 1)
    sibling_lists = sibling[:, rows_dev // share, :picks].astype(jnp.int32)
    lists = jnp.concatenate([own_lists, sibling_lists], axis=0)
    offset = jnp.mod(lists // key_blocks - cycle_place, cycle_size)
    above = offset <= reach_hops
    hops = jnp.where(above, offset, cycle_size - offset)
    outer = jnp.logical_or(cycle_place % 4 == 0, cycle_place % 4 == 3)
    from_above = (cycle_place % 2 == (core == outer)) if pairs else core == 1
    place = 2 * hops - jnp.where(above == from_above, 1, 0)
    slots = lists % key_blocks + key_blocks * jnp.where(offset == 0, 0, place)

    steps = []
    far_values = values
    for _ in range(reach_hops):
        far_values = [sent(half, share, pairs) for half in far_values]
        steps.append(far_values)
    rows = rows_dev // share
    own_weights, own_total, held = block_weights(slots[:heads_dev], own, key_parts, rows)
    sibling_weights, sibling_total = block_weights(slots[heads_dev:], sibling, [held], rows)
    weights = (own_weights, sibling_weights)
    totals = (own_total, sibling_total)

    inner = slots % key_blocks
    places = slots // key_blocks * (key_blocks // 2) + inner % (key_blocks // 2)
    parity = jnp.arange(slots.shape[0])[:, None] % 2
    turned_places = (2 * reach_hops + 1) * (key_blocks // 2)
    ready = own_weights
    moved = []
    for half in range(2):
        *far_values, ready = lax.optimization_barrier((*[step[half] for step in steps], ready))
        value_parts = [values[half]]
        for far in far_values:
            value_parts += [far, swapped(far, 1)]
        side = jnp.bitwise_xor(inner // (key_blocks // 2), jnp.bitwise_xor(parity, half))
        outputs = functools.partial(
            block_outputs,
            places + turned_places * side,
            weights,
            totals,
            value_parts,
            groups,
            half,
        )
        if half == 0 or groups == 1:
            pieces = outputs(0, groups)
        else:
            pieces = [None, *outputs(1, groups)]
        sent_pieces = [swapped(pieces[n], across(n, share)) for n in range(1, groups)]
        if pieces[0] is None:
            pieces[0] = outputs(0, 1)[0]
        moved += [pieces[0], *sent_pieces]
        ready = pieces[0]
    return join_pieces(moved, share, head_width)


def solution(mesh):
    placed = (
        P(("groups", "ctx"), "head", None),
        P(("groups", "ctx")),
        P("groups", "ctx", None),
        P("groups", "ctx", None),
        P("groups", None, "ctx"),
        P(),
        P(("groups", "head"), None, None),
    )
    return jax.shard_map(
        on_device,
        mesh=mesh,
        in_specs=placed,
        out_specs=P(("groups", "ctx", "head"), None),
        check_vma=False,
    )
```

```python
import functools
import math

import jax
import jax.numpy as jnp
from jax import lax
from jax.experimental import pallas as pl
from jax.experimental.pallas import tpu as pltpu
from jax.sharding import PartitionSpec as P

GROUP = 16
BLOCK = 128
ROW_TILE = 16
ABREAST = 2
ROPE_BASE = 500000.0
VMEM_GRANT = 16 * 2**20

in_vmem = pl.BlockSpec(memory_space=pltpu.VMEM)
granted = pltpu.CompilerParams(vmem_limit_bytes=VMEM_GRANT)


def paired(cycle, hops):
    return hops == 1 and cycle % 2 == 0


def source(place, part, cycle, pairs):
    if not pairs:
        return (place + (1 if part else -1)) % cycle, part
    outer = place % 4 in (0, 3)
    odd = part == outer
    other = (place + (1 if place % 2 == odd else -1)) % cycle
    return other, int((other % 4 in (0, 3)) == odd)


def sent(x, share, pairs):
    cycle = lax.axis_size("ctx")
    heads = lax.axis_size("head")
    moves = []
    for place in range(cycle):
        for head in range(heads):
            part = head % share
            other, core = source(place, part, cycle, pairs)
            moves.append((other * heads + head - part + core, place * heads + head))
    return lax.ppermute(x, ("ctx", "head"), moves)


def across(n, share):
    return n * share ^ n % share


def swapped(x, mask):
    return lax.ppermute(x, "head", [(i, i ^ mask) for i in range(lax.axis_size("head"))])


def fetch(index_hbm, table_hbm, codes_hbm, index_ref, table_ref, codes_ref, arrived, row):
    groups = index_hbm.shape[1]
    kv_head = lax.axis_index("head") * groups // lax.axis_size("head")
    copies = [
        pltpu.make_async_copy(source, target, arrived.at[n])
        for n, (source, target) in enumerate(
            (
                (index_hbm, index_ref),
                (table_hbm, table_ref),
                (codes_hbm.at[kv_head], codes_ref),
            )
        )
    ]
    for copy in copies:
        copy.start()
    for copy in copies[:2]:
        copy.wait()
    scales = [
        table_ref[row, index_ref[row, kv_head, block]] for block in range(index_hbm.shape[2])
    ]
    copies[2].wait()
    return scales


def key_kernel(index_hbm, table_hbm, codes_hbm, out_ref, *scratch):
    codes_ref = scratch[2]
    for block, scale in enumerate(fetch(index_hbm, table_hbm, codes_hbm, *scratch, 0)):
        codes = codes_ref[block * BLOCK : (block + 1) * BLOCK, :].astype(jnp.float32)
        out_ref[block] = (codes * scale).astype(jnp.bfloat16)


def half_kernel(index_hbm, table_hbm, codes_hbm, _, *rest):
    *others, index_ref, table_ref, codes_ref, arrived = rest
    scratch = (index_ref, table_ref, codes_ref, arrived)
    count = len(others) // 2 - 1
    first_ref, second_ref = others[count : count + 2]
    copies = [
        pltpu.make_async_copy(others[n], others[count + 2 + n], arrived.at[3 + n])
        for n in range(count)
    ]
    for copy in copies:
        copy.start()
    scales = fetch(index_hbm, table_hbm, codes_hbm, *scratch, 1)
    pairs = first_ref.shape[0]
    width = codes_ref.shape[1]
    low = lower_half((BLOCK, width))
    for pair in range(pairs):
        left, right = (
            codes_ref[block * BLOCK : (block + 1) * BLOCK, :].astype(jnp.float32) * scales[block]
            for block in (pair, pair + pairs)
        )
        first = jnp.where(low, left, pltpu.roll(right, width // 2, 1))
        second = jnp.where(low, pltpu.roll(left, width // 2, 1), right)
        first_ref[pair] = first.astype(jnp.bfloat16)
        second_ref[pair] = second.astype(jnp.bfloat16)
    for copy in copies:
        copy.wait()


def lower_half(shape):
    return lax.broadcasted_iota(jnp.int32, shape, 1) < shape[1] // 2


def begin(kernel, scale_index, scale_table, codes, outputs, *after, others=()):
    _, keys_dev, width = codes.shape
    blocks = keys_dev // BLOCK // outputs
    stay = functools.partial(pltpu.with_memory_space_constraint, memory_space=pltpu.HBM)
    return pl.pallas_call(
        kernel,
        in_specs=[pl.BlockSpec(memory_space=pltpu.HBM)] * 3
        + [pl.BlockSpec(memory_space=pl.ANY)] * len(after)
        + [pl.BlockSpec(memory_space=pltpu.HBM)] * len(others),
        out_specs=[in_vmem] * (outputs + len(others)),
        out_shape=[pltpu.VMEM((blocks, BLOCK, width), jnp.bfloat16)] * outputs
        + [pltpu.VMEM(other.shape, other.dtype) for other in others],
        scratch_shapes=[
            pltpu.SMEM(scale_index.shape, scale_index.dtype),
            pltpu.SMEM(scale_table.shape, scale_table.dtype),
            pltpu.VMEM((keys_dev, width), codes.dtype),
            pltpu.SemaphoreType.DMA((3 + len(others),)),
        ],
        compiler_params=granted,
        name=kernel.__name__,
    )(
        stay(scale_index),
        stay(scale_table),
        stay(codes),
        *after,
        *[stay(other) for other in others],
    )


def turn_kernel(queries_ref, cosine_ref, sine_ref, lists_ref, own_ref, sibling_ref):
    heads_dev, rows, width = own_ref.shape
    cosine = cosine_ref[...]
    sine = sine_ref[...]
    even = lax.rem(lax.broadcasted_iota(jnp.int32, cosine.shape, 1), 2) == 0
    for head in range(heads_dev):
        plain = queries_ref[head].astype(jnp.float32)
        other = jnp.where(even, pltpu.roll(plain, width - 1, 1), pltpu.roll(plain, 1, 1))
        turned = (plain * cosine + other * sine).astype(jnp.bfloat16)
        own_ref[head] = turned[:rows]
        sibling_ref[head, :rows] = turned[rows:]
        sibling_ref[head, rows:] = jnp.broadcast_to(
            lists_ref[head : head + 1], sibling_ref[head, rows:].shape
        )


def turn_queries(queries, cosine, sine, lists):
    heads_dev, rows, width = queries.shape
    half = (heads_dev, rows // 2, width)
    more = (heads_dev, rows // 2 + ROW_TILE, width)
    return pl.pallas_call(
        turn_kernel,
        in_specs=[in_vmem] * 4,
        out_specs=[in_vmem] * 2,
        out_shape=[
            jax.ShapeDtypeStruct(half, jnp.bfloat16),
            jax.ShapeDtypeStruct(more, jnp.bfloat16),
        ],
        compiler_params=granted,
        name="turn_queries",
    )(queries, cosine, sine, lists)


def score_kernel(slots_ref, queries_ref, *rest, inputs):
    parts = rest[:inputs]
    weights_ref, total_ref, store = rest[inputs : inputs + 3]
    heads, rows, width = total_ref.shape
    picks = slots_ref.shape[1]
    slots = slots_ref[...]
    factor = math.log2(math.e) / math.sqrt(width)
    at = 0
    for part in parts:
        for block in range(part.shape[0]):
            store[at] = part[block].astype(jnp.float32).T.astype(jnp.bfloat16)
            at += 1
    for head in range(heads):
        turned = queries_ref[head, :rows]
        scores = []
        for i in range(0, picks, ABREAST):
            wide = jnp.concatenate([store[slots[head, i + j]] for j in range(ABREAST)], axis=1)
            wide = jnp.dot(turned, wide, preferred_element_type=jnp.float32)
            scores += [wide[:, j * BLOCK : (j + 1) * BLOCK] for j in range(ABREAST)]
        top = scores[0]
        for i in range(1, picks):
            top = jnp.maximum(top, scores[i])
        top = jnp.max(top, axis=1, keepdims=True)
        total = jnp.zeros((rows, BLOCK), jnp.float32)
        for i in range(picks):
            weight = jnp.exp2((scores[i] - top) * factor)
            total = total + weight
            weights_ref[head, :, i * BLOCK : (i + 1) * BLOCK] = weight.astype(jnp.bfloat16)
        total = jnp.sum(total, axis=1, keepdims=True)
        total_ref[head] = jnp.broadcast_to(1.0 / total, (rows, width))


def held_kernel(slots_ref, queries_ref, store, weights_ref, total_ref):
    score_kernel(slots_ref, queries_ref, weights_ref, total_ref, store, inputs=0)


def block_weights(slots, queries, parts, rows):
    width = queries.shape[2]
    heads, picks = slots.shape
    blocks = sum(part.shape[0] for part in parts)
    outputs = [
        jax.ShapeDtypeStruct((heads, rows, picks * BLOCK), jnp.bfloat16),
        jax.ShapeDtypeStruct((heads, rows, width), jnp.float32),
    ]
    if len(parts) > 1:
        outputs.append(jax.ShapeDtypeStruct((blocks, width, BLOCK), jnp.bfloat16))
    return pl.pallas_call(
        functools.partial(score_kernel, inputs=len(parts)) if len(parts) > 1 else held_kernel,
        in_specs=[in_vmem] * (2 + len(parts)),
        out_specs=[in_vmem] * len(outputs),
        out_shape=outputs,
        compiler_params=granted,
        name="block_weights",
    )(slots, queries, *parts)


def value_kernel(slots_ref, *rest, inputs, flip, first, last):
    weights = rest[:2]
    totals = rest[2:4]
    parts = rest[4 : 4 + inputs]
    pieces = rest[4 + inputs : -1]
    store = rest[-1]
    heads_dev, _, width = totals[0].shape
    heads, picks = slots_ref.shape
    rows = pieces[0].shape[0]
    slots = slots_ref[...]
    half = store.shape[0] // 2
    at = 0
    for part in parts:
        for pair in range(part.shape[0]):
            block = part[pair]
            store[at] = block
            turned = pltpu.roll(block.astype(jnp.float32), width // 2, 1)
            store[half + at] = turned.astype(jnp.bfloat16)
            at += 1
    low = lower_half((last - first, width))
    for pair in range(heads // 2):
        both = []
        for head in (2 * pair, 2 * pair + 1):
            picked = jnp.concatenate([store[slots[head, i]] for i in range(picks)], axis=0)
            owner, place = divmod(head, heads_dev)
            weight = weights[owner][place, first:last]
            out = jnp.dot(weight, picked, preferred_element_type=jnp.float32)
            both.append(out * totals[owner][place, first:last])
        out = jnp.where(low, both[flip], both[1 - flip])
        for n, piece in enumerate(pieces):
            piece[:, pair * width : (pair + 1) * width] = out[n * rows : (n + 1) * rows].astype(
                jnp.bfloat16
            )


def block_outputs(slots, weights, totals, parts, pieces, flip, first, last):
    heads = slots.shape[0]
    _, rows, width = totals[0].shape
    pairs = sum(part.shape[0] for part in parts)
    rows //= pieces
    pieces = last - first
    piece = jax.ShapeDtypeStruct((rows, heads // 2 * width), jnp.bfloat16)
    return pl.pallas_call(
        functools.partial(
            value_kernel,
            inputs=len(parts),
            flip=flip,
            first=first * rows,
            last=last * rows,
        ),
        in_specs=[in_vmem] * (5 + len(parts)),
        out_specs=[in_vmem] * pieces,
        out_shape=[piece] * pieces,
        scratch_shapes=[pltpu.VMEM((2 * pairs, BLOCK, width), jnp.bfloat16)],
        compiler_params=granted,
        name="block_outputs",
    )(slots, *weights, *totals, *parts)


def join_kernel(*refs, share, width):
    *pieces, out_ref = refs
    place = lax.axis_index("head")
    chips = len(pieces) // 2
    rows = out_ref.shape[0]
    pairs = pieces[0].shape[1] // width // share
    low = lower_half((rows, width))
    for n in range(chips):
        for part in range(share):
            column = jnp.bitwise_xor(place, across(n, share) ^ part) * (2 * pairs * width)
            for pair in range(pairs):
                at = (part * pairs + pair) * width
                first, second = (
                    piece[:, at : at + width].astype(jnp.float32)
                    for piece in (pieces[n], pieces[chips + n])
                )
                even = jnp.where(low, first, second)
                odd = pltpu.roll(jnp.where(low, second, first), width // 2, 1)
                for m, out in enumerate((even, odd)):
                    to = pl.multiple_of(column + (2 * pair + m) * width, width)
                    out_ref[:, pl.ds(to, width)] = out.astype(jnp.bfloat16)


def join_pieces(pieces, share, width):
    rows, across = pieces[0].shape
    return pl.pallas_call(
        functools.partial(join_kernel, share=share, width=width),
        in_specs=[in_vmem] * len(pieces),
        out_specs=in_vmem,
        out_shape=jax.ShapeDtypeStruct((rows, across * len(pieces)), jnp.bfloat16),
        compiler_params=granted,
        name="join_pieces",
    )(*pieces)


def on_device(queries, positions, key_codes, value_codes, scale_index, scale_table, block_lists):
    cycle_size = lax.axis_size("ctx")
    cycle_place = lax.axis_index("ctx")
    head_count = lax.axis_size("head")
    head_place = lax.axis_index("head")
    reach_hops = min(3, (cycle_size - 1) // 2)
    pairs = paired(cycle_size, reach_hops)
    rows_dev, heads_dev, head_width = queries.shape
    key_blocks = key_codes.shape[1] // BLOCK
    share = GROUP // heads_dev
    assert share == 2 and rows_dev == BLOCK
    core = head_place % share
    group = head_place // share
    groups = head_count // share

    (keys,) = begin(key_kernel, scale_index, scale_table, key_codes, 1)
    *values, brought, positions, block_lists = begin(
        half_kernel,
        scale_index,
        scale_table,
        value_codes,
        2,
        keys,
        others=(queries.reshape(-1, head_width), positions, block_lists),
    )
    queries = brought.reshape(queries.shape)
    far_keys = keys
    key_parts = []
    for _ in range(reach_hops):
        far_keys = sent(far_keys, share, pairs)
        key_parts.append(far_keys)
    own_lists = lax.dynamic_index_in_dim(block_lists, cycle_place, 1, keepdims=False)

    def ordered(x):
        cut = x.reshape((groups, share, rows_dev // head_count) + x.shape[1:])
        taken = [
            lax.dynamic_slice(
                cut,
                (jnp.bitwise_xor(group, n), jnp.bitwise_xor(core, part ^ n % share))
                + (0,) * x.ndim,
                (1, 1) + cut.shape[2:],
            )
            for part in range(share)
            for n in range(groups)
        ]
        return jnp.concatenate(taken, axis=0).reshape(x.shape)

    frequency = ROPE_BASE ** (
        -2.0 * (jnp.arange(head_width) // 2).astype(jnp.float32) / head_width
    )
    angles = ordered(positions).astype(jnp.float32)[:, None] * frequency[None, :]
    signs = jnp.where(jnp.arange(head_width) % 2 == 0, -1.0, 1.0)
    cosine = jnp.cos(angles)
    sine = jnp.sin(angles) * signs[None, :]

    picks = own_lists.shape[1]
    carried = jnp.pad(own_lists.astype(jnp.bfloat16), ((0, 0), (0, head_width - picks)))
    own, sibling = turn_queries(
        jnp.transpose(ordered(queries), (1, 0, 2)), cosine, sine, carried
    )
    sibling, key_parts[0] = lax.optimization_barrier((sibling, key_parts[0]))
    key_parts = [keys] + [part for far in key_parts for part in (far, swapped(far, 1))]
    sibling = swapped(sibling, 1)
    sibling_lists = sibling[:, rows_dev // share, :picks].astype(jnp.int32)
    lists = jnp.concatenate([own_lists, sibling_lists], axis=0)
    offset = jnp.mod(lists // key_blocks - cycle_place, cycle_size)
    above = offset <= reach_hops
    hops = jnp.where(above, offset, cycle_size - offset)
    outer = jnp.logical_or(cycle_place % 4 == 0, cycle_place % 4 == 3)
    from_above = (cycle_place % 2 == (core == outer)) if pairs else core == 1
    place = 2 * hops - jnp.where(above == from_above, 1, 0)
    slots = lists % key_blocks + key_blocks * jnp.where(offset == 0, 0, place)

    steps = []
    far_values = values
    for _ in range(reach_hops):
        far_values = [sent(half, share, pairs) for half in far_values]
        steps.append(far_values)
    rows = rows_dev // share
    own_weights, own_total, held = block_weights(slots[:heads_dev], own, key_parts, rows)
    sibling_weights, sibling_total = block_weights(slots[heads_dev:], sibling, [held], rows)
    weights = (own_weights, sibling_weights)
    totals = (own_total, sibling_total)

    inner = slots % key_blocks
    places = slots // key_blocks * (key_blocks // 2) + inner % (key_blocks // 2)
    parity = jnp.arange(slots.shape[0])[:, None] % 2
    turned_places = (2 * reach_hops + 1) * (key_blocks // 2)
    ready = own_weights
    moved = []
    for half in range(2):
        *far_values, ready = lax.optimization_barrier((*[step[half] for step in steps], ready))
        value_parts = [values[half]]
        for far in far_values:
            value_parts += [far, swapped(far, 1)]
        side = jnp.bitwise_xor(inner // (key_blocks // 2), jnp.bitwise_xor(parity, half))
        outputs = functools.partial(
            block_outputs,
            places + turned_places * side,
            weights,
            totals,
            value_parts,
            groups,
            half,
        )
        if half == 0 or groups == 1:
            pieces = outputs(0, groups)
        else:
            pieces = [None, *outputs(1, groups)]
        sent_pieces = [swapped(pieces[n], across(n, share)) for n in range(1, groups)]
        if pieces[0] is None:
            pieces[0] = outputs(0, 1)[0]
        moved += [pieces[0], *sent_pieces]
        ready = pieces[0]
    return join_pieces(moved, share, head_width)


def solution(mesh):
    placed = (
        P(("groups", "ctx"), "head", None),
        P(("groups", "ctx")),
        P("groups", "ctx", None),
        P("groups", "ctx", None),
        P("groups", None, "ctx"),
        P(),
        P(("groups", "head"), None, None),
    )
    return jax.shard_map(
        on_device,
        mesh=mesh,
        in_specs=placed,
        out_specs=P(("groups", "ctx", "head"), None),
        check_vma=False,
    )
```

```python
import functools
import math

import jax
import jax.numpy as jnp
from jax import lax
from jax.experimental import pallas as pl
from jax.experimental.pallas import tpu as pltpu
from jax.sharding import PartitionSpec as P

GROUP = 16
BLOCK = 128
ROW_TILE = 16
ABREAST = 2
ROPE_BASE = 500000.0
VMEM_GRANT = 16 * 2**20

in_vmem = pl.BlockSpec(memory_space=pltpu.VMEM)
granted = pltpu.CompilerParams(vmem_limit_bytes=VMEM_GRANT)


def paired(cycle, hops):
    return hops == 1 and cycle % 2 == 0


def source(place, part, cycle, pairs):
    if not pairs:
        return (place + (1 if part else -1)) % cycle, part
    outer = place % 4 in (0, 3)
    odd = part == outer
    other = (place + (1 if place % 2 == odd else -1)) % cycle
    return other, int((other % 4 in (0, 3)) == odd)


def sent(x, share, pairs):
    cycle = lax.axis_size("ctx")
    heads = lax.axis_size("head")
    moves = []
    for place in range(cycle):
        for head in range(heads):
            part = head % share
            other, core = source(place, part, cycle, pairs)
            moves.append((other * heads + head - part + core, place * heads + head))
    return lax.ppermute(x, ("ctx", "head"), moves)


def across(n, share):
    return n * share ^ n % share


def swapped(x, mask):
    return lax.ppermute(x, "head", [(i, i ^ mask) for i in range(lax.axis_size("head"))])


def fetch(index_hbm, table_hbm, codes_hbm, index_ref, table_ref, codes_ref, arrived, row):
    groups = index_hbm.shape[1]
    kv_head = lax.axis_index("head") * groups // lax.axis_size("head")
    copies = [
        pltpu.make_async_copy(source, target, arrived.at[n])
        for n, (source, target) in enumerate(
            (
                (index_hbm, index_ref),
                (table_hbm, table_ref),
                (codes_hbm.at[kv_head], codes_ref),
            )
        )
    ]
    for copy in copies:
        copy.start()
    for copy in copies[:2]:
        copy.wait()
    scales = [
        table_ref[row, index_ref[row, kv_head, block]] for block in range(index_hbm.shape[2])
    ]
    copies[2].wait()
    return scales


def key_kernel(index_hbm, table_hbm, codes_hbm, out_ref, *scratch):
    codes_ref = scratch[2]
    for block, scale in enumerate(fetch(index_hbm, table_hbm, codes_hbm, *scratch, 0)):
        codes = codes_ref[block * BLOCK : (block + 1) * BLOCK, :].astype(jnp.float32)
        out_ref[block] = (codes * scale).astype(jnp.bfloat16)


def half_kernel(index_hbm, table_hbm, codes_hbm, _, *rest):
    *others, index_ref, table_ref, codes_ref, arrived = rest
    scratch = (index_ref, table_ref, codes_ref, arrived)
    count = len(others) // 2 - 1
    first_ref, second_ref = others[count : count + 2]
    copies = [
        pltpu.make_async_copy(others[n], others[count + 2 + n], arrived.at[3 + n])
        for n in range(count)
    ]
    for copy in copies:
        copy.start()
    scales = fetch(index_hbm, table_hbm, codes_hbm, *scratch, 1)
    pairs = first_ref.shape[0]
    width = codes_ref.shape[1]
    low = lower_half((BLOCK, width))
    for pair in range(pairs):
        left, right = (
            codes_ref[block * BLOCK : (block + 1) * BLOCK, :].astype(jnp.float32) * scales[block]
            for block in (pair, pair + pairs)
        )
        first = jnp.where(low, left, pltpu.roll(right, width // 2, 1))
        second = jnp.where(low, pltpu.roll(left, width // 2, 1), right)
        first_ref[pair] = first.astype(jnp.bfloat16)
        second_ref[pair] = second.astype(jnp.bfloat16)
    for copy in copies:
        copy.wait()


def lower_half(shape):
    return lax.broadcasted_iota(jnp.int32, shape, 1) < shape[1] // 2


def begin(kernel, scale_index, scale_table, codes, outputs, *after, others=()):
    _, keys_dev, width = codes.shape
    blocks = keys_dev // BLOCK // outputs
    stay = functools.partial(pltpu.with_memory_space_constraint, memory_space=pltpu.HBM)
    return pl.pallas_call(
        kernel,
        in_specs=[pl.BlockSpec(memory_space=pltpu.HBM)] * 3
        + [pl.BlockSpec(memory_space=pl.ANY)] * len(after)
        + [pl.BlockSpec(memory_space=pltpu.HBM)] * len(others),
        out_specs=[in_vmem] * (outputs + len(others)),
        out_shape=[pltpu.VMEM((blocks, BLOCK, width), jnp.bfloat16)] * outputs
        + [pltpu.VMEM(other.shape, other.dtype) for other in others],
        scratch_shapes=[
            pltpu.SMEM(scale_index.shape, scale_index.dtype),
            pltpu.SMEM(scale_table.shape, scale_table.dtype),
            pltpu.VMEM((keys_dev, width), codes.dtype),
            pltpu.SemaphoreType.DMA((3 + len(others),)),
        ],
        compiler_params=granted,
        name=kernel.__name__,
    )(
        stay(scale_index),
        stay(scale_table),
        stay(codes),
        *after,
        *[stay(other) for other in others],
    )


def turn_kernel(queries_ref, cosine_ref, sine_ref, lists_ref, own_ref, sibling_ref):
    heads_dev, rows, width = own_ref.shape
    cosine = cosine_ref[...]
    sine = sine_ref[...]
    even = lax.rem(lax.broadcasted_iota(jnp.int32, cosine.shape, 1), 2) == 0
    for head in range(heads_dev):
        plain = queries_ref[head].astype(jnp.float32)
        other = jnp.where(even, pltpu.roll(plain, width - 1, 1), pltpu.roll(plain, 1, 1))
        turned = (plain * cosine + other * sine).astype(jnp.bfloat16)
        own_ref[head] = turned[:rows]
        sibling_ref[head, :rows] = turned[rows:]
        sibling_ref[head, rows:] = jnp.broadcast_to(
            lists_ref[head : head + 1], sibling_ref[head, rows:].shape
        )


def turn_queries(queries, cosine, sine, lists):
    heads_dev, rows, width = queries.shape
    half = (heads_dev, rows // 2, width)
    more = (heads_dev, rows // 2 + ROW_TILE, width)
    return pl.pallas_call(
        turn_kernel,
        in_specs=[in_vmem] * 4,
        out_specs=[in_vmem] * 2,
        out_shape=[
            jax.ShapeDtypeStruct(half, jnp.bfloat16),
            jax.ShapeDtypeStruct(more, jnp.bfloat16),
        ],
        compiler_params=granted,
        name="turn_queries",
    )(queries, cosine, sine, lists)


def score_kernel(slots_ref, queries_ref, *rest, inputs):
    parts = rest[:inputs]
    weights_ref, total_ref, store = rest[inputs : inputs + 3]
    heads, rows, width = total_ref.shape
    picks = slots_ref.shape[1]
    slots = slots_ref[...]
    factor = math.log2(math.e) / math.sqrt(width)
    at = 0
    for part in parts:
        for block in range(part.shape[0]):
            store[at] = part[block].astype(jnp.float32).T.astype(jnp.bfloat16)
            at += 1
    for head in range(heads):
        turned = queries_ref[head, :rows]
        scores = []
        for i in range(0, picks, ABREAST):
            wide = jnp.concatenate([store[slots[head, i + j]] for j in range(ABREAST)], axis=1)
            wide = jnp.dot(turned, wide, preferred_element_type=jnp.float32)
            scores += [wide[:, j * BLOCK : (j + 1) * BLOCK] for j in range(ABREAST)]
        top = scores[0]
        for i in range(1, picks):
            top = jnp.maximum(top, scores[i])
        top = jnp.max(top, axis=1, keepdims=True)
        total = jnp.zeros((rows, BLOCK), jnp.float32)
        for i in range(picks):
            weight = jnp.exp2((scores[i] - top) * factor)
            total = total + weight
            weights_ref[head, :, i * BLOCK : (i + 1) * BLOCK] = weight.astype(jnp.bfloat16)
        total = jnp.sum(total, axis=1, keepdims=True)
        total_ref[head] = jnp.broadcast_to(1.0 / total, (rows, width))


def held_kernel(slots_ref, queries_ref, store, weights_ref, total_ref):
    score_kernel(slots_ref, queries_ref, weights_ref, total_ref, store, inputs=0)


def block_weights(slots, queries, parts, rows):
    width = queries.shape[2]
    heads, picks = slots.shape
    blocks = sum(part.shape[0] for part in parts)
    outputs = [
        jax.ShapeDtypeStruct((heads, rows, picks * BLOCK), jnp.bfloat16),
        jax.ShapeDtypeStruct((heads, rows, width), jnp.float32),
    ]
    if len(parts) > 1:
        outputs.append(jax.ShapeDtypeStruct((blocks, width, BLOCK), jnp.bfloat16))
    return pl.pallas_call(
        functools.partial(score_kernel, inputs=len(parts)) if len(parts) > 1 else held_kernel,
        in_specs=[in_vmem] * (2 + len(parts)),
        out_specs=[in_vmem] * len(outputs),
        out_shape=outputs,
        compiler_params=granted,
        name="block_weights",
    )(slots, queries, *parts)


def value_kernel(slots_ref, *rest, inputs, flip, first, last):
    weights = rest[:2]
    totals = rest[2:4]
    parts = rest[4 : 4 + inputs]
    pieces = rest[4 + inputs : -1]
    store = rest[-1]
    heads_dev, _, width = totals[0].shape
    heads, picks = slots_ref.shape
    rows = pieces[0].shape[0]
    slots = slots_ref[...]
    half = store.shape[0] // 2
    at = 0
    for part in parts:
        for pair in range(part.shape[0]):
            block = part[pair]
            store[at] = block
            turned = pltpu.roll(block.astype(jnp.float32), width // 2, 1)
            store[half + at] = turned.astype(jnp.bfloat16)
            at += 1
    low = lower_half((last - first, width))
    for pair in range(heads // 2):
        both = []
        for head in (2 * pair, 2 * pair + 1):
            picked = jnp.concatenate([store[slots[head, i]] for i in range(picks)], axis=0)
            owner, place = divmod(head, heads_dev)
            weight = weights[owner][place, first:last]
            out = jnp.dot(weight, picked, preferred_element_type=jnp.float32)
            both.append(out * totals[owner][place, first:last])
        out = jnp.where(low, both[flip], both[1 - flip])
        for n, piece in enumerate(pieces):
            piece[:, pair * width : (pair + 1) * width] = out[n * rows : (n + 1) * rows].astype(
                jnp.bfloat16
            )


def block_outputs(slots, weights, totals, parts, pieces, flip, first, last):
    heads = slots.shape[0]
    _, rows, width = totals[0].shape
    pairs = sum(part.shape[0] for part in parts)
    rows //= pieces
    pieces = last - first
    piece = jax.ShapeDtypeStruct((rows, heads // 2 * width), jnp.bfloat16)
    return pl.pallas_call(
        functools.partial(
            value_kernel,
            inputs=len(parts),
            flip=flip,
            first=first * rows,
            last=last * rows,
        ),
        in_specs=[in_vmem] * (5 + len(parts)),
        out_specs=[in_vmem] * pieces,
        out_shape=[piece] * pieces,
        scratch_shapes=[pltpu.VMEM((2 * pairs, BLOCK, width), jnp.bfloat16)],
        compiler_params=granted,
        name="block_outputs",
    )(slots, *weights, *totals, *parts)


def join_kernel(*refs, share, width):
    *pieces, out_hbm, held, left = refs
    place = lax.axis_index("head")
    chips = len(pieces) // 2
    rows = held.shape[0]
    pairs = pieces[0].shape[1] // width // share
    size = 2 * pairs * width
    low = lower_half((rows, width))
    copies = []
    for n in range(chips):
        for part in range(share):
            base = (n * share + part) * size
            for pair in range(pairs):
                at = (part * pairs + pair) * width
                first, second = (
                    piece[:, at : at + width].astype(jnp.float32)
                    for piece in (pieces[n], pieces[chips + n])
                )
                even = jnp.where(low, first, second)
                odd = pltpu.roll(jnp.where(low, second, first), width // 2, 1)
                for m, out in enumerate((even, odd)):
                    to = base + (2 * pair + m) * width
                    held[:, to : to + width] = out.astype(jnp.bfloat16)
            column = jnp.bitwise_xor(place, across(n, share) ^ part) * size
            copy = pltpu.make_async_copy(
                held.at[:, pl.ds(base, size)],
                out_hbm.at[:, pl.ds(pl.multiple_of(column, size), size)],
                left.at[n * share + part],
            )
            copy.start()
            copies.append(copy)
    for copy in copies:
        copy.wait()


def join_pieces(pieces, share, width):
    rows, columns = pieces[0].shape
    shape = (rows, columns * len(pieces))
    return pl.pallas_call(
        functools.partial(join_kernel, share=share, width=width),
        in_specs=[in_vmem] * len(pieces),
        out_specs=pl.BlockSpec(memory_space=pltpu.HBM),
        out_shape=jax.ShapeDtypeStruct(shape, jnp.bfloat16),
        scratch_shapes=[
            pltpu.VMEM(shape, jnp.bfloat16),
            pltpu.SemaphoreType.DMA((len(pieces) // 2 * share,)),
        ],
        compiler_params=granted,
        name="join_pieces",
    )(*pieces)


def on_device(queries, positions, key_codes, value_codes, scale_index, scale_table, block_lists):
    cycle_size = lax.axis_size("ctx")
    cycle_place = lax.axis_index("ctx")
    head_count = lax.axis_size("head")
    head_place = lax.axis_index("head")
    reach_hops = min(3, (cycle_size - 1) // 2)
    pairs = paired(cycle_size, reach_hops)
    rows_dev, heads_dev, head_width = queries.shape
    key_blocks = key_codes.shape[1] // BLOCK
    share = GROUP // heads_dev
    assert share == 2 and rows_dev == BLOCK
    core = head_place % share
    group = head_place // share
    groups = head_count // share

    (keys,) = begin(key_kernel, scale_index, scale_table, key_codes, 1)
    *values, brought, positions, block_lists = begin(
        half_kernel,
        scale_index,
        scale_table,
        value_codes,
        2,
        keys,
        others=(queries.reshape(-1, head_width), positions, block_lists),
    )
    queries = brought.reshape(queries.shape)
    far_keys = keys
    key_parts = []
    for _ in range(reach_hops):
        far_keys = sent(far_keys, share, pairs)
        key_parts.append(far_keys)
    own_lists = lax.dynamic_index_in_dim(block_lists, cycle_place, 1, keepdims=False)

    def ordered(x):
        cut = x.reshape((groups, share, rows_dev // head_count) + x.shape[1:])
        taken = [
            lax.dynamic_slice(
                cut,
                (jnp.bitwise_xor(group, n), jnp.bitwise_xor(core, part ^ n % share))
                + (0,) * x.ndim,
                (1, 1) + cut.shape[2:],
            )
            for part in range(share)
            for n in range(groups)
        ]
        return jnp.concatenate(taken, axis=0).reshape(x.shape)

    frequency = ROPE_BASE ** (
        -2.0 * (jnp.arange(head_width) // 2).astype(jnp.float32) / head_width
    )
    angles = ordered(positions).astype(jnp.float32)[:, None] * frequency[None, :]
    signs = jnp.where(jnp.arange(head_width) % 2 == 0, -1.0, 1.0)
    cosine = jnp.cos(angles)
    sine = jnp.sin(angles) * signs[None, :]

    picks = own_lists.shape[1]
    carried = jnp.pad(own_lists.astype(jnp.bfloat16), ((0, 0), (0, head_width - picks)))
    own, sibling = turn_queries(
        jnp.transpose(ordered(queries), (1, 0, 2)), cosine, sine, carried
    )
    sibling, key_parts[0] = lax.optimization_barrier((sibling, key_parts[0]))
    key_parts = [keys] + [part for far in key_parts for part in (far, swapped(far, 1))]
    sibling = swapped(sibling, 1)
    sibling_lists = sibling[:, rows_dev // share, :picks].astype(jnp.int32)
    lists = jnp.concatenate([own_lists, sibling_lists], axis=0)
    offset = jnp.mod(lists // key_blocks - cycle_place, cycle_size)
    above = offset <= reach_hops
    hops = jnp.where(above, offset, cycle_size - offset)
    outer = jnp.logical_or(cycle_place % 4 == 0, cycle_place % 4 == 3)
    from_above = (cycle_place % 2 == (core == outer)) if pairs else core == 1
    place = 2 * hops - jnp.where(above == from_above, 1, 0)
    slots = lists % key_blocks + key_blocks * jnp.where(offset == 0, 0, place)

    steps = []
    far_values = values
    for _ in range(reach_hops):
        far_values = [sent(half, share, pairs) for half in far_values]
        steps.append(far_values)
    rows = rows_dev // share
    own_weights, own_total, held = block_weights(slots[:heads_dev], own, key_parts, rows)
    sibling_weights, sibling_total = block_weights(slots[heads_dev:], sibling, [held], rows)
    weights = (own_weights, sibling_weights)
    totals = (own_total, sibling_total)

    inner = slots % key_blocks
    places = slots // key_blocks * (key_blocks // 2) + inner % (key_blocks // 2)
    parity = jnp.arange(slots.shape[0])[:, None] % 2
    turned_places = (2 * reach_hops + 1) * (key_blocks // 2)
    ready = own_weights
    moved = []
    for half in range(2):
        *far_values, ready = lax.optimization_barrier((*[step[half] for step in steps], ready))
        value_parts = [values[half]]
        for far in far_values:
            value_parts += [far, swapped(far, 1)]
        side = jnp.bitwise_xor(inner // (key_blocks // 2), jnp.bitwise_xor(parity, half))
        outputs = functools.partial(
            block_outputs,
            places + turned_places * side,
            weights,
            totals,
            value_parts,
            groups,
            half,
        )
        if half == 0 or groups == 1:
            pieces = outputs(0, groups)
        else:
            pieces = [None, *outputs(1, groups)]
        sent_pieces = [swapped(pieces[n], across(n, share)) for n in range(1, groups)]
        if pieces[0] is None:
            pieces[0] = outputs(0, 1)[0]
        moved += [pieces[0], *sent_pieces]
        ready = pieces[0]
    return join_pieces(moved, share, head_width)


def solution(mesh):
    placed = (
        P(("groups", "ctx"), "head", None),
        P(("groups", "ctx")),
        P("groups", "ctx", None),
        P("groups", "ctx", None),
        P("groups", None, "ctx"),
        P(),
        P(("groups", "head"), None, None),
    )
    return jax.shard_map(
        on_device,
        mesh=mesh,
        in_specs=placed,
        out_specs=P(("groups", "ctx", "head"), None),
        check_vma=False,
    )
```

```python
import functools
import math

import jax
import jax.numpy as jnp
from jax import lax
from jax.experimental import pallas as pl
from jax.experimental.pallas import tpu as pltpu
from jax.sharding import PartitionSpec as P

GROUP = 16
BLOCK = 128
ROW_TILE = 16
ABREAST = 4
ROPE_BASE = 500000.0
VMEM_GRANT = 16 * 2**20

in_vmem = pl.BlockSpec(memory_space=pltpu.VMEM)
granted = pltpu.CompilerParams(vmem_limit_bytes=VMEM_GRANT)


def paired(cycle, hops):
    return hops == 1 and cycle % 2 == 0


def source(place, part, cycle, pairs):
    if not pairs:
        return (place + (1 if part else -1)) % cycle, part
    outer = place % 4 in (0, 3)
    odd = part == outer
    other = (place + (1 if place % 2 == odd else -1)) % cycle
    return other, int((other % 4 in (0, 3)) == odd)


def sent(x, share, pairs):
    cycle = lax.axis_size("ctx")
    heads = lax.axis_size("head")
    moves = []
    for place in range(cycle):
        for head in range(heads):
            part = head % share
            other, core = source(place, part, cycle, pairs)
            moves.append((other * heads + head - part + core, place * heads + head))
    return lax.ppermute(x, ("ctx", "head"), moves)


def across(n, share):
    return n * share ^ n % share


def swapped(x, mask):
    return lax.ppermute(x, "head", [(i, i ^ mask) for i in range(lax.axis_size("head"))])


def fetch(index_hbm, table_hbm, codes_hbm, index_ref, table_ref, codes_ref, arrived, row):
    groups = index_hbm.shape[1]
    kv_head = lax.axis_index("head") * groups // lax.axis_size("head")
    copies = [
        pltpu.make_async_copy(source, target, arrived.at[n])
        for n, (source, target) in enumerate(
            (
                (index_hbm, index_ref),
                (table_hbm, table_ref),
                (codes_hbm.at[kv_head], codes_ref),
            )
        )
    ]
    for copy in copies:
        copy.start()
    for copy in copies[:2]:
        copy.wait()
    scales = [
        table_ref[row, index_ref[row, kv_head, block]] for block in range(index_hbm.shape[2])
    ]
    copies[2].wait()
    return scales


def key_kernel(index_hbm, table_hbm, codes_hbm, out_ref, *scratch):
    codes_ref = scratch[2]
    for block, scale in enumerate(fetch(index_hbm, table_hbm, codes_hbm, *scratch, 0)):
        codes = codes_ref[block * BLOCK : (block + 1) * BLOCK, :].astype(jnp.float32)
        out_ref[block] = (codes * scale).astype(jnp.bfloat16)


def half_kernel(index_hbm, table_hbm, codes_hbm, _, *rest):
    *others, index_ref, table_ref, codes_ref, arrived = rest
    scratch = (index_ref, table_ref, codes_ref, arrived)
    count = len(others) // 2 - 1
    first_ref, second_ref = others[count : count + 2]
    copies = [
        pltpu.make_async_copy(others[n], others[count + 2 + n], arrived.at[3 + n])
        for n in range(count)
    ]
    for copy in copies:
        copy.start()
    scales = fetch(index_hbm, table_hbm, codes_hbm, *scratch, 1)
    pairs = first_ref.shape[0]
    width = codes_ref.shape[1]
    low = lower_half((BLOCK, width))
    for pair in range(pairs):
        left, right = (
            codes_ref[block * BLOCK : (block + 1) * BLOCK, :].astype(jnp.float32) * scales[block]
            for block in (pair, pair + pairs)
        )
        first = jnp.where(low, left, pltpu.roll(right, width // 2, 1))
        second = jnp.where(low, pltpu.roll(left, width // 2, 1), right)
        first_ref[pair] = first.astype(jnp.bfloat16)
        second_ref[pair] = second.astype(jnp.bfloat16)
    for copy in copies:
        copy.wait()


def lower_half(shape):
    return lax.broadcasted_iota(jnp.int32, shape, 1) < shape[1] // 2


def begin(kernel, scale_index, scale_table, codes, outputs, *after, others=()):
    _, keys_dev, width = codes.shape
    blocks = keys_dev // BLOCK // outputs
    stay = functools.partial(pltpu.with_memory_space_constraint, memory_space=pltpu.HBM)
    return pl.pallas_call(
        kernel,
        in_specs=[pl.BlockSpec(memory_space=pltpu.HBM)] * 3
        + [pl.BlockSpec(memory_space=pl.ANY)] * len(after)
        + [pl.BlockSpec(memory_space=pltpu.HBM)] * len(others),
        out_specs=[in_vmem] * (outputs + len(others)),
        out_shape=[pltpu.VMEM((blocks, BLOCK, width), jnp.bfloat16)] * outputs
        + [pltpu.VMEM(other.shape, other.dtype) for other in others],
        scratch_shapes=[
            pltpu.SMEM(scale_index.shape, scale_index.dtype),
            pltpu.SMEM(scale_table.shape, scale_table.dtype),
            pltpu.VMEM((keys_dev, width), codes.dtype),
            pltpu.SemaphoreType.DMA((3 + len(others),)),
        ],
        compiler_params=granted,
        name=kernel.__name__,
    )(
        stay(scale_index),
        stay(scale_table),
        stay(codes),
        *after,
        *[stay(other) for other in others],
    )


def turn_kernel(queries_ref, cosine_ref, sine_ref, lists_ref, own_ref, sibling_ref):
    heads_dev, rows, width = own_ref.shape
    cosine = cosine_ref[...]
    sine = sine_ref[...]
    even = lax.rem(lax.broadcasted_iota(jnp.int32, cosine.shape, 1), 2) == 0
    for head in range(heads_dev):
        plain = queries_ref[head].astype(jnp.float32)
        other = jnp.where(even, pltpu.roll(plain, width - 1, 1), pltpu.roll(plain, 1, 1))
        turned = (plain * cosine + other * sine).astype(jnp.bfloat16)
        own_ref[head] = turned[:rows]
        sibling_ref[head, :rows] = turned[rows:]
        sibling_ref[head, rows:] = jnp.broadcast_to(
            lists_ref[head : head + 1], sibling_ref[head, rows:].shape
        )


def turn_queries(queries, cosine, sine, lists):
    heads_dev, rows, width = queries.shape
    half = (heads_dev, rows // 2, width)
    more = (heads_dev, rows // 2 + ROW_TILE, width)
    return pl.pallas_call(
        turn_kernel,
        in_specs=[in_vmem] * 4,
        out_specs=[in_vmem] * 2,
        out_shape=[
            jax.ShapeDtypeStruct(half, jnp.bfloat16),
            jax.ShapeDtypeStruct(more, jnp.bfloat16),
        ],
        compiler_params=granted,
        name="turn_queries",
    )(queries, cosine, sine, lists)


def score_kernel(slots_ref, queries_ref, *rest, inputs):
    parts = rest[:inputs]
    weights_ref, total_ref, store = rest[inputs : inputs + 3]
    heads, rows, width = total_ref.shape
    picks = slots_ref.shape[1]
    slots = slots_ref[...]
    factor = math.log2(math.e) / math.sqrt(width)
    at = 0
    for part in parts:
        for block in range(part.shape[0]):
            store[at] = part[block].astype(jnp.float32).T.astype(jnp.bfloat16)
            at += 1
    for head in range(heads):
        turned = queries_ref[head, :rows]
        scores = []
        for i in range(0, picks, ABREAST):
            wide = jnp.concatenate([store[slots[head, i + j]] for j in range(ABREAST)], axis=1)
            wide = jnp.dot(turned, wide, preferred_element_type=jnp.float32)
            scores += [wide[:, j * BLOCK : (j + 1) * BLOCK] for j in range(ABREAST)]
        top = scores[0]
        for i in range(1, picks):
            top = jnp.maximum(top, scores[i])
        top = jnp.max(top, axis=1, keepdims=True)
        total = jnp.zeros((rows, BLOCK), jnp.float32)
        for i in range(picks):
            weight = jnp.exp2((scores[i] - top) * factor)
            total = total + weight
            weights_ref[head, :, i * BLOCK : (i + 1) * BLOCK] = weight.astype(jnp.bfloat16)
        total = jnp.sum(total, axis=1, keepdims=True)
        total_ref[head] = jnp.broadcast_to(1.0 / total, (rows, width))


def held_kernel(slots_ref, queries_ref, store, weights_ref, total_ref):
    score_kernel(slots_ref, queries_ref, weights_ref, total_ref, store, inputs=0)


def block_weights(slots, queries, parts, rows):
    width = queries.shape[2]
    heads, picks = slots.shape
    blocks = sum(part.shape[0] for part in parts)
    outputs = [
        jax.ShapeDtypeStruct((heads, rows, picks * BLOCK), jnp.bfloat16),
        jax.ShapeDtypeStruct((heads, rows, width), jnp.float32),
    ]
    if len(parts) > 1:
        outputs.append(jax.ShapeDtypeStruct((blocks, width, BLOCK), jnp.bfloat16))
    return pl.pallas_call(
        functools.partial(score_kernel, inputs=len(parts)) if len(parts) > 1 else held_kernel,
        in_specs=[in_vmem] * (2 + len(parts)),
        out_specs=[in_vmem] * len(outputs),
        out_shape=outputs,
        compiler_params=granted,
        name="block_weights",
    )(slots, queries, *parts)


def value_kernel(slots_ref, *rest, inputs, flip, first, last):
    weights = rest[:2]
    totals = rest[2:4]
    parts = rest[4 : 4 + inputs]
    pieces = rest[4 + inputs : -1]
    store = rest[-1]
    heads_dev, _, width = totals[0].shape
    heads, picks = slots_ref.shape
    rows = pieces[0].shape[0]
    slots = slots_ref[...]
    half = store.shape[0] // 2
    at = 0
    for part in parts:
        for pair in range(part.shape[0]):
            block = part[pair]
            store[at] = block
            turned = pltpu.roll(block.astype(jnp.float32), width // 2, 1)
            store[half + at] = turned.astype(jnp.bfloat16)
            at += 1
    low = lower_half((last - first, width))
    for pair in range(heads // 2):
        both = []
        for head in (2 * pair, 2 * pair + 1):
            picked = jnp.concatenate([store[slots[head, i]] for i in range(picks)], axis=0)
            owner, place = divmod(head, heads_dev)
            weight = weights[owner][place, first:last]
            out = jnp.dot(weight, picked, preferred_element_type=jnp.float32)
            both.append(out * totals[owner][place, first:last])
        out = jnp.where(low, both[flip], both[1 - flip])
        for n, piece in enumerate(pieces):
            piece[:, pair * width : (pair + 1) * width] = out[n * rows : (n + 1) * rows].astype(
                jnp.bfloat16
            )


def block_outputs(slots, weights, totals, parts, pieces, flip, first, last):
    heads = slots.shape[0]
    _, rows, width = totals[0].shape
    pairs = sum(part.shape[0] for part in parts)
    rows //= pieces
    pieces = last - first
    piece = jax.ShapeDtypeStruct((rows, heads // 2 * width), jnp.bfloat16)
    return pl.pallas_call(
        functools.partial(
            value_kernel,
            inputs=len(parts),
            flip=flip,
            first=first * rows,
            last=last * rows,
        ),
        in_specs=[in_vmem] * (5 + len(parts)),
        out_specs=[in_vmem] * pieces,
        out_shape=[piece] * pieces,
        scratch_shapes=[pltpu.VMEM((2 * pairs, BLOCK, width), jnp.bfloat16)],
        compiler_params=granted,
        name="block_outputs",
    )(slots, *weights, *totals, *parts)


def join_kernel(*refs, share, width):
    *pieces, out_hbm, held, left = refs
    place = lax.axis_index("head")
    chips = len(pieces) // 2
    rows = held.shape[0]
    pairs = pieces[0].shape[1] // width // share
    size = 2 * pairs * width
    low = lower_half((rows, width))
    copies = []
    for n in range(chips):
        for part in range(share):
            base = (n * share + part) * size
            for pair in range(pairs):
                at = (part * pairs + pair) * width
                first, second = (
                    piece[:, at : at + width].astype(jnp.float32)
                    for piece in (pieces[n], pieces[chips + n])
                )
                even = jnp.where(low, first, second)
                odd = pltpu.roll(jnp.where(low, second, first), width // 2, 1)
                for m, out in enumerate((even, odd)):
                    to = base + (2 * pair + m) * width
                    held[:, to : to + width] = out.astype(jnp.bfloat16)
            column = jnp.bitwise_xor(place, across(n, share) ^ part) * size
            copy = pltpu.make_async_copy(
                held.at[:, pl.ds(base, size)],
                out_hbm.at[:, pl.ds(pl.multiple_of(column, size), size)],
                left.at[n * share + part],
            )
            copy.start()
            copies.append(copy)
    for copy in copies:
        copy.wait()


def join_pieces(pieces, share, width):
    rows, columns = pieces[0].shape
    shape = (rows, columns * len(pieces))
    return pl.pallas_call(
        functools.partial(join_kernel, share=share, width=width),
        in_specs=[in_vmem] * len(pieces),
        out_specs=pl.BlockSpec(memory_space=pltpu.HBM),
        out_shape=jax.ShapeDtypeStruct(shape, jnp.bfloat16),
        scratch_shapes=[
            pltpu.VMEM(shape, jnp.bfloat16),
            pltpu.SemaphoreType.DMA((len(pieces) // 2 * share,)),
        ],
        compiler_params=granted,
        name="join_pieces",
    )(*pieces)


def on_device(queries, positions, key_codes, value_codes, scale_index, scale_table, block_lists):
    cycle_size = lax.axis_size("ctx")
    cycle_place = lax.axis_index("ctx")
    head_count = lax.axis_size("head")
    head_place = lax.axis_index("head")
    reach_hops = min(3, (cycle_size - 1) // 2)
    pairs = paired(cycle_size, reach_hops)
    rows_dev, heads_dev, head_width = queries.shape
    key_blocks = key_codes.shape[1] // BLOCK
    share = GROUP // heads_dev
    assert share == 2 and rows_dev == BLOCK
    core = head_place % share
    group = head_place // share
    groups = head_count // share

    (keys,) = begin(key_kernel, scale_index, scale_table, key_codes, 1)
    *values, brought, positions, block_lists = begin(
        half_kernel,
        scale_index,
        scale_table,
        value_codes,
        2,
        keys,
        others=(queries.reshape(-1, head_width), positions, block_lists),
    )
    queries = brought.reshape(queries.shape)
    far_keys = keys
    key_parts = []
    for _ in range(reach_hops):
        far_keys = sent(far_keys, share, pairs)
        key_parts.append(far_keys)
    own_lists = lax.dynamic_index_in_dim(block_lists, cycle_place, 1, keepdims=False)

    def ordered(x):
        cut = x.reshape((groups, share, rows_dev // head_count) + x.shape[1:])
        taken = [
            lax.dynamic_slice(
                cut,
                (jnp.bitwise_xor(group, n), jnp.bitwise_xor(core, part ^ n % share))
                + (0,) * x.ndim,
                (1, 1) + cut.shape[2:],
            )
            for part in range(share)
            for n in range(groups)
        ]
        return jnp.concatenate(taken, axis=0).reshape(x.shape)

    frequency = ROPE_BASE ** (
        -2.0 * (jnp.arange(head_width) // 2).astype(jnp.float32) / head_width
    )
    angles = ordered(positions).astype(jnp.float32)[:, None] * frequency[None, :]
    signs = jnp.where(jnp.arange(head_width) % 2 == 0, -1.0, 1.0)
    cosine = jnp.cos(angles)
    sine = jnp.sin(angles) * signs[None, :]

    picks = own_lists.shape[1]
    carried = jnp.pad(own_lists.astype(jnp.bfloat16), ((0, 0), (0, head_width - picks)))
    own, sibling = turn_queries(
        jnp.transpose(ordered(queries), (1, 0, 2)), cosine, sine, carried
    )
    sibling, key_parts[0] = lax.optimization_barrier((sibling, key_parts[0]))
    key_parts = [keys] + [part for far in key_parts for part in (far, swapped(far, 1))]
    sibling = swapped(sibling, 1)
    sibling_lists = sibling[:, rows_dev // share, :picks].astype(jnp.int32)
    lists = jnp.concatenate([own_lists, sibling_lists], axis=0)
    offset = jnp.mod(lists // key_blocks - cycle_place, cycle_size)
    above = offset <= reach_hops
    hops = jnp.where(above, offset, cycle_size - offset)
    outer = jnp.logical_or(cycle_place % 4 == 0, cycle_place % 4 == 3)
    from_above = (cycle_place % 2 == (core == outer)) if pairs else core == 1
    place = 2 * hops - jnp.where(above == from_above, 1, 0)
    slots = lists % key_blocks + key_blocks * jnp.where(offset == 0, 0, place)

    steps = []
    far_values = values
    for _ in range(reach_hops):
        far_values = [sent(half, share, pairs) for half in far_values]
        steps.append(far_values)
    rows = rows_dev // share
    own_weights, own_total, held = block_weights(slots[:heads_dev], own, key_parts, rows)
    sibling_weights, sibling_total = block_weights(slots[heads_dev:], sibling, [held], rows)
    weights = (own_weights, sibling_weights)
    totals = (own_total, sibling_total)

    inner = slots % key_blocks
    places = slots // key_blocks * (key_blocks // 2) + inner % (key_blocks // 2)
    parity = jnp.arange(slots.shape[0])[:, None] % 2
    turned_places = (2 * reach_hops + 1) * (key_blocks // 2)
    ready = own_weights
    moved = []
    for half in range(2):
        *far_values, ready = lax.optimization_barrier((*[step[half] for step in steps], ready))
        value_parts = [values[half]]
        for far in far_values:
            value_parts += [far, swapped(far, 1)]
        side = jnp.bitwise_xor(inner // (key_blocks // 2), jnp.bitwise_xor(parity, half))
        outputs = functools.partial(
            block_outputs,
            places + turned_places * side,
            weights,
            totals,
            value_parts,
            groups,
            half,
        )
        if half == 0 or groups == 1:
            pieces = outputs(0, groups)
        else:
            pieces = [None, *outputs(1, groups)]
        sent_pieces = [swapped(pieces[n], across(n, share)) for n in range(1, groups)]
        if pieces[0] is None:
            pieces[0] = outputs(0, 1)[0]
        moved += [pieces[0], *sent_pieces]
        ready = pieces[0]
    return join_pieces(moved, share, head_width)


def solution(mesh):
    placed = (
        P(("groups", "ctx"), "head", None),
        P(("groups", "ctx")),
        P("groups", "ctx", None),
        P("groups", "ctx", None),
        P("groups", None, "ctx"),
        P(),
        P(("groups", "head"), None, None),
    )
    return jax.shard_map(
        on_device,
        mesh=mesh,
        in_specs=placed,
        out_specs=P(("groups", "ctx", "head"), None),
        check_vma=False,
    )
```
